32 devices in a mesh: dp: 2 (over y), expert: 16 (over z, x, core).
Axes of the slice: x: 2, y: 2, z: 4, core: 2. Of those that a mesh axis runs over, the one named last changes fastest.
Arguments:
- tokens: bfloat16 [4096, 2048], P(('dp', 'expert')), may hold values from -6 to 6
- out_grad: bfloat16 [4096, 2048], P(('dp', 'expert')), may hold values from -6 to 6
- expert_ids: int32 [4096, 6], P(('dp', 'expert')), may hold values from 0 to 15, all different within a row; in each aligned block of 128 rows (0 to 127, 128 to 255, ...) at most 56 rows name the same one
- route_weights: bfloat16 [4096, 6], P(('dp', 'expert')), may hold values from 0.019897461 to 0.5
- blocks: bfloat16 [16, 3, 12, 128, 128], P('expert'), may hold values from -0.5 to 0.5
- layout: int32 [16, 3, 12, 2], P('expert'), may hold values from 0 to 15, as said below
- moments: float32 [16, 3, 12, 128, 128], P('expert', None, None, 'dp'), may hold values from -12 to 12
- partner: int32 [16], replicated, may hold values from 0 to 15, as said below
Outputs:
- token_grad: bfloat16 [4096, 2048], P(('dp', 'expert'))
- route_grad: bfloat16 [4096, 6], P(('dp', 'expert'))
- new_blocks: bfloat16 [16, 3, 12, 128, 128], P('expert')
- new_moments: float32 [16, 3, 12, 128, 128], P('expert', None, None, 'dp')
The draws below stay inside these ranges and needn't reach their ends.
Inputs may be any that keep to these rules, and one draw needn't show every extreme that they name: `layout`: within one expert and matrix the stored blocks are at distinct places; for gate and up an entry is (block of the 2048 features, block of the 1408 hidden units), for down (block of the hidden units, block of the features). partner pairs the experts: partner[partner[e]] == e and partner[e] != e. `expert_ids`: each row names 6 different experts; among the rows of one device no expert is named more than 56 times, a bound that some block reaches.
All inputs are finite; a program needn't handle non-finite values.
Results may differ from the reference program's by a relative error of at most 0.0064.
Values may be sent and summed in bfloat16 or wider, within the bound.
No kernel may reach another device: no remote copies, remote signals or barrier semaphores. Data moves between devices by JAX's collectives and lax.ppermute only.
A program may use at most 128 MiB of HBM per device.

```python
import math
import jax
import jax.numpy as jnp
import numpy as np
from jax import lax

D = 2048
HID = 1408
TOPK = 6
BLK = 128
NB = 12
TOK_DEV = 128
EXPERTS = 16
CAP = 56
TOKENS = 4096
N_DP = 2
N_EXPERT = 16


def draw_layout(key, part):
    feat_blocks = D // BLK
    hidden_blocks = HID // BLK
    cell_count = feat_blocks * hidden_blocks
    matrix_keys = jax.random.split(jax.random.fold_in(key, 11), EXPERTS * 3)
    chosen = jax.vmap(lambda one_key: jax.random.permutation(one_key, cell_count)[:NB])(matrix_keys)
    chosen = chosen.reshape(EXPERTS, 3, NB).astype(jnp.int32)
    first_rows = chosen[:, :2] // hidden_blocks
    first_cols = chosen[:, :2] % hidden_blocks
    down_rows = chosen[:, 2:] // feat_blocks
    down_cols = chosen[:, 2:] % feat_blocks
    row_part = jnp.concatenate([first_rows, down_rows], axis=1)
    col_part = jnp.concatenate([first_cols, down_cols], axis=1)
    return jnp.stack([row_part, col_part], axis=-1).astype(jnp.int32)


def draw_partner(key, part):
    order = jax.random.permutation(jax.random.fold_in(key, 23), EXPERTS).astype(jnp.int32)
    evens = order[0::2]
    odds = order[1::2]
    paired = jnp.zeros((EXPERTS,), jnp.int32).at[evens].set(odds).at[odds].set(evens)
    return paired


def block_levels(key, shape, cuts, smallest, top_value):
    gain, own = 1.0, jax.random.fold_in(key, 6)
    for dim, parts in cuts:
        heights = jnp.exp(jax.random.uniform(jax.random.fold_in(own, dim), (parts,), jnp.float32, smallest / len(cuts), top_value / len(cuts)))
        gain = gain * jnp.repeat(heights, shape[dim] // parts).reshape([-1 if axis == dim else 1 for axis in range(len(shape))])
    return gain


def shared_out(key, own, number, rows, amount, top, reach, skew):
    ranking = jax.random.permutation(key, amount)
    heavy_load, common = shares(amount, rows * top, reach, skew, True), shares(amount, rows * top, reach, skew, False)
    places = jnp.arange(amount)

    def named(sizes, offset_by):
        used = int((sizes > 0).sum())
        fixed = max(1, used // 4)
        moved = fixed + (places - fixed + offset_by * (used - fixed)) % max(1, amount - fixed)
        return jnp.zeros((amount,), jnp.int32).at[ranking[jnp.where(places < fixed, places, moved)]].set(jnp.asarray(sizes, jnp.int32))

    sizes = jnp.where(number % 4 == 0, named(heavy_load, number // 4), named(common, number - number // 4 - 1))
    mixed = jax.random.permutation(jax.random.fold_in(own, 3), amount)
    source_of, receiver = mixed[0:amount // 2 * 2:2], mixed[1:amount // 2 * 2:2]
    room = jnp.minimum(sizes[source_of] - 1, reach - sizes[receiver]) // 2
    room = jnp.where((source_of == ranking[0]) | (receiver == ranking[0]) | (sizes[receiver] == 0), 0, jnp.maximum(room, 0))
    moved = jax.random.randint(jax.random.fold_in(own, 4), (amount // 2,), 0, 1 << 20) % (room + 1)
    sizes = sizes.at[source_of].add(-moved).at[receiver].add(moved)
    items = jnp.searchsorted(jnp.cumsum(sizes), jnp.arange(rows * top), side="right").astype(jnp.int32)
    table = items.reshape(top, rows).T
    table = table[jax.random.permutation(jax.random.fold_in(own, 1), rows)]
    offset_by = jax.random.randint(jax.random.fold_in(own, 2), (rows, 1), 0, top)
    return jnp.take_along_axis(table, (jnp.arange(top)[None, :] + offset_by) % top, axis=1)


def shares(amount, total, bound, lean, full):
    weights = [(1 << 20) // math.isqrt(rank ** lean) + 1 for rank in range(1, amount + 1)]
    largest = bound if full else min(bound, max(-(-total // amount), total * weights[0] // sum(weights)))
    least = 1 if total - largest >= amount - 1 else 0
    holding, rest = [largest] + [least] * (amount - 1), total - largest - least * (amount - 1)
    while rest > 0:
        candidates = [i for i in range(1, amount) if holding[i] < largest] or [i for i in range(1, amount) if holding[i] < bound]
        whole, remaining = sum([weights[i] for i in candidates]), rest
        for i in candidates:
            more = min(bound - holding[i], max(1, remaining * weights[i] // whole), rest)
            holding[i] = holding[i] + more
            rest = rest - more
    return np.array(holding)


def centred(stream_key, shape, deviation, bound, cuts=(), kind=jnp.bfloat16):
    result = deviation * jax.random.normal(stream_key, shape, jnp.float32)
    if cuts:
        result = result * block_levels(stream_key, shape, cuts, -0.22, 0.18)
    return jnp.clip(result, -bound, bound).astype(kind)


def setup_inputs(seed: int = 0) -> dict:
    key_list = jax.random.split(jax.random.key(seed), 9)
    tokens = centred(key_list[0], (TOKENS, D), 1.0, 6.0, ((0, 32),))
    out_grad = centred(key_list[1], (TOKENS, D), 1.0, 6.0, ((0, 32),))
    expert_ids_keys = jax.random.split(jax.random.fold_in(key_list[2], 1), TOKENS // TOK_DEV)
    expert_ids_turns = jax.random.permutation(jax.random.fold_in(key_list[2], 3), TOKENS // TOK_DEV)
    expert_ids = jax.vmap(lambda own, number: shared_out(jax.random.fold_in(key_list[2], 2), own, number, TOK_DEV, EXPERTS, TOPK, CAP, 2))(expert_ids_keys, expert_ids_turns).reshape((TOKENS, TOPK))
    route_weights = jnp.clip(jnp.exp(math.log(0.5) - 3.224016 * jax.random.uniform(key_list[3], (TOKENS, TOPK), jnp.float32) ** block_levels(key_list[3], (TOKENS, TOPK), ((0, 32),), -0.2, 0.2)), 0.019897461, 0.5).astype(jnp.bfloat16)
    blocks = centred(key_list[4], (EXPERTS, 3, NB, BLK, BLK), BLK ** -0.5, 0.5, ((0, 16),))
    layout = draw_layout(jax.random.fold_in(key_list[8], 71), 0)
    moments = centred(key_list[6], (EXPERTS, 3, NB, BLK, BLK), 2.0, 12.0, ((0, 16), (3, 2)), jnp.float32)
    partner = draw_partner(jax.random.fold_in(key_list[8], 71), 0)
    return {"tokens": tokens, "out_grad": out_grad, "expert_ids": expert_ids, "route_weights": route_weights, "blocks": blocks, "layout": layout, "moments": moments, "partner": partner}


momentum_decay = 0.9
step_rate = 0.01


def block_product(left, mats, source_idx, target_idx, target_count, flipped):
    row_count = left.shape[0]
    block_size = mats.shape[-1]
    pieces = jnp.take(left.reshape(row_count, -1, block_size), source_idx, axis=1).astype(jnp.float32)
    wide = mats.astype(jnp.float32)
    if flipped:
        partial_out = jnp.einsum("rbk,bnk->rbn", pieces, wide, precision=lax.Precision.HIGHEST)
    else:
        partial_out = jnp.einsum("rbk,bkn->rbn", pieces, wide, precision=lax.Precision.HIGHEST)
    select = (target_idx[:, None] == jnp.arange(target_count, dtype=jnp.int32)[None, :]).astype(jnp.float32)
    placed = jnp.einsum("rbn,bc->rcn", partial_out, select, precision=lax.Precision.HIGHEST)
    return placed.reshape(row_count, target_count * block_size)


def block_outer(left, right, left_idx, right_idx, block_size):
    row_count = left.shape[0]
    left_pieces = jnp.take(left.reshape(row_count, -1, block_size), left_idx, axis=1).astype(jnp.float32)
    right_pieces = jnp.take(right.reshape(row_count, -1, block_size), right_idx, axis=1).astype(jnp.float32)
    return jnp.einsum("rbk,rbn->bkn", left_pieces, right_pieces, precision=lax.Precision.HIGHEST)


def expert_forward(inputs, matrices, layout_one, hidden_blocks, feat_blocks):
    gate_pre = block_product(inputs, matrices[0], layout_one[0, :, 0], layout_one[0, :, 1], hidden_blocks, False)
    up_pre = block_product(inputs, matrices[1], layout_one[1, :, 0], layout_one[1, :, 1], hidden_blocks, False)
    sigmoid_gate = jax.nn.sigmoid(gate_pre)
    activated = gate_pre * sigmoid_gate
    hidden = (activated * up_pre).astype(jnp.bfloat16)
    output = block_product(hidden, matrices[2], layout_one[2, :, 0], layout_one[2, :, 1], feat_blocks, False)
    return (gate_pre, up_pre, sigmoid_gate, activated, hidden, output)


def expert_backward(inputs, upstream, weights_col, matrices, layout_one, hidden_blocks, feat_blocks, saved):
    gate_pre, up_pre, sigmoid_gate, activated, hidden, output = saved
    score = jnp.sum(output * upstream.astype(jnp.float32), axis=1).astype(jnp.bfloat16)
    scaled = (weights_col.astype(jnp.float32)[:, None] * upstream.astype(jnp.float32)).astype(jnp.bfloat16)
    hidden_grad = block_product(scaled, matrices[2], layout_one[2, :, 1], layout_one[2, :, 0], hidden_blocks, True)
    gate_grad = (hidden_grad * up_pre * sigmoid_gate * (1.0 + gate_pre * (1.0 - sigmoid_gate))).astype(jnp.bfloat16)
    up_grad = (hidden_grad * activated).astype(jnp.bfloat16)
    input_grad = (block_product(gate_grad, matrices[0], layout_one[0, :, 1], layout_one[0, :, 0], feat_blocks, True)
                  + block_product(up_grad, matrices[1], layout_one[1, :, 1], layout_one[1, :, 0], feat_blocks, True)).astype(jnp.bfloat16)
    block_size = matrices.shape[-1]
    weight_grad = jnp.stack([
        block_outer(inputs, gate_grad, layout_one[0, :, 0], layout_one[0, :, 1], block_size),
        block_outer(inputs, up_grad, layout_one[1, :, 0], layout_one[1, :, 1], block_size),
        block_outer(hidden, scaled, layout_one[2, :, 0], layout_one[2, :, 1], block_size)])
    return score, input_grad, weight_grad


def reference(tokens, out_grad, expert_ids, route_weights, blocks, layout, moments, partner):
    pick_total = TOKENS * TOPK
    flat_ids = expert_ids.reshape(-1)
    order = jnp.argsort(flat_ids, stable=True).astype(jnp.int32)
    counts = jnp.bincount(flat_ids, length=EXPERTS).astype(jnp.int32)
    starts = (jnp.cumsum(counts) - counts).astype(jnp.int32)
    most_rows = CAP * N_DP * N_EXPERT
    padded_order = jnp.concatenate([order, jnp.full((most_rows,), pick_total, jnp.int32)])
    feat_blocks = D // BLK
    hidden_blocks = HID // BLK
    flat_weights = route_weights.reshape(-1)

    def per_expert(carry, expert):
        grad_total, score_total = carry
        position = lax.dynamic_slice_in_dim(padded_order, starts[expert].astype(jnp.int32), most_rows)
        filled = jnp.arange(most_rows, dtype=jnp.int32) < counts[expert]
        safe_pick = jnp.minimum(position, pick_total - 1).astype(jnp.int32)
        token_of = (safe_pick // TOPK).astype(jnp.int32)
        inputs = jnp.where(filled[:, None], tokens[token_of], jnp.zeros((), tokens.dtype))
        upstream = jnp.where(filled[:, None], out_grad[token_of], jnp.zeros((), out_grad.dtype))
        weights_col = jnp.where(filled, flat_weights[safe_pick], jnp.zeros((), route_weights.dtype))
        matrices = blocks[expert]
        layout_one = layout[expert]
        saved = expert_forward(inputs, matrices, layout_one, hidden_blocks, feat_blocks)
        score, input_grad, weight_grad = expert_backward(inputs, upstream, weights_col, matrices, layout_one, hidden_blocks, feat_blocks, saved)
        target = jnp.where(filled, token_of, TOKENS).astype(jnp.int32)
        grad_total = grad_total.at[target].add(input_grad.astype(jnp.float32), mode="drop")
        pick_target = jnp.where(filled, safe_pick, pick_total).astype(jnp.int32)
        score_total = score_total.at[pick_target].set(score.astype(jnp.float32), mode="drop")
        return (grad_total, score_total), weight_grad

    start_carry = (jnp.zeros((TOKENS, D), jnp.float32), jnp.zeros((pick_total,), jnp.float32))
    (grad_total, score_total), weight_grads = lax.scan(per_expert, start_carry, jnp.arange(EXPERTS, dtype=jnp.int32))
    token_grad = grad_total.astype(jnp.bfloat16)
    route_grad = score_total.reshape(TOKENS, TOPK).astype(jnp.bfloat16)
    moment = momentum_decay * moments + weight_grads
    updated = (blocks.astype(jnp.float32) - step_rate * moment).astype(jnp.bfloat16)
    return token_grad, route_grad, updated[partner], moment[partner]
```

```python
import functools

import jax
import jax.numpy as jnp
from jax import lax
from jax.experimental import pallas as pl
from jax.experimental.pallas import tpu as pltpu
from jax.sharding import PartitionSpec as P

HID = 1408
LANES = 128

momentum_decay = 0.9
step_rate = 0.01

NN = (((1,), (0,)), ((), ()))
NT = (((1,), (1,)), ((), ()))
TN = (((0,), (0,)), ((), ()))


def dot(left, right, dims):
    return lax.dot_general(left, right, dims, preferred_element_type=jnp.float32)


def expert_kernel(
    sources,
    slots,
    lay_ref,
    expert_ref,
    x_ref,
    g_ref,
    w_ref,
    t_ref,
    dw_ref,
    xs,
    gs,
    ss,
    gate,
    up,
    hid,
    hgrad,
    ggrad,
    ugrad,
    pgrad,
    pgrad_wide,
    prod,
):
    tok = LANES
    feat = xs.shape[0]
    hidden = gate.shape[0]
    width = feat * LANES
    count = w_ref.shape[0] // 3
    rows = sources * slots
    expert = expert_ref[0]
    token_row = lax.broadcasted_iota(jnp.int32, (tok, tok), 0)
    token_col = lax.broadcasted_iota(jnp.int32, (tok, tok), 1)
    earlier_row = (token_row < token_col).astype(jnp.bfloat16)
    earlier_col = (token_col < token_row).astype(jnp.bfloat16)
    table_lanes = x_ref.shape[1] - width
    lane_tok = lax.broadcasted_iota(jnp.int32, (tok, table_lanes), 1)
    lane_few = lax.broadcasted_iota(jnp.int32, (8, table_lanes), 1)
    own_few = (lane_few == expert).astype(jnp.bfloat16)
    slot_rows = lax.broadcasted_iota(jnp.int32, (slots, tok), 0).astype(jnp.float32)
    slot_cols = lax.broadcasted_iota(jnp.int32, (tok, slots), 1).astype(jnp.float32)

    @pl.when(pl.program_id(0) == 0)
    def _():
        dw_ref[...] = jnp.zeros_like(dw_ref)

    spread = []
    for s in range(sources):
        here = slice(s * tok, (s + 1) * tok)
        there = slice(s * slots, (s + 1) * slots)
        table = x_ref[here, width:]
        weight_row = dot(own_few, table, NT)[0:1]
        picked_row = weight_row > 0.0
        rank_row = dot(
            jnp.broadcast_to(picked_row, (8, tok)).astype(jnp.bfloat16), earlier_row, NN
        )[0:1]
        gather = jnp.where(
            jnp.logical_and(slot_rows == rank_row, picked_row), 1.0, 0.0
        )
        weight = jnp.sum(gather * weight_row, axis=1, keepdims=True)
        picked_col = jnp.max(
            jnp.where(lane_tok == expert, table.astype(jnp.float32), 0.0), axis=1, keepdims=True
        ) > 0.0
        rank_col = dot(
            earlier_col, jnp.broadcast_to(picked_col, (tok, tok)).astype(jnp.bfloat16), NN
        )[:, 0:1]
        spread.append(
            jnp.where(jnp.logical_and(slot_cols == rank_col, picked_col), 1.0, 0.0).astype(
                jnp.bfloat16
            )
        )
        gather = gather.astype(jnp.bfloat16)
        x_rows = dot(gather, x_ref[here, :width], NN).astype(jnp.bfloat16)
        g_rows = dot(gather, g_ref[here, :], NN)
        s_rows = (g_rows * weight).astype(jnp.bfloat16)
        g_rows = g_rows.astype(jnp.bfloat16)
        for c in range(feat):
            cut = slice(c * LANES, (c + 1) * LANES)
            xs[c, there, :] = x_rows[:, cut]
            gs[c, there, :] = g_rows[:, cut]
            ss[c, there, :] = s_rows[:, cut]

    gate[...] = jnp.zeros_like(gate)
    up[...] = jnp.zeros_like(up)
    hgrad[...] = jnp.zeros_like(hgrad)
    pgrad[...] = jnp.zeros_like(pgrad)

    def place(m, b):
        return lay_ref[2 * (m * count + b)], lay_ref[2 * (m * count + b) + 1]

    for b in range(count):
        r, c = place(0, b)
        gate[c] += dot(xs[r], w_ref[b], NN)
        r, c = place(1, b)
        up[c] += dot(xs[r], w_ref[count + b], NN)
        r, c = place(2, b)
        hgrad[r] += dot(ss[c], w_ref[2 * count + b], NT)
    for h in range(hidden):
        gate_pre = gate[h]
        up_pre = up[h]
        sig = jax.nn.sigmoid(gate_pre)
        activated = gate_pre * sig
        hid[h] = (activated * up_pre).astype(jnp.bfloat16)
        hidden_grad = hgrad[h]
        ggrad[h] = (hidden_grad * up_pre * sig * (1.0 + gate_pre * (1.0 - sig))).astype(
            jnp.bfloat16
        )
        ugrad[h] = (hidden_grad * activated).astype(jnp.bfloat16)
    prod[...] = jnp.zeros_like(prod)
    for b in range(count):
        r, c = place(0, b)
        pgrad[r] += dot(ggrad[c], w_ref[b], NT)
        dw_ref[b] += dot(xs[r], ggrad[c], TN)
        r, c = place(1, b)
        pgrad[r] += dot(ugrad[c], w_ref[count + b], NT)
        dw_ref[count + b] += dot(xs[r], ugrad[c], TN)
        r, c = place(2, b)
        prod[...] += dot(hid[r], w_ref[2 * count + b], NN) * gs[c].astype(jnp.float32)
        dw_ref[2 * count + b] += dot(hid[r], ss[c], TN)
    for c in range(feat):
        pgrad_wide[:, c * LANES : (c + 1) * LANES] = pgrad[c].astype(jnp.bfloat16)
    score = jnp.sum(prod[...], axis=1, keepdims=True).astype(jnp.bfloat16)
    own_lane = lax.broadcasted_iota(jnp.int32, (rows, table_lanes), 1) == expert
    pgrad_wide[:, width:] = jnp.where(
        own_lane, jnp.broadcast_to(score.astype(jnp.float32), (rows, table_lanes)), 0.0
    ).astype(jnp.bfloat16)
    for s in range(sources):
        t_ref[s * tok : (s + 1) * tok, :] = dot(
            spread[s], pgrad_wide[s * slots : (s + 1) * slots, :], NN
        ).astype(jnp.bfloat16)


def run_expert(x_all, g_all, mats, layout_one, expert, slots, sources):
    total_rows, table_width = x_all.shape
    width = g_all.shape[1]
    feat = width // LANES
    hidden = HID // LANES
    rows = sources * slots
    steps = total_rows // (sources * LANES)
    block_count = mats.shape[0]
    bf16, f32 = jnp.bfloat16, jnp.float32
    return pl.pallas_call(
        functools.partial(expert_kernel, sources, slots),
        grid=(steps,),
        in_specs=[
            pl.BlockSpec(memory_space=pltpu.SMEM),
            pl.BlockSpec(memory_space=pltpu.SMEM),
            pl.BlockSpec((sources * LANES, table_width), lambda i: (i, 0)),
            pl.BlockSpec((sources * LANES, width), lambda i: (i, 0)),
            pl.BlockSpec((block_count, LANES, LANES), lambda i: (0, 0, 0)),
        ],
        out_specs=[
            pl.BlockSpec((sources * LANES, table_width), lambda i: (i, 0)),
            pl.BlockSpec((block_count, LANES, LANES), lambda i: (0, 0, 0)),
        ],
        out_shape=[
            jax.ShapeDtypeStruct((total_rows, table_width), bf16),
            jax.ShapeDtypeStruct((block_count, LANES, LANES), f32),
        ],
        scratch_shapes=[
            pltpu.VMEM((feat, rows, LANES), bf16),
            pltpu.VMEM((feat, rows, LANES), bf16),
            pltpu.VMEM((feat, rows, LANES), bf16),
            pltpu.VMEM((hidden, rows, LANES), f32),
            pltpu.VMEM((hidden, rows, LANES), f32),
            pltpu.VMEM((hidden, rows, LANES), bf16),
            pltpu.VMEM((hidden, rows, LANES), f32),
            pltpu.VMEM((hidden, rows, LANES), bf16),
            pltpu.VMEM((hidden, rows, LANES), bf16),
            pltpu.VMEM((feat, rows, LANES), f32),
            pltpu.VMEM((rows, table_width), bf16),
            pltpu.VMEM((rows, LANES), f32),
        ],
        compiler_params=pltpu.CompilerParams(vmem_limit_bytes=56 * 1024 * 1024),
    )(layout_one, expert, x_all, g_all, mats)


def exchange(state, partner, expert_count):
    pieces = state.reshape(expert_count, -1, LANES)
    spread = lax.all_to_all(pieces, "expert", split_axis=0, concat_axis=0, tiled=True)
    moved = jnp.take(spread, partner, axis=0)
    collected = lax.all_to_all(moved, "expert", split_axis=0, concat_axis=0, tiled=True)
    return collected.reshape(state.shape)


def body(tokens, out_grad, expert_ids, route_weights, blocks, layout, moments, partner):
    expert_count = lax.axis_size("expert")
    replica_count = lax.axis_size("dp")
    tok_count, topk_count = expert_ids.shape
    width = tokens.shape[1]
    block_size = blocks.shape[-1]
    capacity = max(2, tok_count * topk_count * 7 // (expert_count * 6))
    slots = -(-capacity // 16) * 16
    sources = max(1, min(8, 256 // slots, expert_count))
    table_lanes = -(-expert_count // LANES) * LANES
    bf16, f32 = jnp.bfloat16, jnp.float32

    lane = jnp.arange(table_lanes, dtype=jnp.int32)
    named = expert_ids[:, :, None] == lane[None, None, :]
    table = jnp.sum(
        jnp.where(named, route_weights[:, :, None].astype(f32), 0.0), axis=1
    ).astype(bf16)
    me = lax.axis_index("expert")
    mine = partner[me].astype(jnp.int32)

    x_all = lax.all_gather(
        jnp.concatenate([tokens, table], axis=1), "expert", axis=0, tiled=True
    )
    row_share = block_size // replica_count
    own_rows = lax.dynamic_slice_in_dim(blocks[0], lax.axis_index("dp") * row_share, row_share, 2)
    moved_rows = exchange(own_rows, partner, expert_count)
    mats = lax.all_gather(moved_rows, "dp", axis=2, tiled=True)
    layouts = lax.all_gather(layout.reshape(1, -1), "expert", axis=0, tiled=True)
    layout_one = layouts[mine]
    g_all = lax.all_gather(out_grad, "expert", axis=0, tiled=True)
    moved_moments = exchange(moments[0].astype(bf16), partner, expert_count)

    part, weight_grad = run_expert(
        x_all,
        g_all,
        mats.reshape(-1, block_size, block_size),
        layout_one,
        mine.reshape(1),
        slots,
        sources,
    )
    total = lax.psum_scatter(part, "expert", scatter_dimension=0, tiled=True)
    token_grad = total[:, :width]
    scores = total[:, width:]
    route_grad = jnp.sum(
        jnp.where(named, scores[:, None, :].astype(f32), 0.0), axis=2
    ).astype(bf16)

    shard_grad = lax.psum_scatter(
        weight_grad.astype(bf16).reshape(mats.shape), "dp", scatter_dimension=2, tiled=True
    )
    new_moment = momentum_decay * moved_moments.astype(f32) + shard_grad.astype(f32)
    new_shard = (moved_rows.astype(f32) - step_rate * new_moment).astype(bf16)
    gathered = lax.all_gather(new_shard, "dp", axis=2, tiled=True)
    return (token_grad, route_grad, gathered[None], new_moment[None])


def solution(mesh):
    placed = (
        P(("dp", "expert"), None),
        P(("dp", "expert"), None),
        P(("dp", "expert"), None),
        P(("dp", "expert"), None),
        P("expert", None, None, None, None),
        P("expert", None, None, None),
        P("expert", None, None, "dp", None),
        P(),
    )
    return jax.shard_map(
        body,
        mesh=mesh,
        in_specs=placed,
        out_specs=(
            P(("dp", "expert"), None),
            P(("dp", "expert"), None),
            P("expert", None, None, None, None),
            P("expert", None, None, "dp", None),
        ),
        check_vma=False,
    )
```

```python
import functools

import jax
import jax.numpy as jnp
from jax import lax
from jax.experimental import pallas as pl
from jax.experimental.pallas import tpu as pltpu
from jax.sharding import PartitionSpec as P

HID = 1408
LANES = 128

momentum_decay = 0.9
step_rate = 0.01

NN = (((1,), (0,)), ((), ()))
NT = (((1,), (1,)), ((), ()))
TN = (((0,), (0,)), ((), ()))


def dot(left, right, dims):
    return lax.dot_general(left, right, dims, preferred_element_type=jnp.float32)


def expert_kernel(
    shards,
    slots,
    half,
    lay_ref,
    expert_ref,
    *refs,
):
    x_refs, refs = refs[:shards], refs[shards:]
    g_refs, refs = refs[:shards], refs[shards:]
    w_ref, refs = refs[0], refs[1:]
    low_refs, refs = refs[:shards], refs[shards:]
    high_refs, refs = refs[:shards], refs[shards:]
    (
        dw_ref,
        xs,
        gs,
        ss,
        gate,
        up,
        hid,
        hgrad,
        ggrad,
        ugrad,
        pgrad,
        wide,
        spread,
        prod,
    ) = refs
    tok = LANES
    feat = xs.shape[1]
    hidden = gate.shape[0]
    width = feat * LANES
    count = w_ref.shape[0] // 6
    rows = shards * slots
    table_lanes = x_refs[0].shape[1] - width
    token_row = lax.broadcasted_iota(jnp.int32, (tok, tok), 0)
    token_col = lax.broadcasted_iota(jnp.int32, (tok, tok), 1)
    earlier_row = (token_row < token_col).astype(jnp.bfloat16)
    earlier_col = (token_col < token_row).astype(jnp.bfloat16)
    lane_tok = lax.broadcasted_iota(jnp.int32, (tok, table_lanes), 1)
    lane_few = lax.broadcasted_iota(jnp.int32, (8, table_lanes), 1)
    slot_rows = lax.broadcasted_iota(jnp.int32, (slots, tok), 0).astype(jnp.float32)
    slot_cols = lax.broadcasted_iota(jnp.int32, (tok, slots), 1).astype(jnp.float32)

    for s in range(shards):
        there = slice(s * slots, (s + 1) * slots)
        table = x_refs[s][:, width:]
        gathers, weights = [], []
        for q in range(2):
            expert = expert_ref[q]
            weight_row = dot((lane_few == expert).astype(jnp.bfloat16), table, NT)[0:1]
            picked_row = weight_row > 0.0
            rank_row = dot(
                jnp.broadcast_to(picked_row, (8, tok)).astype(jnp.bfloat16), earlier_row, NN
            )[0:1]
            gather = jnp.where(jnp.logical_and(slot_rows == rank_row, picked_row), 1.0, 0.0)
            gathers.append(gather)
            weights.append(jnp.sum(gather * weight_row, axis=1, keepdims=True))
            picked_col = (
                jnp.max(
                    jnp.where(lane_tok == expert, table.astype(jnp.float32), 0.0),
                    axis=1,
                    keepdims=True,
                )
                > 0.0
            )
            rank_col = dot(
                earlier_col, jnp.broadcast_to(picked_col, (tok, tok)).astype(jnp.bfloat16), NN
            )[:, 0:1]
            spread[s, q] = jnp.where(
                jnp.logical_and(slot_cols == rank_col, picked_col), 1.0, 0.0
            ).astype(jnp.bfloat16)
        gather = jnp.concatenate(gathers, axis=0).astype(jnp.bfloat16)
        weight = jnp.concatenate(weights, axis=0)
        x_rows = dot(gather, x_refs[s][:, :width], NN).astype(jnp.bfloat16)
        g_rows = dot(gather, g_refs[s][...], NN)
        s_rows = (g_rows * weight).astype(jnp.bfloat16)
        g_rows = g_rows.astype(jnp.bfloat16)
        for q in range(2):
            own = slice(q * slots, (q + 1) * slots)
            for c in range(feat):
                cut = slice(c * LANES, (c + 1) * LANES)
                xs[q, c, there, :] = x_rows[own, cut]
                gs[q, c, there, :] = g_rows[own, cut]
                ss[q, c, there, :] = s_rows[own, cut]

    def one_expert(q, carry):
        gate[...] = jnp.zeros_like(gate)
        up[...] = jnp.zeros_like(up)
        hgrad[...] = jnp.zeros_like(hgrad)
        pgrad[...] = jnp.zeros_like(pgrad)
        first = q * (3 * count)

        def place(m, b):
            at = 2 * (first + m * count + b)
            return lay_ref[at], lay_ref[at + 1]

        for b in range(count):
            r, c = place(0, b)
            gate[c] += dot(xs[q, r], w_ref[first + b], NN)
            r, c = place(1, b)
            up[c] += dot(xs[q, r], w_ref[first + count + b], NN)
            r, c = place(2, b)
            hgrad[r] += dot(ss[q, c], w_ref[first + 2 * count + b], NT)
        for h in range(hidden):
            gate_pre = gate[h]
            up_pre = up[h]
            sig = jax.nn.sigmoid(gate_pre)
            activated = gate_pre * sig
            hid[h] = (activated * up_pre).astype(jnp.bfloat16)
            hidden_grad = hgrad[h]
            ggrad[h] = (hidden_grad * up_pre * sig * (1.0 + gate_pre * (1.0 - sig))).astype(
                jnp.bfloat16
            )
            ugrad[h] = (hidden_grad * activated).astype(jnp.bfloat16)
        prod[...] = jnp.zeros_like(prod)
        for b in range(count):
            r, c = place(0, b)
            pgrad[r] += dot(ggrad[c], w_ref[first + b], NT)
            dw_ref[first + b] = dot(xs[q, r], ggrad[c], TN)
            r, c = place(1, b)
            pgrad[r] += dot(ugrad[c], w_ref[first + count + b], NT)
            dw_ref[first + count + b] = dot(xs[q, r], ugrad[c], TN)
            r, c = place(2, b)
            prod[...] += dot(hid[r], w_ref[first + 2 * count + b], NN) * gs[q, c].astype(
                jnp.float32
            )
            dw_ref[first + 2 * count + b] = dot(hid[r], ss[q, c], TN)
        for s in range(shards):
            there = slice(s * slots, (s + 1) * slots)
            for c in range(feat):
                wide[s, q, :, c * LANES : (c + 1) * LANES] = pgrad[c, there, :].astype(
                    jnp.bfloat16
                )
            score = jnp.sum(prod[there, :], axis=1, keepdims=True).astype(jnp.bfloat16)
            own_lane = (
                lax.broadcasted_iota(jnp.int32, (slots, table_lanes), 1) == expert_ref[q]
            )
            wide[s, q, :, width:] = jnp.where(own_lane, score.astype(jnp.float32), 0.0).astype(
                jnp.bfloat16
            )
        return carry

    lax.fori_loop(0, 2, one_expert, 0)
    for s in range(shards):
        total = dot(spread[s, 0], wide[s, 0], NN) + dot(spread[s, 1], wide[s, 1], NN)
        low_refs[s][...] = total[:, :half].astype(jnp.bfloat16)
        high_refs[s][...] = total[:, half:].astype(jnp.bfloat16)


def run_experts(x_list, g_list, mats, layouts, experts, slots):
    shards = len(x_list)
    tok, table_width = x_list[0].shape
    width = g_list[0].shape[1]
    half = width // 2
    feat = width // LANES
    hidden = HID // LANES
    rows = shards * slots
    block_count = mats.shape[0]
    bf16, f32 = jnp.bfloat16, jnp.float32
    smem = pl.BlockSpec(memory_space=pltpu.SMEM)
    vmem = pl.BlockSpec(memory_space=pltpu.VMEM)
    outs = pl.pallas_call(
        functools.partial(expert_kernel, shards, slots, half),
        in_specs=[smem, smem] + [vmem] * (2 * shards + 1),
        out_specs=[vmem] * (2 * shards + 1),
        out_shape=[jax.ShapeDtypeStruct((tok, half), bf16)] * shards
        + [jax.ShapeDtypeStruct((tok, table_width - half), bf16)] * shards
        + [jax.ShapeDtypeStruct((block_count, LANES, LANES), f32)],
        scratch_shapes=[
            pltpu.VMEM((2, feat, rows, LANES), bf16),
            pltpu.VMEM((2, feat, rows, LANES), bf16),
            pltpu.VMEM((2, feat, rows, LANES), bf16),
            pltpu.VMEM((hidden, rows, LANES), f32),
            pltpu.VMEM((hidden, rows, LANES), f32),
            pltpu.VMEM((hidden, rows, LANES), bf16),
            pltpu.VMEM((hidden, rows, LANES), f32),
            pltpu.VMEM((hidden, rows, LANES), bf16),
            pltpu.VMEM((hidden, rows, LANES), bf16),
            pltpu.VMEM((feat, rows, LANES), f32),
            pltpu.VMEM((shards, 2, slots, table_width), bf16),
            pltpu.VMEM((shards, 2, tok, slots), bf16),
            pltpu.VMEM((rows, LANES), f32),
        ],
        compiler_params=pltpu.CompilerParams(vmem_limit_bytes=48 * 1024 * 1024),
        cost_estimate=pl.CostEstimate(
            flops=2 * 2 * 108 * rows * LANES * LANES * 4,
            bytes_accessed=shards * tok * table_width * 6 + block_count * LANES * LANES * 6,
            transcendentals=0,
        ),
    )(layouts, experts, *x_list, *g_list, mats)
    return outs[:shards], outs[shards : 2 * shards], outs[2 * shards]


def chip_ring(chips):
    tall, broad = 4, chips // 4
    walk = []
    for row in range(tall):
        columns = list(range(0 if row == 0 else 1, broad))
        walk += [(row, c) for c in (columns if row % 2 == 0 else columns[::-1])]
    walk += [(row, 0) for row in range(tall - 1, 0, -1)]
    return [row * broad + c for row, c in walk]


def spread_out(state, expert_count):
    pieces = state.reshape(expert_count, -1, LANES)
    return lax.all_to_all(pieces, "expert", split_axis=0, concat_axis=0, tiled=True)


def collect(spread, partner, shape):
    moved = jnp.take(spread, partner, axis=0)
    return lax.all_to_all(moved, "expert", split_axis=0, concat_axis=0, tiled=True).reshape(shape)


def body(tokens, out_grad, expert_ids, route_weights, blocks, layout, moments, partner):
    expert_count = lax.axis_size("expert")
    replica_count = lax.axis_size("dp")
    tok_count, topk_count = expert_ids.shape
    width = tokens.shape[1]
    block_size = blocks.shape[-1]
    capacity = max(2, tok_count * topk_count * 7 // (expert_count * 6))
    slots = -(-capacity // 16) * 16
    table_lanes = -(-expert_count // LANES) * LANES
    bf16, f32 = jnp.bfloat16, jnp.float32
    chips = expert_count // 2
    ring = chip_ring(chips)
    steps = list(zip(ring, ring[1:] + ring[:1]))
    onward = [(2 * a + core, 2 * b + core) for a, b in steps for core in range(2)]
    backward = [(b, a) for a, b in onward]
    sister = [(i, i ^ 1) for i in range(expert_count)]
    row_share = block_size // replica_count
    replica = lax.axis_index("dp")

    def step_on(value):
        return lax.ppermute(value, "expert", onward)

    def step_back(value):
        return lax.ppermute(value, "expert", backward)

    def own_rows(value):
        return lax.dynamic_slice_in_dim(value, replica * row_share, row_share, 2)

    def join_rows(rows):
        if replica_count != 2:
            return lax.all_gather(rows, "dp", axis=2, tiled=True)
        other = lax.ppermute(rows, "dp", [(0, 1), (1, 0)])
        first = replica == 0
        return jnp.concatenate(
            [jnp.where(first, rows, other), jnp.where(first, other, rows)], axis=2
        )

    def sum_rows(value):
        if replica_count != 2:
            return lax.psum_scatter(value, "dp", scatter_dimension=2, tiled=True).astype(f32)
        theirs = lax.dynamic_slice_in_dim(value, (1 - replica) * row_share, row_share, 2)
        other = lax.ppermute(theirs, "dp", [(0, 1), (1, 0)])
        return own_rows(value).astype(f32) + other.astype(f32)

    lane = jnp.arange(table_lanes, dtype=jnp.int32)
    named = expert_ids[:, :, None] == lane[None, None, :]
    table = jnp.sum(jnp.where(named, route_weights[:, :, None].astype(f32), 0.0), axis=1).astype(
        bf16
    )
    me = lax.axis_index("expert")
    slots_here = jnp.stack([me, me ^ 1])
    experts = jnp.take(partner, slots_here).astype(jnp.int32)

    x_at = {0: jnp.concatenate([tokens, table], axis=1)}
    g_at = {0: out_grad}
    most = chips // 2
    for s in range(1, most + 1):
        x_at[-s] = step_on(x_at[1 - s])
        g_at[s] = step_back(g_at[s - 1])
        if s < most:
            x_at[s] = step_back(x_at[s - 1])
            g_at[-s] = step_on(g_at[1 - s])
    x_at[most] = x_at[-most]

    rows_now = own_rows(blocks[0])
    moved_rows = collect(spread_out(rows_now, expert_count), partner, rows_now.shape)
    own_mats = join_rows(moved_rows)
    other_mats = lax.ppermute(own_mats, "expert", sister)
    square = (-1, block_size, block_size)
    mats = jnp.concatenate([own_mats.reshape(square), other_mats.reshape(square)], axis=0)
    layouts = lax.all_gather(layout.reshape(1, -1), "expert", axis=0, tiled=True)
    layouts = jnp.take(layouts, experts, axis=0).reshape(-1)
    moved_moments = collect(
        spread_out(moments[0].astype(bf16), expert_count), partner, rows_now.shape
    )

    near = [0]
    for s in range(1, most):
        near += [s, -s]
    near += [most]
    groups = [near[:-3], near[-3:]] if chips <= 8 else [near[i : i + 8] for i in range(0, chips, 8)]
    parts, weight_grad = {}, None
    for group in groups:
        lows, highs, grads = run_experts(
            [x_at[d] for d in group], [g_at[d] for d in group], mats, layouts, experts, slots
        )
        for d, low, high in zip(group, lows, highs):
            parts[d] = (low, high)
        weight_grad = grads if weight_grad is None else weight_grad + grads

    def add(left, right):
        return (left.astype(f32) + right.astype(f32)).astype(bf16)

    def carry_home(part, direction, move, include):
        held = parts[most][part] if include else parts[direction * (most - 1)][part]
        if include:
            held = move(held)
            held = add(held, parts[direction * (most - 1)][part])
        for s in range(most - 2, 0, -1):
            held = add(move(held), parts[direction * s][part])
        return move(held)

    homes = []
    for part in range(2):
        up_way = carry_home(part, 1, step_on, part == 0)
        down_way = carry_home(part, -1, step_back, part == 1)
        homes.append(
            (
                parts[0][part].astype(f32) + up_way.astype(f32) + down_way.astype(f32)
            ).astype(bf16)
        )
    half = homes[0].shape[1]
    token_grad = jnp.concatenate([homes[0], homes[1][:, : width - half]], axis=1)
    scores = homes[1][:, width - half :]
    route_grad = jnp.sum(jnp.where(named, scores[:, None, :].astype(f32), 0.0), axis=2).astype(bf16)

    own_grad, other_grad = jnp.split(weight_grad.astype(bf16), 2, axis=0)
    from_sister = lax.ppermute(other_grad, "expert", sister)
    chip_grad = add(own_grad, from_sister).reshape(blocks[0].shape)
    shard_grad = sum_rows(chip_grad)
    new_moment = momentum_decay * moved_moments.astype(f32) + shard_grad
    new_shard = (moved_rows.astype(f32) - step_rate * new_moment).astype(bf16)
    return (token_grad, route_grad, join_rows(new_shard)[None], new_moment[None])


def solution(mesh):
    placed = (
        P(("dp", "expert"), None),
        P(("dp", "expert"), None),
        P(("dp", "expert"), None),
        P(("dp", "expert"), None),
        P("expert", None, None, None, None),
        P("expert", None, None, None),
        P("expert", None, None, "dp", None),
        P(),
    )
    return jax.shard_map(
        body,
        mesh=mesh,
        in_specs=placed,
        out_specs=(
            P(("dp", "expert"), None),
            P(("dp", "expert"), None),
            P("expert", None, None, None, None),
            P("expert", None, None, "dp", None),
        ),
        check_vma=False,
    )
```

```python
import functools

import jax
import jax.numpy as jnp
from jax import lax
from jax.experimental import pallas as pl
from jax.experimental.pallas import tpu as pltpu
from jax.sharding import PartitionSpec as P

HID = 1408
LANES = 128

momentum_decay = 0.9
step_rate = 0.01

NN = (((1,), (0,)), ((), ()))
NT = (((1,), (1,)), ((), ()))
TN = (((0,), (0,)), ((), ()))


def dot(left, right, dims):
    return lax.dot_general(left, right, dims, preferred_element_type=jnp.float32)


def expert_kernel(
    shards,
    slots,
    half,
    pieces,
    resumed,
    final,
    lay_ref,
    expert_ref,
    place_ref,
    *refs,
):
    x_refs, refs = refs[:shards], refs[shards:]
    g_refs, refs = refs[:shards], refs[shards:]
    piece_refs, refs = refs[:pieces], refs[pieces:]
    if resumed:
        so_far_ref, refs = refs[0], refs[1:]
    low_refs, refs = refs[:shards], refs[shards:]
    high_refs, refs = refs[:shards], refs[shards:]
    if final:
        own_ref, other_ref, refs = refs[0], refs[1], refs[2:]
    else:
        dw_ref, refs = refs[0], refs[1:]
    (
        w_ref,
        xs,
        gs,
        ss,
        gate,
        up,
        hid,
        hgrad,
        ggrad,
        ugrad,
        pgrad,
        wide,
        spread,
        prod,
    ) = refs
    tok = LANES
    feat = xs.shape[1]
    hidden = gate.shape[0]
    width = feat * LANES
    count = w_ref.shape[0] // 6
    rows = shards * slots
    table_lanes = x_refs[0].shape[1] - width
    token_row = lax.broadcasted_iota(jnp.int32, (tok, tok), 0)
    token_col = lax.broadcasted_iota(jnp.int32, (tok, tok), 1)
    earlier_row = (token_row < token_col).astype(jnp.bfloat16)
    earlier_col = (token_col < token_row).astype(jnp.bfloat16)
    lane_tok = lax.broadcasted_iota(jnp.int32, (tok, table_lanes), 1)
    lane_few = lax.broadcasted_iota(jnp.int32, (8, table_lanes), 1)
    slot_rows = lax.broadcasted_iota(jnp.int32, (slots, tok), 0).astype(jnp.float32)
    slot_cols = lax.broadcasted_iota(jnp.int32, (tok, slots), 1).astype(jnp.float32)

    in_expert = pieces // 2
    for i, piece in enumerate(piece_refs):
        q, rows_in = i // in_expert, piece.shape[1]
        first = pl.multiple_of(place_ref[i % in_expert], 16)
        w_ref[q * 3 * count : (q + 1) * 3 * count, pl.ds(first, rows_in), :] = piece[...]

    for s in range(shards):
        there = slice(s * slots, (s + 1) * slots)
        table = x_refs[s][:, width:]
        gathers, weights = [], []
        for q in range(2):
            expert = expert_ref[q]
            weight_row = dot((lane_few == expert).astype(jnp.bfloat16), table, NT)[0:1]
            picked_row = weight_row > 0.0
            rank_row = dot(
                jnp.broadcast_to(picked_row, (8, tok)).astype(jnp.bfloat16), earlier_row, NN
            )[0:1]
            gather = jnp.where(jnp.logical_and(slot_rows == rank_row, picked_row), 1.0, 0.0)
            gathers.append(gather)
            weights.append(jnp.sum(gather * weight_row, axis=1, keepdims=True))
            picked_col = (
                jnp.max(
                    jnp.where(lane_tok == expert, table.astype(jnp.float32), 0.0),
                    axis=1,
                    keepdims=True,
                )
                > 0.0
            )
            rank_col = dot(
                earlier_col, jnp.broadcast_to(picked_col, (tok, tok)).astype(jnp.bfloat16), NN
            )[:, 0:1]
            spread[s, q] = jnp.where(
                jnp.logical_and(slot_cols == rank_col, picked_col), 1.0, 0.0
            ).astype(jnp.bfloat16)
        gather = jnp.concatenate(gathers, axis=0).astype(jnp.bfloat16)
        weight = jnp.concatenate(weights, axis=0)
        x_rows = dot(gather, x_refs[s][:, :width], NN).astype(jnp.bfloat16)
        g_rows = dot(gather, g_refs[s][...], NN)
        s_rows = (g_rows * weight).astype(jnp.bfloat16)
        g_rows = g_rows.astype(jnp.bfloat16)
        for q in range(2):
            own = slice(q * slots, (q + 1) * slots)
            for c in range(feat):
                cut = slice(c * LANES, (c + 1) * LANES)
                xs[q, c, there, :] = x_rows[own, cut]
                gs[q, c, there, :] = g_rows[own, cut]
                ss[q, c, there, :] = s_rows[own, cut]

    def one_expert(q, carry):
        gate[...] = jnp.zeros_like(gate)
        up[...] = jnp.zeros_like(up)
        hgrad[...] = jnp.zeros_like(hgrad)
        pgrad[...] = jnp.zeros_like(pgrad)
        first = q * (3 * count)

        def keep(b, grad):
            if resumed:
                grad = grad + so_far_ref[first + b]
            if not final:
                dw_ref[first + b] = grad
                return

            @pl.when(q == 0)
            def _():
                own_ref[b] = grad.astype(jnp.bfloat16)

            @pl.when(q == 1)
            def _():
                other_ref[b] = grad.astype(jnp.bfloat16)

        def place(m, b):
            at = 2 * (first + m * count + b)
            return lay_ref[at], lay_ref[at + 1]

        for b in range(count):
            r, c = place(0, b)
            gate[c] += dot(xs[q, r], w_ref[first + b], NN)
            r, c = place(1, b)
            up[c] += dot(xs[q, r], w_ref[first + count + b], NN)
            r, c = place(2, b)
            hgrad[r] += dot(ss[q, c], w_ref[first + 2 * count + b], NT)
        for h in range(hidden):
            gate_pre = gate[h]
            up_pre = up[h]
            sig = jax.nn.sigmoid(gate_pre)
            activated = gate_pre * sig
            hid[h] = (activated * up_pre).astype(jnp.bfloat16)
            hidden_grad = hgrad[h]
            ggrad[h] = (hidden_grad * up_pre * sig * (1.0 + gate_pre * (1.0 - sig))).astype(
                jnp.bfloat16
            )
            ugrad[h] = (hidden_grad * activated).astype(jnp.bfloat16)
        prod[...] = jnp.zeros_like(prod)
        for b in range(count):
            r, c = place(0, b)
            pgrad[r] += dot(ggrad[c], w_ref[first + b], NT)
            keep(b, dot(xs[q, r], ggrad[c], TN))
            r, c = place(1, b)
            pgrad[r] += dot(ugrad[c], w_ref[first + count + b], NT)
            keep(count + b, dot(xs[q, r], ugrad[c], TN))
            r, c = place(2, b)
            prod[...] += dot(hid[r], w_ref[first + 2 * count + b], NN) * gs[q, c].astype(
                jnp.float32
            )
            keep(2 * count + b, dot(hid[r], ss[q, c], TN))
        for s in range(shards):
            there = slice(s * slots, (s + 1) * slots)
            for c in range(feat):
                wide[s, q, :, c * LANES : (c + 1) * LANES] = pgrad[c, there, :].astype(
                    jnp.bfloat16
                )
            score = jnp.sum(prod[there, :], axis=1, keepdims=True).astype(jnp.bfloat16)
            own_lane = (
                lax.broadcasted_iota(jnp.int32, (slots, table_lanes), 1) == expert_ref[q]
            )
            wide[s, q, :, width:] = jnp.where(own_lane, score.astype(jnp.float32), 0.0).astype(
                jnp.bfloat16
            )
        return carry

    lax.fori_loop(0, 2, one_expert, 0)
    for s in range(shards):
        total = dot(spread[s, 0], wide[s, 0], NN) + dot(spread[s, 1], wide[s, 1], NN)
        low_refs[s][...] = total[:, :half].astype(jnp.bfloat16)
        high_refs[s][...] = total[:, half:].astype(jnp.bfloat16)


def run_experts(x_list, g_list, weights, places, layouts, experts, slots, so_far, final):
    shards = len(x_list)
    tok, table_width = x_list[0].shape
    width = g_list[0].shape[1]
    half = width // 2
    feat = width // LANES
    hidden = HID // LANES
    rows = shards * slots
    block_count = 2 * weights[0].shape[0]
    resumed = so_far is not None
    bf16, f32 = jnp.bfloat16, jnp.float32
    smem = pl.BlockSpec(memory_space=pltpu.SMEM)
    vmem = pl.BlockSpec(memory_space=pltpu.VMEM)
    grads = jax.ShapeDtypeStruct((block_count, LANES, LANES), f32)
    one_grads = jax.ShapeDtypeStruct((block_count // 2, LANES, LANES), bf16)
    grad_out = [one_grads, one_grads] if final else [grads]
    operands = [*x_list, *g_list, *weights] + ([so_far] if resumed else [])
    outs = pl.pallas_call(
        functools.partial(
            expert_kernel, shards, slots, half, len(weights), resumed, final
        ),
        in_specs=[smem] * 3 + [vmem] * len(operands),
        out_specs=[vmem] * (2 * shards + len(grad_out)),
        out_shape=[jax.ShapeDtypeStruct((tok, half), bf16)] * shards
        + [jax.ShapeDtypeStruct((tok, table_width - half), bf16)] * shards
        + grad_out,
        scratch_shapes=[
            pltpu.VMEM((block_count, LANES, LANES), bf16),
            pltpu.VMEM((2, feat, rows, LANES), bf16),
            pltpu.VMEM((2, feat, rows, LANES), bf16),
            pltpu.VMEM((2, feat, rows, LANES), bf16),
            pltpu.VMEM((hidden, rows, LANES), f32),
            pltpu.VMEM((hidden, rows, LANES), f32),
            pltpu.VMEM((hidden, rows, LANES), bf16),
            pltpu.VMEM((hidden, rows, LANES), f32),
            pltpu.VMEM((hidden, rows, LANES), bf16),
            pltpu.VMEM((hidden, rows, LANES), bf16),
            pltpu.VMEM((feat, rows, LANES), f32),
            pltpu.VMEM((shards, 2, slots, table_width), bf16),
            pltpu.VMEM((shards, 2, tok, slots), bf16),
            pltpu.VMEM((rows, LANES), f32),
        ],
        compiler_params=pltpu.CompilerParams(vmem_limit_bytes=44 * 1024 * 1024),
        cost_estimate=pl.CostEstimate(
            flops=2 * 2 * 108 * rows * LANES * LANES * 4,
            bytes_accessed=shards * tok * table_width * 6 + block_count * LANES * LANES * 6,
            transcendentals=0,
        ),
    )(layouts, experts, places, *operands)
    return outs[:shards], outs[shards : 2 * shards], outs[2 * shards :]


def chip_ring(chips):
    tall, broad = 4, chips // 4
    walk = []
    for row in range(tall):
        columns = list(range(0 if row == 0 else 1, broad))
        walk += [(row, c) for c in (columns if row % 2 == 0 else columns[::-1])]
    walk += [(row, 0) for row in range(tall - 1, 0, -1)]
    return [row * broad + c for row, c in walk]


def swap_all(pieces):
    return lax.all_to_all(pieces, "expert", split_axis=0, concat_axis=0, tiled=True)


def body(tokens, out_grad, expert_ids, route_weights, blocks, layout, moments, partner):
    expert_count = lax.axis_size("expert")
    replica_count = lax.axis_size("dp")
    tok_count, topk_count = expert_ids.shape
    width = tokens.shape[1]
    block_size = blocks.shape[-1]
    capacity = max(2, tok_count * topk_count * 7 // (expert_count * 6))
    slots = -(-capacity // 16) * 16
    table_lanes = -(-expert_count // LANES) * LANES
    bf16, f32 = jnp.bfloat16, jnp.float32
    chips = expert_count // 2
    ring = chip_ring(chips)
    steps = list(zip(ring, ring[1:] + ring[:1]))
    onward = [(2 * a + core, 2 * b + core) for a, b in steps for core in range(2)]
    backward = [(b, a) for a, b in onward]
    sister = [(i, i ^ 1) for i in range(expert_count)]
    row_share = block_size // replica_count
    replica = lax.axis_index("dp")

    def step_on(value):
        return lax.ppermute(value, "expert", onward)

    def step_back(value):
        return lax.ppermute(value, "expert", backward)

    def own_rows(value):
        return lax.dynamic_slice_in_dim(value, replica * row_share, row_share, 2)

    def other_replica(value):
        return lax.ppermute(value, "dp", [(0, 1), (1, 0)])

    def other_core(value):
        return lax.ppermute(value, "expert", sister)

    def join_rows(rows):
        if replica_count != 2:
            return lax.all_gather(rows, "dp", axis=2, tiled=True)
        mine_here = (jnp.arange(2, dtype=jnp.int32) == replica)[None, None, :, None, None]
        both = jnp.where(mine_here, rows[:, :, None], other_replica(rows)[:, :, None])
        return both.reshape(rows.shape[:2] + (block_size,) + rows.shape[3:])

    def sum_rows(one, two):
        if replica_count != 2:
            return lax.psum_scatter(add(one, two), "dp", scatter_dimension=2, tiled=True).astype(f32)

        def half_of(index):
            return sum(
                lax.dynamic_slice_in_dim(value, index * row_share, row_share, 2).astype(f32)
                for value in (one, two)
            )

        theirs = other_replica(half_of(1 - replica).astype(bf16))
        return half_of(replica) + theirs.astype(f32)

    def add(left, right):
        return (left.astype(f32) + right.astype(f32)).astype(bf16)

    lane = jnp.arange(table_lanes, dtype=jnp.int32)
    named = expert_ids[:, :, None] == lane[None, None, :]
    table = jnp.sum(jnp.where(named, route_weights[:, :, None].astype(f32), 0.0), axis=1).astype(
        bf16
    )
    me = lax.axis_index("expert")
    slots_here = jnp.stack([me, me ^ 1])
    experts = jnp.take(partner, slots_here).astype(jnp.int32)

    x_at = {0: jnp.concatenate([tokens, table], axis=1)}
    most = chips // 2
    x_at[-1], x_at[1] = step_on(x_at[0]), step_back(x_at[0])
    rows_now = own_rows(blocks[0])
    x_at[-1], x_at[1], rows_ready, g_ready = lax.optimization_barrier(
        (x_at[-1], x_at[1], rows_now, out_grad)
    )

    note_rows = 16
    layout_flat = layout.reshape(-1)
    layout_note = jnp.zeros((note_rows * LANES,), bf16).at[: layout_flat.shape[0]].set(
        layout_flat.astype(bf16)
    )
    pieces = rows_ready.reshape(expert_count, -1, LANES)
    piece_rows = pieces.shape[1]
    pieces = jnp.concatenate(
        [
            pieces,
            jnp.broadcast_to(
                layout_note.reshape(1, note_rows, LANES), (expert_count, note_rows, LANES)
            ),
        ],
        axis=1,
    )
    spread = swap_all(pieces)
    layouts = spread[:, piece_rows:].reshape(expert_count, -1)[:, : layout_flat.shape[0]]
    layouts = jnp.take(layouts, experts, axis=0).reshape(-1).astype(jnp.int32)
    moved_rows = swap_all(jnp.take(spread[:, :piece_rows], partner, axis=0)).reshape(
        rows_now.shape
    )
    moved_rows, moments_ready = lax.optimization_barrier((moved_rows, moments))
    moment_pieces = moments_ready[0].astype(bf16).reshape(expert_count, -1, LANES)
    moved_moments = swap_all(jnp.take(swap_all(moment_pieces), partner, axis=0)).reshape(
        rows_now.shape
    )

    g_at = {0: g_ready}
    for s in range(1, most + 1):
        if s > 1:
            x_at[-s] = step_on(x_at[1 - s])
            if s < most:
                x_at[s] = step_back(x_at[s - 1])
        g_at[s] = step_back(g_at[s - 1])
        if s < most:
            g_at[-s] = step_on(g_at[1 - s])
    x_at[most] = x_at[-most]

    if replica_count == 2:
        halves = [moved_rows, other_replica(moved_rows)]
        places = jnp.stack([replica * row_share, (1 - replica) * row_share]).astype(jnp.int32)
    else:
        halves = [join_rows(moved_rows)]
        places = jnp.zeros((1,), jnp.int32)
    weights = halves + [other_core(value) for value in halves]
    weights = [value.reshape(-1, value.shape[2], LANES) for value in weights]

    near = [0]
    for s in range(1, most):
        near += [s, -s]
    near += [most]
    if chips <= 8:
        groups = [near[:3], near[3:-1], near[-1:]]
    else:
        groups = [near[i : i + 8] for i in range(0, chips, 8)]
    parts, sums = {}, [None]
    for group in groups:
        lows, highs, sums = run_experts(
            [x_at[d] for d in group],
            [g_at[d] for d in group],
            weights,
            places,
            layouts,
            experts,
            slots,
            sums[0],
            group is groups[-1],
        )
        for d, low, high in zip(group, lows, highs):
            parts[d] = (low, high)
    own_grad, other_grad = (value.reshape(blocks[0].shape) for value in sums)
    from_sister = other_core(other_grad)

    def carry_home(part, direction, move, include):
        held = parts[most][part] if include else parts[direction * (most - 1)][part]
        if include:
            held = move(held)
            held = add(held, parts[direction * (most - 1)][part])
        for s in range(most - 2, 0, -1):
            held = add(move(held), parts[direction * s][part])
        return move(held)

    homes = []
    for part in range(2):
        up_way = carry_home(part, 1, step_on, part == 0)
        down_way = carry_home(part, -1, step_back, part == 1)
        homes.append(
            (
                parts[0][part].astype(f32) + up_way.astype(f32) + down_way.astype(f32)
            ).astype(bf16)
        )
    half = homes[0].shape[1]
    token_grad = jnp.concatenate([homes[0], homes[1][:, : width - half]], axis=1)
    scores = homes[1][:, width - half :]
    route_grad = jnp.sum(jnp.where(named, scores[:, None, :].astype(f32), 0.0), axis=2).astype(bf16)

    shard_grad = sum_rows(own_grad, from_sister)
    new_moment = momentum_decay * moved_moments.astype(f32) + shard_grad
    new_shard = (moved_rows.astype(f32) - step_rate * new_moment).astype(bf16)
    return (token_grad, route_grad, join_rows(new_shard)[None], new_moment[None])


def solution(mesh):
    placed = (
        P(("dp", "expert"), None),
        P(("dp", "expert"), None),
        P(("dp", "expert"), None),
        P(("dp", "expert"), None),
        P("expert", None, None, None, None),
        P("expert", None, None, None),
        P("expert", None, None, "dp", None),
        P(),
    )
    return jax.shard_map(
        body,
        mesh=mesh,
        in_specs=placed,
        out_specs=(
            P(("dp", "expert"), None),
            P(("dp", "expert"), None),
            P("expert", None, None, None, None),
            P("expert", None, None, "dp", None),
        ),
        check_vma=False,
    )
```

```python
import functools

import jax
import jax.numpy as jnp
from jax import lax
from jax.experimental import pallas as pl
from jax.experimental.pallas import tpu as pltpu
from jax.sharding import PartitionSpec as P

HID = 1408
LANES = 128

momentum_decay = 0.9
step_rate = 0.01

NN = (((1,), (0,)), ((), ()))
NT = (((1,), (1,)), ((), ()))
TN = (((0,), (0,)), ((), ()))


def dot(left, right, dims):
    return lax.dot_general(left, right, dims, preferred_element_type=jnp.float32)


def expert_kernel(
    shards,
    slots,
    half,
    pieces,
    resumed,
    lay_ref,
    expert_ref,
    place_ref,
    *refs,
):
    x_refs, refs = refs[:shards], refs[shards:]
    g_refs, refs = refs[:shards], refs[shards:]
    piece_refs, refs = refs[:pieces], refs[pieces:]
    if resumed:
        so_far_ref, refs = refs[0], refs[1:]
    low_refs, refs = refs[:shards], refs[shards:]
    high_refs, refs = refs[:shards], refs[shards:]
    (
        dw_ref,
        w_ref,
        xs,
        gs,
        ss,
        gate,
        up,
        hid,
        hgrad,
        ggrad,
        ugrad,
        pgrad,
        wide,
        spread,
        prod,
    ) = refs
    tok = LANES
    feat = xs.shape[1]
    hidden = gate.shape[0]
    width = feat * LANES
    count = w_ref.shape[0] // 6
    rows = shards * slots
    table_lanes = x_refs[0].shape[1] - width
    token_row = lax.broadcasted_iota(jnp.int32, (tok, tok), 0)
    token_col = lax.broadcasted_iota(jnp.int32, (tok, tok), 1)
    earlier_row = (token_row < token_col).astype(jnp.bfloat16)
    earlier_col = (token_col < token_row).astype(jnp.bfloat16)
    lane_tok = lax.broadcasted_iota(jnp.int32, (tok, table_lanes), 1)
    lane_few = lax.broadcasted_iota(jnp.int32, (8, table_lanes), 1)
    slot_rows = lax.broadcasted_iota(jnp.int32, (slots, tok), 0).astype(jnp.float32)
    slot_cols = lax.broadcasted_iota(jnp.int32, (tok, slots), 1).astype(jnp.float32)

    in_expert = pieces // 2
    for i, piece in enumerate(piece_refs):
        q, rows_in = i // in_expert, piece.shape[1]
        first = pl.multiple_of(place_ref[i % in_expert], 16)
        w_ref[q * 3 * count : (q + 1) * 3 * count, pl.ds(first, rows_in), :] = piece[...]

    for s in range(shards):
        there = slice(s * slots, (s + 1) * slots)
        table = x_refs[s][:, width:]
        gathers, weights = [], []
        for q in range(2):
            expert = expert_ref[q]
            weight_row = dot((lane_few == expert).astype(jnp.bfloat16), table, NT)[0:1]
            picked_row = weight_row > 0.0
            rank_row = dot(
                jnp.broadcast_to(picked_row, (8, tok)).astype(jnp.bfloat16), earlier_row, NN
            )[0:1]
            gather = jnp.where(jnp.logical_and(slot_rows == rank_row, picked_row), 1.0, 0.0)
            gathers.append(gather)
            weights.append(jnp.sum(gather * weight_row, axis=1, keepdims=True))
            picked_col = (
                jnp.max(
                    jnp.where(lane_tok == expert, table.astype(jnp.float32), 0.0),
                    axis=1,
                    keepdims=True,
                )
                > 0.0
            )
            rank_col = dot(
                earlier_col, jnp.broadcast_to(picked_col, (tok, tok)).astype(jnp.bfloat16), NN
            )[:, 0:1]
            spread[s, q] = jnp.where(
                jnp.logical_and(slot_cols == rank_col, picked_col), 1.0, 0.0
            ).astype(jnp.bfloat16)
        gather = jnp.concatenate(gathers, axis=0).astype(jnp.bfloat16)
        weight = jnp.concatenate(weights, axis=0)
        x_rows = dot(gather, x_refs[s][:, :width], NN).astype(jnp.bfloat16)
        g_rows = dot(gather, g_refs[s][...], NN)
        s_rows = (g_rows * weight).astype(jnp.bfloat16)
        g_rows = g_rows.astype(jnp.bfloat16)
        for q in range(2):
            own = slice(q * slots, (q + 1) * slots)
            for c in range(feat):
                cut = slice(c * LANES, (c + 1) * LANES)
                xs[q, c, there, :] = x_rows[own, cut]
                gs[q, c, there, :] = g_rows[own, cut]
                ss[q, c, there, :] = s_rows[own, cut]

    def one_expert(q, carry):
        gate[...] = jnp.zeros_like(gate)
        up[...] = jnp.zeros_like(up)
        hgrad[...] = jnp.zeros_like(hgrad)
        pgrad[...] = jnp.zeros_like(pgrad)
        first = q * (3 * count)

        def keep(b, grad):
            if resumed:
                grad = grad + so_far_ref[first + b]
            dw_ref[first + b] = grad.astype(dw_ref.dtype)

        def place(m, b):
            at = 2 * (first + m * count + b)
            return lay_ref[at], lay_ref[at + 1]

        for b in range(count):
            r, c = place(0, b)
            gate[c] += dot(xs[q, r], w_ref[first + b], NN)
            r, c = place(1, b)
            up[c] += dot(xs[q, r], w_ref[first + count + b], NN)
            r, c = place(2, b)
            hgrad[r] += dot(ss[q, c], w_ref[first + 2 * count + b], NT)
        for h in range(hidden):
            gate_pre = gate[h]
            up_pre = up[h]
            sig = jax.nn.sigmoid(gate_pre)
            activated = gate_pre * sig
            hid[h] = (activated * up_pre).astype(jnp.bfloat16)
            hidden_grad = hgrad[h]
            ggrad[h] = (hidden_grad * up_pre * sig * (1.0 + gate_pre * (1.0 - sig))).astype(
                jnp.bfloat16
            )
            ugrad[h] = (hidden_grad * activated).astype(jnp.bfloat16)
        prod[...] = jnp.zeros_like(prod)
        for b in range(count):
            r, c = place(0, b)
            pgrad[r] += dot(ggrad[c], w_ref[first + b], NT)
            keep(b, dot(xs[q, r], ggrad[c], TN))
            r, c = place(1, b)
            pgrad[r] += dot(ugrad[c], w_ref[first + count + b], NT)
            keep(count + b, dot(xs[q, r], ugrad[c], TN))
            r, c = place(2, b)
            prod[...] += dot(hid[r], w_ref[first + 2 * count + b], NN) * gs[q, c].astype(
                jnp.float32
            )
            keep(2 * count + b, dot(hid[r], ss[q, c], TN))
        for s in range(shards):
            there = slice(s * slots, (s + 1) * slots)
            for c in range(feat):
                wide[s, q, :, c * LANES : (c + 1) * LANES] = pgrad[c, there, :].astype(
                    jnp.bfloat16
                )
            score = jnp.sum(prod[there, :], axis=1, keepdims=True).astype(jnp.bfloat16)
            own_lane = (
                lax.broadcasted_iota(jnp.int32, (slots, table_lanes), 1) == expert_ref[q]
            )
            wide[s, q, :, width:] = jnp.where(own_lane, score.astype(jnp.float32), 0.0).astype(
                jnp.bfloat16
            )
        return carry

    lax.fori_loop(0, 2, one_expert, 0)
    for s in range(shards):
        total = dot(spread[s, 0], wide[s, 0], NN) + dot(spread[s, 1], wide[s, 1], NN)
        low_refs[s][...] = total[:, :half].astype(jnp.bfloat16)
        high_refs[s][...] = total[:, half:].astype(jnp.bfloat16)


def run_experts(x_list, g_list, weights, places, layouts, experts, slots, so_far, final):
    shards = len(x_list)
    tok, table_width = x_list[0].shape
    width = g_list[0].shape[1]
    half = width // 2
    feat = width // LANES
    hidden = HID // LANES
    rows = shards * slots
    block_count = 2 * weights[0].shape[0]
    resumed = so_far is not None
    bf16, f32 = jnp.bfloat16, jnp.float32
    smem = pl.BlockSpec(memory_space=pltpu.SMEM)
    vmem = pl.BlockSpec(memory_space=pltpu.VMEM)
    grads = jax.ShapeDtypeStruct((block_count, LANES, LANES), bf16 if final else f32)
    operands = [*x_list, *g_list, *weights] + ([so_far] if resumed else [])
    outs = pl.pallas_call(
        functools.partial(
            expert_kernel, shards, slots, half, len(weights), resumed
        ),
        in_specs=[smem] * 3 + [vmem] * len(operands),
        out_specs=[vmem] * (2 * shards + 1),
        out_shape=[jax.ShapeDtypeStruct((tok, half), bf16)] * shards
        + [jax.ShapeDtypeStruct((tok, table_width - half), bf16)] * shards
        + [grads],
        scratch_shapes=[
            pltpu.VMEM((block_count, LANES, LANES), bf16),
            pltpu.VMEM((2, feat, rows, LANES), bf16),
            pltpu.VMEM((2, feat, rows, LANES), bf16),
            pltpu.VMEM((2, feat, rows, LANES), bf16),
            pltpu.VMEM((hidden, rows, LANES), f32),
            pltpu.VMEM((hidden, rows, LANES), f32),
            pltpu.VMEM((hidden, rows, LANES), bf16),
            pltpu.VMEM((hidden, rows, LANES), f32),
            pltpu.VMEM((hidden, rows, LANES), bf16),
            pltpu.VMEM((hidden, rows, LANES), bf16),
            pltpu.VMEM((feat, rows, LANES), f32),
            pltpu.VMEM((shards, 2, slots, table_width), bf16),
            pltpu.VMEM((shards, 2, tok, slots), bf16),
            pltpu.VMEM((rows, LANES), f32),
        ],
        compiler_params=pltpu.CompilerParams(vmem_limit_bytes=44 * 1024 * 1024),
        cost_estimate=pl.CostEstimate(
            flops=2 * 2 * 108 * rows * LANES * LANES * 4,
            bytes_accessed=shards * tok * table_width * 6 + block_count * LANES * LANES * 6,
            transcendentals=0,
        ),
    )(layouts, experts, places, *operands)
    return outs[:shards], outs[shards : 2 * shards], outs[2 * shards]


def chip_ring(chips):
    tall, broad = 4, chips // 4
    walk = []
    for row in range(tall):
        columns = list(range(0 if row == 0 else 1, broad))
        walk += [(row, c) for c in (columns if row % 2 == 0 else columns[::-1])]
    walk += [(row, 0) for row in range(tall - 1, 0, -1)]
    return [row * broad + c for row, c in walk]


def swap_all(pieces):
    return lax.all_to_all(pieces, "expert", split_axis=0, concat_axis=0, tiled=True)


def body(tokens, out_grad, expert_ids, route_weights, blocks, layout, moments, partner):
    expert_count = lax.axis_size("expert")
    replica_count = lax.axis_size("dp")
    tok_count, topk_count = expert_ids.shape
    width = tokens.shape[1]
    block_size = blocks.shape[-1]
    capacity = max(2, tok_count * topk_count * 7 // (expert_count * 6))
    slots = -(-capacity // 16) * 16
    table_lanes = -(-expert_count // LANES) * LANES
    bf16, f32 = jnp.bfloat16, jnp.float32
    chips = expert_count // 2
    ring = chip_ring(chips)
    steps = list(zip(ring, ring[1:] + ring[:1]))
    onward = [(2 * a + core, 2 * b + core) for a, b in steps for core in range(2)]
    backward = [(b, a) for a, b in onward]
    sister = [(i, i ^ 1) for i in range(expert_count)]
    row_share = block_size // replica_count
    replica = lax.axis_index("dp")

    def step_on(value):
        return lax.ppermute(value, "expert", onward)

    def step_back(value):
        return lax.ppermute(value, "expert", backward)

    def own_rows(value):
        return lax.dynamic_slice_in_dim(value, replica * row_share, row_share, 2)

    def other_replica(value):
        return lax.ppermute(value, "dp", [(0, 1), (1, 0)])

    def other_core(value):
        return lax.ppermute(value, "expert", sister)

    def join_rows(rows):
        if replica_count != 2:
            return lax.all_gather(rows, "dp", axis=2, tiled=True)
        mine_here = (jnp.arange(2, dtype=jnp.int32) == replica)[None, None, :, None, None]
        both = jnp.where(mine_here, rows[:, :, None], other_replica(rows)[:, :, None])
        return both.reshape(rows.shape[:2] + (block_size,) + rows.shape[3:])

    def sum_rows(one, two):
        if replica_count != 2:
            return lax.psum_scatter(add(one, two), "dp", scatter_dimension=2, tiled=True).astype(f32)

        def half_of(index):
            return sum(
                lax.dynamic_slice_in_dim(value, index * row_share, row_share, 2).astype(f32)
                for value in (one, two)
            )

        theirs = other_replica(half_of(1 - replica).astype(bf16))
        return half_of(replica) + theirs.astype(f32)

    def add(left, right):
        return (left.astype(f32) + right.astype(f32)).astype(bf16)

    lane = jnp.arange(table_lanes, dtype=jnp.int32)
    named = expert_ids[:, :, None] == lane[None, None, :]
    table = jnp.sum(jnp.where(named, route_weights[:, :, None].astype(f32), 0.0), axis=1).astype(
        bf16
    )
    me = lax.axis_index("expert")
    slots_here = jnp.stack([me, me ^ 1])
    experts = jnp.take(partner, slots_here).astype(jnp.int32)

    note_rows = 16
    layout_flat = layout.reshape(-1)
    layout_note = jnp.zeros((note_rows * LANES,), bf16).at[: layout_flat.shape[0]].set(
        layout_flat.astype(bf16)
    )
    rows_now = own_rows(blocks[0])
    pieces = rows_now.reshape(expert_count, -1, LANES)
    piece_rows = pieces.shape[1]
    note = jnp.broadcast_to(
        layout_note.reshape(1, note_rows, LANES), (expert_count, note_rows, LANES)
    )
    state = {"pieces": jnp.concatenate([pieces, note], axis=1)}
    moment_pieces = moments[0].astype(bf16).reshape(expert_count, -1, LANES)
    x_at = {0: jnp.concatenate([tokens, table], axis=1)}
    g_at = {0: out_grad}
    most = chips // 2
    near = [0]
    for s in range(1, most):
        near += [s, -s]
    near += [most]
    if chips <= 8:
        groups = [near[:3], near[3:-1], near[-1:]]
    else:
        groups = [near[i : i + 8] for i in range(0, chips, 8)]
    parts = {}

    def run_group(group, so_far):
        lows, highs, sums = run_experts(
            [x_at[d] for d in group],
            [g_at[d] for d in group],
            state["weights"],
            places,
            state["layouts"],
            experts,
            slots,
            so_far,
            group is groups[-1],
        )
        for d, low, high in zip(group, lows, highs):
            parts[d] = (low, high)
        return sums

    if replica_count == 2:
        places = jnp.stack([replica * row_share, (1 - replica) * row_share]).astype(jnp.int32)
    else:
        places = jnp.zeros((1,), jnp.int32)
    for s in range(1, most + 1):
        x_at[-s] = step_on(x_at[1 - s])
        g_at[s] = step_back(g_at[s - 1])
        if s < most:
            x_at[s] = step_back(x_at[s - 1])
            g_at[-s] = step_on(g_at[1 - s])
        if s == 1:
            state["spread"] = swap_all(state.pop("pieces"))
        elif s == 2:
            spread = state.pop("spread")
            layouts = spread[:, piece_rows:].reshape(expert_count, -1)[:, : layout_flat.shape[0]]
            state["layouts"] = jnp.take(layouts, experts, axis=0).reshape(-1).astype(jnp.int32)
            state["rows"] = swap_all(jnp.take(spread[:, :piece_rows], partner, axis=0)).reshape(
                rows_now.shape
            )
        elif s == 3:
            halves = [state["rows"]]
            if replica_count == 2:
                halves.append(other_replica(state["rows"]))
            else:
                halves = [join_rows(state["rows"])]
            weights = halves + [other_core(value) for value in halves]
            state["weights"] = [value.reshape(-1, value.shape[2], LANES) for value in weights]
            state["moments"] = swap_all(moment_pieces)
        elif s == 4:
            state["sums"] = run_group(groups[0], None)
        x_at, g_at, state, parts = lax.optimization_barrier((x_at, g_at, state, parts))
    x_at[most] = x_at[-most]
    sums = state["sums"]
    moved_moments = swap_all(jnp.take(state["moments"], partner, axis=0)).reshape(rows_now.shape)
    for group in groups[1:-1]:
        sums = run_group(group, sums)
    sums, moved_moments = lax.optimization_barrier((sums, moved_moments))
    sums = run_group(groups[-1], sums)
    half_count = sums.shape[0] // 2
    own_grad = sums[:half_count].reshape(blocks[0].shape)
    from_sister = other_core(sums[half_count:].reshape(blocks[0].shape))
    moved_rows = state["rows"]

    def own_share(distance, part):
        return parts[distance][part]

    upward = [step_on(own_share(most, 0)), None]
    downward = [None, step_back(own_share(most, 1))]
    for s in range(most - 1, 0, -1):
        for part in range(2):
            share = own_share(s, part)
            upward[part] = step_on(share if upward[part] is None else add(upward[part], share))
            share = own_share(-s, part)
            downward[part] = step_back(
                share if downward[part] is None else add(downward[part], share)
            )
        if s == most - 1:
            upward[0], from_sister = lax.optimization_barrier((upward[0], from_sister))
            shard_grad = sum_rows(own_grad, from_sister)
        elif s == most - 2:
            upward[0], shard_grad = lax.optimization_barrier((upward[0], shard_grad))
            new_moment = momentum_decay * moved_moments.astype(f32) + shard_grad
            new_shard = (moved_rows.astype(f32) - step_rate * new_moment).astype(bf16)
    homes = [
        (parts[0][part].astype(f32) + upward[part].astype(f32) + downward[part].astype(f32)).astype(
            bf16
        )
        for part in range(2)
    ]
    half = homes[0].shape[1]
    token_grad = jnp.concatenate([homes[0], homes[1][:, : width - half]], axis=1)
    scores = homes[1][:, width - half :]
    route_grad = jnp.sum(jnp.where(named, scores[:, None, :].astype(f32), 0.0), axis=2).astype(bf16)
    return (token_grad, route_grad, join_rows(new_shard)[None], new_moment[None])


def solution(mesh):
    placed = (
        P(("dp", "expert"), None),
        P(("dp", "expert"), None),
        P(("dp", "expert"), None),
        P(("dp", "expert"), None),
        P("expert", None, None, None, None),
        P("expert", None, None, None),
        P("expert", None, None, "dp", None),
        P(),
    )
    return jax.shard_map(
        body,
        mesh=mesh,
        in_specs=placed,
        out_specs=(
            P(("dp", "expert"), None),
            P(("dp", "expert"), None),
            P("expert", None, None, None, None),
            P("expert", None, None, "dp", None),
        ),
        check_vma=False,
    )
```

```python
import functools

import jax
import jax.numpy as jnp
from jax import lax
from jax.experimental import pallas as pl
from jax.experimental.pallas import tpu as pltpu
from jax.sharding import PartitionSpec as P

HID = 1408
LANES = 128

momentum_decay = 0.9
step_rate = 0.01

NN = (((1,), (0,)), ((), ()))
NT = (((1,), (1,)), ((), ()))
TN = (((0,), (0,)), ((), ()))


def dot(left, right, dims):
    return lax.dot_general(left, right, dims, preferred_element_type=jnp.float32)


def expert_kernel(
    shards,
    slots,
    half,
    pieces,
    resumed,
    added,
    lay_ref,
    expert_ref,
    place_ref,
    *refs,
):
    x_refs, refs = refs[:shards], refs[shards:]
    g_refs, refs = refs[:shards], refs[shards:]
    piece_refs, refs = refs[:pieces], refs[pieces:]
    if resumed:
        so_far_ref, refs = refs[0], refs[1:]
    if added:
        low_so_far, refs = refs[:shards], refs[shards:]
        high_so_far, refs = refs[:shards], refs[shards:]
    low_refs, refs = refs[:shards], refs[shards:]
    high_refs, refs = refs[:shards], refs[shards:]
    (
        dw_ref,
        w_ref,
        xs,
        gs,
        ss,
        gate,
        up,
        hid,
        hgrad,
        ggrad,
        ugrad,
        pgrad,
        wide,
        spread,
        prod,
    ) = refs
    tok = LANES
    feat = xs.shape[1]
    hidden = gate.shape[0]
    width = feat * LANES
    count = w_ref.shape[0] // 6
    rows = shards * slots
    table_lanes = x_refs[0].shape[1] - width
    token_row = lax.broadcasted_iota(jnp.int32, (tok, tok), 0)
    token_col = lax.broadcasted_iota(jnp.int32, (tok, tok), 1)
    earlier_row = (token_row < token_col).astype(jnp.bfloat16)
    earlier_col = (token_col < token_row).astype(jnp.bfloat16)
    lane_tok = lax.broadcasted_iota(jnp.int32, (tok, table_lanes), 1)
    lane_few = lax.broadcasted_iota(jnp.int32, (8, table_lanes), 1)
    slot_rows = lax.broadcasted_iota(jnp.int32, (slots, tok), 0).astype(jnp.float32)
    slot_cols = lax.broadcasted_iota(jnp.int32, (tok, slots), 1).astype(jnp.float32)

    in_expert = pieces // 2
    for i, piece in enumerate(piece_refs):
        q, rows_in = i // in_expert, piece.shape[1]
        first = pl.multiple_of(place_ref[i % in_expert], 16)
        w_ref[q * 3 * count : (q + 1) * 3 * count, pl.ds(first, rows_in), :] = piece[...]

    for s in range(shards):
        there = slice(s * slots, (s + 1) * slots)
        table = x_refs[s][:, width:]
        gathers, weights = [], []
        for q in range(2):
            expert = expert_ref[q]
            weight_row = dot((lane_few == expert).astype(jnp.bfloat16), table, NT)[0:1]
            picked_row = weight_row > 0.0
            rank_row = dot(
                jnp.broadcast_to(picked_row, (8, tok)).astype(jnp.bfloat16), earlier_row, NN
            )[0:1]
            gather = jnp.where(jnp.logical_and(slot_rows == rank_row, picked_row), 1.0, 0.0)
            gathers.append(gather)
            weights.append(jnp.sum(gather * weight_row, axis=1, keepdims=True))
            picked_col = (
                jnp.max(
                    jnp.where(lane_tok == expert, table.astype(jnp.float32), 0.0),
                    axis=1,
                    keepdims=True,
                )
                > 0.0
            )
            rank_col = dot(
                earlier_col, jnp.broadcast_to(picked_col, (tok, tok)).astype(jnp.bfloat16), NN
            )[:, 0:1]
            spread[s, q] = jnp.where(
                jnp.logical_and(slot_cols == rank_col, picked_col), 1.0, 0.0
            ).astype(jnp.bfloat16)
        gather = jnp.concatenate(gathers, axis=0).astype(jnp.bfloat16)
        weight = jnp.concatenate(weights, axis=0)
        x_rows = dot(gather, x_refs[s][:, :width], NN).astype(jnp.bfloat16)
        g_rows = dot(gather, g_refs[s][...], NN)
        s_rows = (g_rows * weight).astype(jnp.bfloat16)
        g_rows = g_rows.astype(jnp.bfloat16)
        for q in range(2):
            own = slice(q * slots, (q + 1) * slots)
            for c in range(feat):
                cut = slice(c * LANES, (c + 1) * LANES)
                xs[q, c, there, :] = x_rows[own, cut]
                gs[q, c, there, :] = g_rows[own, cut]
                ss[q, c, there, :] = s_rows[own, cut]

    def one_expert(q, carry):
        gate[...] = jnp.zeros_like(gate)
        up[...] = jnp.zeros_like(up)
        hgrad[...] = jnp.zeros_like(hgrad)
        pgrad[...] = jnp.zeros_like(pgrad)
        first = q * (3 * count)

        def keep(b, grad):
            if resumed:
                grad = grad + so_far_ref[first + b]
            dw_ref[first + b] = grad.astype(dw_ref.dtype)

        def place(m, b):
            at = 2 * (first + m * count + b)
            return lay_ref[at], lay_ref[at + 1]

        for b in range(count):
            r, c = place(0, b)
            gate[c] += dot(xs[q, r], w_ref[first + b], NN)
            r, c = place(1, b)
            up[c] += dot(xs[q, r], w_ref[first + count + b], NN)
            r, c = place(2, b)
            hgrad[r] += dot(ss[q, c], w_ref[first + 2 * count + b], NT)
        for h in range(hidden):
            gate_pre = gate[h]
            up_pre = up[h]
            sig = jax.nn.sigmoid(gate_pre)
            activated = gate_pre * sig
            hid[h] = (activated * up_pre).astype(jnp.bfloat16)
            hidden_grad = hgrad[h]
            ggrad[h] = (hidden_grad * up_pre * sig * (1.0 + gate_pre * (1.0 - sig))).astype(
                jnp.bfloat16
            )
            ugrad[h] = (hidden_grad * activated).astype(jnp.bfloat16)
        prod[...] = jnp.zeros_like(prod)
        for b in range(count):
            r, c = place(0, b)
            pgrad[r] += dot(ggrad[c], w_ref[first + b], NT)
            keep(b, dot(xs[q, r], ggrad[c], TN))
            r, c = place(1, b)
            pgrad[r] += dot(ugrad[c], w_ref[first + count + b], NT)
            keep(count + b, dot(xs[q, r], ugrad[c], TN))
            r, c = place(2, b)
            prod[...] += dot(hid[r], w_ref[first + 2 * count + b], NN) * gs[q, c].astype(
                jnp.float32
            )
            keep(2 * count + b, dot(hid[r], ss[q, c], TN))
        for s in range(shards):
            there = slice(s * slots, (s + 1) * slots)
            for c in range(feat):
                wide[s, q, :, c * LANES : (c + 1) * LANES] = pgrad[c, there, :].astype(
                    jnp.bfloat16
                )
            score = jnp.sum(prod[there, :], axis=1, keepdims=True).astype(jnp.bfloat16)
            own_lane = (
                lax.broadcasted_iota(jnp.int32, (slots, table_lanes), 1) == expert_ref[q]
            )
            wide[s, q, :, width:] = jnp.where(own_lane, score.astype(jnp.float32), 0.0).astype(
                jnp.bfloat16
            )
        return carry

    lax.fori_loop(0, 2, one_expert, 0)
    for s in range(shards):
        total = dot(spread[s, 0], wide[s, 0], NN) + dot(spread[s, 1], wide[s, 1], NN)
        low, high = total[:, :half], total[:, half:]
        if added:
            low = low + low_so_far[s][...].astype(jnp.float32)
            high = high + high_so_far[s][...].astype(jnp.float32)
        low_refs[s][...] = low.astype(jnp.bfloat16)
        high_refs[s][...] = high.astype(jnp.bfloat16)


def run_experts(
    x_list, g_list, weights, places, layouts, experts, slots, so_far, parts_so_far, final
):
    shards = len(x_list)
    tok, table_width = x_list[0].shape
    width = g_list[0].shape[1]
    half = width // 2
    feat = width // LANES
    hidden = HID // LANES
    rows = shards * slots
    block_count = 2 * weights[0].shape[0]
    resumed = so_far is not None
    bf16, f32 = jnp.bfloat16, jnp.float32
    smem = pl.BlockSpec(memory_space=pltpu.SMEM)
    vmem = pl.BlockSpec(memory_space=pltpu.VMEM)
    grads = jax.ShapeDtypeStruct((block_count, LANES, LANES), bf16 if final else f32)
    added = len(parts_so_far) > 0
    operands = [*x_list, *g_list, *weights] + ([so_far] if resumed else [])
    operands += [low for low, _ in parts_so_far] + [high for _, high in parts_so_far]
    outs = pl.pallas_call(
        functools.partial(
            expert_kernel, shards, slots, half, len(weights), resumed, added
        ),
        in_specs=[smem] * 3 + [vmem] * len(operands),
        out_specs=[vmem] * (2 * shards + 1),
        out_shape=[jax.ShapeDtypeStruct((tok, half), bf16)] * shards
        + [jax.ShapeDtypeStruct((tok, table_width - half), bf16)] * shards
        + [grads],
        scratch_shapes=[
            pltpu.VMEM((block_count, LANES, LANES), bf16),
            pltpu.VMEM((2, feat, rows, LANES), bf16),
            pltpu.VMEM((2, feat, rows, LANES), bf16),
            pltpu.VMEM((2, feat, rows, LANES), bf16),
            pltpu.VMEM((hidden, rows, LANES), f32),
            pltpu.VMEM((hidden, rows, LANES), f32),
            pltpu.VMEM((hidden, rows, LANES), bf16),
            pltpu.VMEM((hidden, rows, LANES), f32),
            pltpu.VMEM((hidden, rows, LANES), bf16),
            pltpu.VMEM((hidden, rows, LANES), bf16),
            pltpu.VMEM((feat, rows, LANES), f32),
            pltpu.VMEM((shards, 2, slots, table_width), bf16),
            pltpu.VMEM((shards, 2, tok, slots), bf16),
            pltpu.VMEM((rows, LANES), f32),
        ],
        compiler_params=pltpu.CompilerParams(vmem_limit_bytes=40 * 1024 * 1024),
        cost_estimate=pl.CostEstimate(
            flops=2 * 2 * 108 * rows * LANES * LANES * 4,
            bytes_accessed=shards * tok * table_width * 6 + block_count * LANES * LANES * 6,
            transcendentals=0,
        ),
    )(layouts, experts, places, *operands)
    return outs[:shards], outs[shards : 2 * shards], outs[2 * shards]


def chip_ring(chips):
    broad = chips // 2
    return list(range(broad)) + list(range(chips - 1, broad - 1, -1))


def swap_all(pieces):
    return lax.all_to_all(pieces, "expert", split_axis=0, concat_axis=0, tiled=True)


def body(tokens, out_grad, expert_ids, route_weights, blocks, layout, moments, partner):
    expert_count = lax.axis_size("expert")
    replica_count = lax.axis_size("dp")
    tok_count, topk_count = expert_ids.shape
    width = tokens.shape[1]
    block_size = blocks.shape[-1]
    capacity = max(2, tok_count * topk_count * 7 // (expert_count * 6))
    slots = -(-capacity // 16) * 16
    table_lanes = -(-expert_count // LANES) * LANES
    bf16, f32 = jnp.bfloat16, jnp.float32
    chips = expert_count // 4
    ring = chip_ring(chips)
    steps = [
        (a + side * chips, b + side * chips)
        for a, b in zip(ring, ring[1:] + ring[:1])
        for side in range(2)
    ]
    onward = [(2 * a + core, 2 * b + core) for a, b in steps for core in range(2)]
    backward = [(b, a) for a, b in onward]
    sister = [(i, i ^ 1) for i in range(expert_count)]
    far = expert_count // 2
    mirror = [(i, i ^ far) for i in range(expert_count)]
    row_share = block_size // replica_count
    replica = lax.axis_index("dp")

    def step_on(value):
        return lax.ppermute(value, "expert", onward)

    def step_back(value):
        return lax.ppermute(value, "expert", backward)

    def own_rows(value):
        return lax.dynamic_slice_in_dim(value, replica * row_share, row_share, 2)

    def other_replica(value):
        return lax.ppermute(value, "dp", [(0, 1), (1, 0)])

    def other_core(value):
        return lax.ppermute(value, "expert", sister)

    def join_rows(rows):
        if replica_count != 2:
            return lax.all_gather(rows, "dp", axis=2, tiled=True)
        mine_here = (jnp.arange(2, dtype=jnp.int32) == replica)[None, None, :, None, None]
        both = jnp.where(mine_here, rows[:, :, None], other_replica(rows)[:, :, None])
        return both.reshape(rows.shape[:2] + (block_size,) + rows.shape[3:])

    def sum_rows(one, two):
        if replica_count != 2:
            return lax.psum_scatter(add(one, two), "dp", scatter_dimension=2, tiled=True).astype(f32)

        def half_of(index):
            return sum(
                lax.dynamic_slice_in_dim(value, index * row_share, row_share, 2).astype(f32)
                for value in (one, two)
            )

        theirs = other_replica(half_of(1 - replica).astype(bf16))
        return half_of(replica) + theirs.astype(f32)

    def add(left, right):
        return (left.astype(f32) + right.astype(f32)).astype(bf16)

    lane = jnp.arange(table_lanes, dtype=jnp.int32)
    named = expert_ids[:, :, None] == lane[None, None, :]
    table = jnp.sum(jnp.where(named, route_weights[:, :, None].astype(f32), 0.0), axis=1).astype(
        bf16
    )
    me = lax.axis_index("expert")

    note_rows = 16
    layout_flat = layout.reshape(-1)
    layout_note = jnp.zeros((note_rows * LANES,), bf16).at[: layout_flat.shape[0]].set(
        layout_flat.astype(bf16)
    )
    rows_now = own_rows(blocks[0])
    pieces = rows_now.reshape(expert_count, -1, LANES)
    piece_rows = pieces.shape[1]
    note = jnp.broadcast_to(
        layout_note.reshape(1, note_rows, LANES), (expert_count, note_rows, LANES)
    )
    spread = swap_all(jnp.concatenate([pieces, note], axis=1))
    all_layouts = spread[:, piece_rows:].reshape(expert_count, -1)[:, : layout_flat.shape[0]]
    all_slots = jnp.arange(expert_count, dtype=jnp.int32)

    def collect(spread_state, slot_order):
        moved = jnp.take(spread_state, jnp.take(partner, slot_order), axis=0)
        return swap_all(moved).reshape(rows_now.shape)

    rows_far = collect(spread[:, :piece_rows], all_slots ^ far)
    rows_far, spread = lax.optimization_barrier((rows_far, spread))
    rows_near = collect(spread[:, :piece_rows], all_slots)

    x_at = {0: jnp.concatenate([tokens, table], axis=1)}
    g_at = {0: out_grad}
    most = chips // 2
    for s in range(1, most + 1):
        x_at[-s] = step_on(x_at[1 - s])
        g_at[s] = step_back(g_at[s - 1])
        if s < most:
            x_at[s] = step_back(x_at[s - 1])
            g_at[-s] = step_on(g_at[1 - s])
    x_at[most] = x_at[-most]
    shards = [0]
    for s in range(1, most):
        shards += [s, -s]
    shards += [most]
    groups = [shards[i : i + 8] for i in range(0, len(shards), 8)]

    if replica_count == 2:
        places = jnp.stack([replica * row_share, (1 - replica) * row_share]).astype(jnp.int32)
    else:
        places = jnp.zeros((1,), jnp.int32)

    def both_cores(rows):
        halves = [rows, other_replica(rows)] if replica_count == 2 else [join_rows(rows)]
        weights = halves + [other_core(value) for value in halves]
        return [value.reshape(-1, value.shape[2], LANES) for value in weights]

    def run_pair(slot, weights, earlier):
        experts = jnp.take(partner, jnp.stack([slot, slot ^ 1])).astype(jnp.int32)
        layouts = jnp.take(all_layouts, experts, axis=0).reshape(-1).astype(jnp.int32)
        parts, sums = {}, None
        for group in groups:
            lows, highs, sums = run_experts(
                [x_at[d] for d in group],
                [g_at[d] for d in group],
                weights,
                places,
                layouts,
                experts,
                slots,
                sums,
                [earlier[d] for d in group] if earlier else [],
                group is groups[-1],
            )
            for d, low, high in zip(group, lows, highs):
                parts[d] = (low, high)
        half_count = sums.shape[0] // 2
        from_sister = other_core(sums[half_count:].reshape(blocks[0].shape))
        return parts, sums[:half_count].reshape(blocks[0].shape), from_sister

    moment_pieces = moments[0].astype(bf16).reshape(expert_count, -1, LANES)
    weights_far = both_cores(rows_far)
    weights_near = both_cores(rows_near)
    weights_far, moment_pieces, rows_near = lax.optimization_barrier(
        (weights_far, moment_pieces, rows_near)
    )
    moment_spread = swap_all(moment_pieces)
    parts, far_grad, far_sister = run_pair(me ^ far, weights_far, None)
    parts, far_grad, far_sister, weights_near, moment_spread = lax.optimization_barrier(
        (parts, far_grad, far_sister, weights_near, moment_spread)
    )
    moved_moments = collect(moment_spread, all_slots)
    far_sum = sum_rows(far_grad, far_sister).astype(bf16)
    from_mirror = lax.ppermute(far_sum, "expert", mirror)
    parts, near_grad, near_sister = run_pair(me, weights_near, parts)
    shard_grad = sum_rows(near_grad, near_sister) + from_mirror.astype(f32)
    new_moment = momentum_decay * moved_moments.astype(f32) + shard_grad
    new_shard = (rows_near.astype(f32) - step_rate * new_moment).astype(bf16)

    def own_share(distance, part):
        return parts[distance][part]

    upward = [step_on(own_share(most, 0)), None]
    downward = [None, step_back(own_share(most, 1))]
    for s in range(most - 1, 0, -1):
        for part in range(2):
            share = own_share(s, part)
            upward[part] = step_on(share if upward[part] is None else add(upward[part], share))
            share = own_share(-s, part)
            downward[part] = step_back(
                share if downward[part] is None else add(downward[part], share)
            )
    homes = [
        (parts[0][part].astype(f32) + upward[part].astype(f32) + downward[part].astype(f32)).astype(
            bf16
        )
        for part in range(2)
    ]
    half = homes[0].shape[1]
    token_grad = jnp.concatenate([homes[0], homes[1][:, : width - half]], axis=1)
    scores = homes[1][:, width - half :]
    route_grad = jnp.sum(jnp.where(named, scores[:, None, :].astype(f32), 0.0), axis=2).astype(bf16)
    return (token_grad, route_grad, join_rows(new_shard)[None], new_moment[None])


def solution(mesh):
    placed = (
        P(("dp", "expert"), None),
        P(("dp", "expert"), None),
        P(("dp", "expert"), None),
        P(("dp", "expert"), None),
        P("expert", None, None, None, None),
        P("expert", None, None, None),
        P("expert", None, None, "dp", None),
        P(),
    )
    return jax.shard_map(
        body,
        mesh=mesh,
        in_specs=placed,
        out_specs=(
            P(("dp", "expert"), None),
            P(("dp", "expert"), None),
            P("expert", None, None, None, None),
            P("expert", None, None, "dp", None),
        ),
        check_vma=False,
    )
```

```python
import functools

import jax
import jax.numpy as jnp
from jax import lax
from jax.experimental import pallas as pl
from jax.experimental.pallas import tpu as pltpu
from jax.sharding import PartitionSpec as P

HID = 1408
LANES = 128

momentum_decay = 0.9
step_rate = 0.01

NN = (((1,), (0,)), ((), ()))
NT = (((1,), (1,)), ((), ()))
TN = (((0,), (0,)), ((), ()))


def dot(left, right, dims):
    return lax.dot_general(left, right, dims, preferred_element_type=jnp.float32)


def expert_kernel(
    shards,
    slots,
    half,
    pieces,
    resumed,
    added,
    lay_ref,
    expert_ref,
    place_ref,
    *refs,
):
    x_refs, refs = refs[:shards], refs[shards:]
    g_refs, refs = refs[:shards], refs[shards:]
    piece_refs, refs = refs[:pieces], refs[pieces:]
    if resumed:
        so_far_ref, refs = refs[0], refs[1:]
    if added:
        low_so_far, refs = refs[:shards], refs[shards:]
        high_so_far, refs = refs[:shards], refs[shards:]
    low_refs, refs = refs[:shards], refs[shards:]
    high_refs, refs = refs[:shards], refs[shards:]
    (
        dw_ref,
        w_ref,
        xs,
        gs,
        ss,
        gate,
        up,
        hid,
        hgrad,
        ggrad,
        ugrad,
        pgrad,
        wide,
        spread,
        prod,
    ) = refs
    tok = LANES
    feat = xs.shape[1]
    hidden = gate.shape[0]
    width = feat * LANES
    count = w_ref.shape[0] // 6
    rows = shards * slots
    table_lanes = x_refs[0].shape[1] - width
    token_row = lax.broadcasted_iota(jnp.int32, (tok, tok), 0)
    token_col = lax.broadcasted_iota(jnp.int32, (tok, tok), 1)
    earlier_row = (token_row < token_col).astype(jnp.bfloat16)
    earlier_col = (token_col < token_row).astype(jnp.bfloat16)
    lane_tok = lax.broadcasted_iota(jnp.int32, (tok, table_lanes), 1)
    lane_few = lax.broadcasted_iota(jnp.int32, (8, table_lanes), 1)
    slot_rows = lax.broadcasted_iota(jnp.int32, (slots, tok), 0).astype(jnp.float32)
    slot_cols = lax.broadcasted_iota(jnp.int32, (tok, slots), 1).astype(jnp.float32)

    in_expert = pieces // 2
    for i, piece in enumerate(piece_refs):
        q, rows_in = i // in_expert, piece.shape[1]
        first = pl.multiple_of(place_ref[i % in_expert], 16)
        w_ref[q * 3 * count : (q + 1) * 3 * count, pl.ds(first, rows_in), :] = piece[...]

    for s in range(shards):
        there = slice(s * slots, (s + 1) * slots)
        table = x_refs[s][:, width:]
        gathers, weights = [], []
        for q in range(2):
            expert = expert_ref[q]
            weight_row = dot((lane_few == expert).astype(jnp.bfloat16), table, NT)[0:1]
            picked_row = weight_row > 0.0
            rank_row = dot(
                jnp.broadcast_to(picked_row, (8, tok)).astype(jnp.bfloat16), earlier_row, NN
            )[0:1]
            gather = jnp.where(jnp.logical_and(slot_rows == rank_row, picked_row), 1.0, 0.0)
            gathers.append(gather)
            weights.append(jnp.sum(gather * weight_row, axis=1, keepdims=True))
            picked_col = (
                jnp.max(
                    jnp.where(lane_tok == expert, table.astype(jnp.float32), 0.0),
                    axis=1,
                    keepdims=True,
                )
                > 0.0
            )
            rank_col = dot(
                earlier_col, jnp.broadcast_to(picked_col, (tok, tok)).astype(jnp.bfloat16), NN
            )[:, 0:1]
            spread[s, q] = jnp.where(
                jnp.logical_and(slot_cols == rank_col, picked_col), 1.0, 0.0
            ).astype(jnp.bfloat16)
        gather = jnp.concatenate(gathers, axis=0).astype(jnp.bfloat16)
        weight = jnp.concatenate(weights, axis=0)
        x_rows = dot(gather, x_refs[s][:, :width], NN).astype(jnp.bfloat16)
        g_rows = dot(gather, g_refs[s][...], NN)
        s_rows = (g_rows * weight).astype(jnp.bfloat16)
        g_rows = g_rows.astype(jnp.bfloat16)
        for q in range(2):
            own = slice(q * slots, (q + 1) * slots)
            for c in range(feat):
                cut = slice(c * LANES, (c + 1) * LANES)
                xs[q, c, there, :] = x_rows[own, cut]
                gs[q, c, there, :] = g_rows[own, cut]
                ss[q, c, there, :] = s_rows[own, cut]

    def one_expert(q, carry):
        gate[...] = jnp.zeros_like(gate)
        up[...] = jnp.zeros_like(up)
        hgrad[...] = jnp.zeros_like(hgrad)
        pgrad[...] = jnp.zeros_like(pgrad)
        first = q * (3 * count)

        def keep(b, grad):
            if resumed:
                grad = grad + so_far_ref[first + b]
            dw_ref[first + b] = grad.astype(dw_ref.dtype)

        def place(m, b):
            at = 2 * (first + m * count + b)
            return lay_ref[at], lay_ref[at + 1]

        for b in range(count):
            r, c = place(0, b)
            gate[c] += dot(xs[q, r], w_ref[first + b], NN)
            r, c = place(1, b)
            up[c] += dot(xs[q, r], w_ref[first + count + b], NN)
            r, c = place(2, b)
            hgrad[r] += dot(ss[q, c], w_ref[first + 2 * count + b], NT)
        for h in range(hidden):
            gate_pre = gate[h]
            up_pre = up[h]
            sig = jax.nn.sigmoid(gate_pre)
            activated = gate_pre * sig
            hid[h] = (activated * up_pre).astype(jnp.bfloat16)
            hidden_grad = hgrad[h]
            ggrad[h] = (hidden_grad * up_pre * sig * (1.0 + gate_pre * (1.0 - sig))).astype(
                jnp.bfloat16
            )
            ugrad[h] = (hidden_grad * activated).astype(jnp.bfloat16)
        prod[...] = jnp.zeros_like(prod)
        for b in range(count):
            r, c = place(0, b)
            pgrad[r] += dot(ggrad[c], w_ref[first + b], NT)
            keep(b, dot(xs[q, r], ggrad[c], TN))
            r, c = place(1, b)
            pgrad[r] += dot(ugrad[c], w_ref[first + count + b], NT)
            keep(count + b, dot(xs[q, r], ugrad[c], TN))
            r, c = place(2, b)
            prod[...] += dot(hid[r], w_ref[first + 2 * count + b], NN) * gs[q, c].astype(
                jnp.float32
            )
            keep(2 * count + b, dot(hid[r], ss[q, c], TN))
        for s in range(shards):
            there = slice(s * slots, (s + 1) * slots)
            for c in range(feat):
                wide[s, q, :, c * LANES : (c + 1) * LANES] = pgrad[c, there, :].astype(
                    jnp.bfloat16
                )
            score = jnp.sum(prod[there, :], axis=1, keepdims=True).astype(jnp.bfloat16)
            own_lane = (
                lax.broadcasted_iota(jnp.int32, (slots, table_lanes), 1) == expert_ref[q]
            )
            wide[s, q, :, width:] = jnp.where(own_lane, score.astype(jnp.float32), 0.0).astype(
                jnp.bfloat16
            )
        return carry

    lax.fori_loop(0, 2, one_expert, 0)
    for s in range(shards):
        total = dot(spread[s, 0], wide[s, 0], NN) + dot(spread[s, 1], wide[s, 1], NN)
        low, high = total[:, :half], total[:, half:]
        if added:
            low = low + low_so_far[s][...].astype(jnp.float32)
            high = high + high_so_far[s][...].astype(jnp.float32)
        low_refs[s][...] = low.astype(jnp.bfloat16)
        high_refs[s][...] = high.astype(jnp.bfloat16)


def run_experts(
    x_list, g_list, weights, places, layouts, experts, slots, so_far, parts_so_far, final
):
    shards = len(x_list)
    tok, table_width = x_list[0].shape
    width = g_list[0].shape[1]
    half = width // 2
    feat = width // LANES
    hidden = HID // LANES
    rows = shards * slots
    block_count = 2 * weights[0].shape[0]
    resumed = so_far is not None
    bf16, f32 = jnp.bfloat16, jnp.float32
    smem = pl.BlockSpec(memory_space=pltpu.SMEM)
    vmem = pl.BlockSpec(memory_space=pltpu.VMEM)
    grads = jax.ShapeDtypeStruct((block_count, LANES, LANES), bf16 if final else f32)
    added = len(parts_so_far) > 0
    operands = [*x_list, *g_list, *weights] + ([so_far] if resumed else [])
    operands += [low for low, _ in parts_so_far] + [high for _, high in parts_so_far]
    outs = pl.pallas_call(
        functools.partial(
            expert_kernel, shards, slots, half, len(weights), resumed, added
        ),
        in_specs=[smem] * 3 + [vmem] * len(operands),
        out_specs=[vmem] * (2 * shards + 1),
        out_shape=[jax.ShapeDtypeStruct((tok, half), bf16)] * shards
        + [jax.ShapeDtypeStruct((tok, table_width - half), bf16)] * shards
        + [grads],
        scratch_shapes=[
            pltpu.VMEM((block_count, LANES, LANES), bf16),
            pltpu.VMEM((2, feat, rows, LANES), bf16),
            pltpu.VMEM((2, feat, rows, LANES), bf16),
            pltpu.VMEM((2, feat, rows, LANES), bf16),
            pltpu.VMEM((hidden, rows, LANES), f32),
            pltpu.VMEM((hidden, rows, LANES), f32),
            pltpu.VMEM((hidden, rows, LANES), bf16),
            pltpu.VMEM((hidden, rows, LANES), f32),
            pltpu.VMEM((hidden, rows, LANES), bf16),
            pltpu.VMEM((hidden, rows, LANES), bf16),
            pltpu.VMEM((feat, rows, LANES), f32),
            pltpu.VMEM((shards, 2, slots, table_width), bf16),
            pltpu.VMEM((shards, 2, tok, slots), bf16),
            pltpu.VMEM((rows, LANES), f32),
        ],
        compiler_params=pltpu.CompilerParams(vmem_limit_bytes=40 * 1024 * 1024),
        cost_estimate=pl.CostEstimate(
            flops=2 * 2 * 108 * rows * LANES * LANES * 4,
            bytes_accessed=shards * tok * table_width * 6 + block_count * LANES * LANES * 6,
            transcendentals=0,
        ),
    )(layouts, experts, places, *operands)
    return outs[:shards], outs[shards : 2 * shards], outs[2 * shards]


def chip_ring(chips):
    broad = chips // 2
    return list(range(broad)) + list(range(chips - 1, broad - 1, -1))


def swap_all(pieces):
    return lax.all_to_all(pieces, "expert", split_axis=0, concat_axis=0, tiled=True)


def body(tokens, out_grad, expert_ids, route_weights, blocks, layout, moments, partner):
    expert_count = lax.axis_size("expert")
    replica_count = lax.axis_size("dp")
    tok_count, topk_count = expert_ids.shape
    width = tokens.shape[1]
    block_size = blocks.shape[-1]
    capacity = max(2, tok_count * topk_count * 7 // (expert_count * 6))
    slots = -(-capacity // 16) * 16
    table_lanes = -(-expert_count // LANES) * LANES
    bf16, f32 = jnp.bfloat16, jnp.float32
    chips = expert_count // 4
    ring = chip_ring(chips)
    steps = [
        (a + side * chips, b + side * chips)
        for a, b in zip(ring, ring[1:] + ring[:1])
        for side in range(2)
    ]
    onward = [(2 * a + core, 2 * b + core) for a, b in steps for core in range(2)]
    backward = [(b, a) for a, b in onward]
    sister = [(i, i ^ 1) for i in range(expert_count)]
    far = expert_count // 2
    mirror = [(i, i ^ far) for i in range(expert_count)]
    row_share = block_size // replica_count
    replica = lax.axis_index("dp")

    def step_on(value):
        return lax.ppermute(value, "expert", onward)

    def step_back(value):
        return lax.ppermute(value, "expert", backward)

    def own_rows(value):
        return lax.dynamic_slice_in_dim(value, replica * row_share, row_share, 2)

    def other_replica(value):
        return lax.ppermute(value, "dp", [(0, 1), (1, 0)])

    def other_core(value):
        return lax.ppermute(value, "expert", sister)

    def join_rows(rows):
        if replica_count != 2:
            return lax.all_gather(rows, "dp", axis=2, tiled=True)
        mine_here = (jnp.arange(2, dtype=jnp.int32) == replica)[None, None, :, None, None]
        both = jnp.where(mine_here, rows[:, :, None], other_replica(rows)[:, :, None])
        return both.reshape(rows.shape[:2] + (block_size,) + rows.shape[3:])

    def sum_rows(one, two):
        if replica_count != 2:
            return lax.psum_scatter(add(one, two), "dp", scatter_dimension=2, tiled=True).astype(f32)

        def half_of(index):
            return sum(
                lax.dynamic_slice_in_dim(value, index * row_share, row_share, 2).astype(f32)
                for value in (one, two)
            )

        theirs = other_replica(half_of(1 - replica).astype(bf16))
        return half_of(replica) + theirs.astype(f32)

    def add(left, right):
        return (left.astype(f32) + right.astype(f32)).astype(bf16)

    lane = jnp.arange(table_lanes, dtype=jnp.int32)
    named = expert_ids[:, :, None] == lane[None, None, :]
    table = jnp.sum(jnp.where(named, route_weights[:, :, None].astype(f32), 0.0), axis=1).astype(
        bf16
    )
    me = lax.axis_index("expert")

    note_rows = 16
    layout_flat = layout.reshape(-1)
    layout_note = jnp.zeros((note_rows * LANES,), bf16).at[: layout_flat.shape[0]].set(
        layout_flat.astype(bf16)
    )
    rows_now = own_rows(blocks[0])
    pieces = rows_now.reshape(expert_count, -1, LANES)
    piece_rows = pieces.shape[1]
    note = jnp.broadcast_to(
        layout_note.reshape(1, note_rows, LANES), (expert_count, note_rows, LANES)
    )
    spread = swap_all(jnp.concatenate([pieces, note], axis=1))
    all_slots = jnp.arange(expert_count, dtype=jnp.int32)

    def collect(spread_state, slot_order):
        order = partner.at[slot_order].get(mode="promise_in_bounds")
        moved = spread_state.at[order].get(mode="promise_in_bounds")
        return swap_all(moved).reshape(rows_now.shape)

    x_at = {0: jnp.concatenate([tokens, table], axis=1)}
    g_at = {0: out_grad}
    most = chips // 2
    for s in range(1, most + 1):
        x_at[-s] = step_on(x_at[1 - s])
        g_at[s] = step_back(g_at[s - 1])
        if s < most:
            x_at[s] = step_back(x_at[s - 1])
            g_at[-s] = step_on(g_at[1 - s])
        if s == 1:
            x_at, g_at, spread = lax.optimization_barrier((x_at, g_at, spread))
            rows_far = collect(spread[:, :piece_rows], all_slots ^ far)
    x_at[most] = x_at[-most]
    x_at, g_at, rows_far, spread = lax.optimization_barrier((x_at, g_at, rows_far, spread))
    rows_near = collect(spread[:, :piece_rows], all_slots)
    all_layouts = spread[:, piece_rows:].reshape(expert_count, -1)[:, : layout_flat.shape[0]]
    shards = [0]
    for s in range(1, most):
        shards += [s, -s]
    shards += [most]
    groups = [shards[i : i + 8] for i in range(0, len(shards), 8)]

    if replica_count == 2:
        places = jnp.stack([replica * row_share, (1 - replica) * row_share]).astype(jnp.int32)
    else:
        places = jnp.zeros((1,), jnp.int32)

    def both_cores(rows):
        halves = [rows, other_replica(rows)] if replica_count == 2 else [join_rows(rows)]
        weights = halves + [other_core(value) for value in halves]
        return [value.reshape(-1, value.shape[2], LANES) for value in weights]

    def run_pair(slot, weights, earlier):
        pair = jnp.stack([slot, slot ^ 1])
        experts = partner.at[pair].get(mode="promise_in_bounds").astype(jnp.int32)
        layouts = all_layouts.at[experts].get(mode="promise_in_bounds")
        layouts = layouts.reshape(-1).astype(jnp.int32)
        parts, sums = {}, None
        for group in groups:
            lows, highs, sums = run_experts(
                [x_at[d] for d in group],
                [g_at[d] for d in group],
                weights,
                places,
                layouts,
                experts,
                slots,
                sums,
                [earlier[d] for d in group] if earlier else [],
                group is groups[-1],
            )
            for d, low, high in zip(group, lows, highs):
                parts[d] = (low, high)
        half_count = sums.shape[0] // 2
        from_sister = other_core(sums[half_count:].reshape(blocks[0].shape))
        return parts, sums[:half_count].reshape(blocks[0].shape), from_sister

    moment_pieces = moments[0].astype(bf16).reshape(expert_count, -1, LANES)
    weights_far = both_cores(rows_far)
    weights_near = both_cores(rows_near)
    weights_far, moment_pieces, rows_near = lax.optimization_barrier(
        (weights_far, moment_pieces, rows_near)
    )
    moment_spread = swap_all(moment_pieces)
    parts, far_grad, far_sister = run_pair(me ^ far, weights_far, None)
    far_sum = sum_rows(far_grad, far_sister).astype(bf16)
    far_sum, weights_near, moment_spread = lax.optimization_barrier(
        (far_sum, weights_near, moment_spread)
    )
    from_mirror = lax.ppermute(far_sum, "expert", mirror)
    moved_moments = collect(moment_spread, all_slots)
    parts, near_grad, near_sister = run_pair(me, weights_near, parts)
    def own_share(distance, part):
        return parts[distance][part]

    upward = [step_on(own_share(most, 0)), None]
    downward = [None, step_back(own_share(most, 1))]
    upward[0], from_mirror = lax.optimization_barrier((upward[0], from_mirror))
    for s in range(most - 1, 0, -1):
        for part in range(2):
            share = own_share(s, part)
            upward[part] = step_on(share if upward[part] is None else add(upward[part], share))
            share = own_share(-s, part)
            downward[part] = step_back(
                share if downward[part] is None else add(downward[part], share)
            )
    shard_grad = sum_rows(near_grad, near_sister) + from_mirror.astype(f32)
    new_moment = momentum_decay * moved_moments.astype(f32) + shard_grad
    new_shard = (rows_near.astype(f32) - step_rate * new_moment).astype(bf16)

    homes = [
        (parts[0][part].astype(f32) + upward[part].astype(f32) + downward[part].astype(f32)).astype(
            bf16
        )
        for part in range(2)
    ]
    half = homes[0].shape[1]
    token_grad = jnp.concatenate([homes[0], homes[1][:, : width - half]], axis=1)
    scores = homes[1][:, width - half :]
    route_grad = jnp.sum(jnp.where(named, scores[:, None, :].astype(f32), 0.0), axis=2).astype(bf16)
    return (token_grad, route_grad, join_rows(new_shard)[None], new_moment[None])


def solution(mesh):
    placed = (
        P(("dp", "expert"), None),
        P(("dp", "expert"), None),
        P(("dp", "expert"), None),
        P(("dp", "expert"), None),
        P("expert", None, None, None, None),
        P("expert", None, None, None),
        P("expert", None, None, "dp", None),
        P(),
    )
    return jax.shard_map(
        body,
        mesh=mesh,
        in_specs=placed,
        out_specs=(
            P(("dp", "expert"), None),
            P(("dp", "expert"), None),
            P("expert", None, None, None, None),
            P("expert", None, None, "dp", None),
        ),
        check_vma=False,
    )
```

```python
import functools

import jax
import jax.numpy as jnp
from jax import lax
from jax.experimental import pallas as pl
from jax.experimental.pallas import tpu as pltpu
from jax.sharding import PartitionSpec as P

HID = 1408
LANES = 128

momentum_decay = 0.9
step_rate = 0.01

NN = (((1,), (0,)), ((), ()))
NT = (((1,), (1,)), ((), ()))
TN = (((0,), (0,)), ((), ()))


def dot(left, right, dims):
    return lax.dot_general(left, right, dims, preferred_element_type=jnp.float32)


def expert_kernel(
    shards,
    slots,
    half,
    pieces,
    resumed,
    added,
    lay_ref,
    expert_ref,
    place_ref,
    *refs,
):
    x_refs, refs = refs[:shards], refs[shards:]
    g_refs, refs = refs[:shards], refs[shards:]
    piece_refs, refs = refs[:pieces], refs[pieces:]
    if resumed:
        so_far_ref, refs = refs[0], refs[1:]
    if added:
        low_so_far, refs = refs[:shards], refs[shards:]
        high_so_far, refs = refs[:shards], refs[shards:]
    low_refs, refs = refs[:shards], refs[shards:]
    high_refs, refs = refs[:shards], refs[shards:]
    (
        dw_ref,
        w_ref,
        xs,
        gs,
        ss,
        gate,
        up,
        hid,
        hgrad,
        ggrad,
        ugrad,
        pgrad,
        wide,
        spread,
        prod,
    ) = refs
    tok = LANES
    feat = xs.shape[1]
    hidden = gate.shape[0]
    width = feat * LANES
    count = w_ref.shape[0] // 6
    rows = shards * slots
    table_lanes = x_refs[0].shape[1] - width
    token_row = lax.broadcasted_iota(jnp.int32, (tok, tok), 0)
    token_col = lax.broadcasted_iota(jnp.int32, (tok, tok), 1)
    earlier_row = (token_row < token_col).astype(jnp.bfloat16)
    earlier_col = (token_col < token_row).astype(jnp.bfloat16)
    lane_tok = lax.broadcasted_iota(jnp.int32, (tok, table_lanes), 1)
    lane_few = lax.broadcasted_iota(jnp.int32, (8, table_lanes), 1)
    slot_rows = lax.broadcasted_iota(jnp.int32, (slots, tok), 0).astype(jnp.float32)
    slot_cols = lax.broadcasted_iota(jnp.int32, (tok, slots), 1).astype(jnp.float32)

    in_expert = pieces // 2
    for i, piece in enumerate(piece_refs):
        q, rows_in = i // in_expert, piece.shape[1]
        first = pl.multiple_of(place_ref[i % in_expert], 16)
        w_ref[q * 3 * count : (q + 1) * 3 * count, pl.ds(first, rows_in), :] = piece[...]

    for s in range(shards):
        there = slice(s * slots, (s + 1) * slots)
        table = x_refs[s][:, width:]
        gathers, weights = [], []
        for q in range(2):
            expert = expert_ref[q]
            weight_row = dot((lane_few == expert).astype(jnp.bfloat16), table, NT)[0:1]
            picked_row = weight_row > 0.0
            rank_row = dot(
                jnp.broadcast_to(picked_row, (8, tok)).astype(jnp.bfloat16), earlier_row, NN
            )[0:1]
            gather = jnp.where(jnp.logical_and(slot_rows == rank_row, picked_row), 1.0, 0.0)
            gathers.append(gather)
            weights.append(jnp.sum(gather * weight_row, axis=1, keepdims=True))
            picked_col = (
                jnp.max(
                    jnp.where(lane_tok == expert, table.astype(jnp.float32), 0.0),
                    axis=1,
                    keepdims=True,
                )
                > 0.0
            )
            rank_col = dot(
                earlier_col, jnp.broadcast_to(picked_col, (tok, tok)).astype(jnp.bfloat16), NN
            )[:, 0:1]
            spread[s, q] = jnp.where(
                jnp.logical_and(slot_cols == rank_col, picked_col), 1.0, 0.0
            ).astype(jnp.bfloat16)
        gather = jnp.concatenate(gathers, axis=0).astype(jnp.bfloat16)
        weight = jnp.concatenate(weights, axis=0)
        x_rows = dot(gather, x_refs[s][:, :width], NN).astype(jnp.bfloat16)
        g_rows = dot(gather, g_refs[s][...], NN)
        s_rows = (g_rows * weight).astype(jnp.bfloat16)
        g_rows = g_rows.astype(jnp.bfloat16)
        for q in range(2):
            own = slice(q * slots, (q + 1) * slots)
            for c in range(feat):
                cut = slice(c * LANES, (c + 1) * LANES)
                xs[q, c, there, :] = x_rows[own, cut]
                gs[q, c, there, :] = g_rows[own, cut]
                ss[q, c, there, :] = s_rows[own, cut]

    def one_expert(q, carry):
        gate[...] = jnp.zeros_like(gate)
        up[...] = jnp.zeros_like(up)
        hgrad[...] = jnp.zeros_like(hgrad)
        pgrad[...] = jnp.zeros_like(pgrad)
        first = q * (3 * count)

        def keep(b, grad):
            if resumed:
                grad = grad + so_far_ref[first + b]
            dw_ref[first + b] = grad.astype(dw_ref.dtype)

        def place(m, b):
            at = 2 * (first + m * count + b)
            return lay_ref[at], lay_ref[at + 1]

        for b in range(count):
            r, c = place(0, b)
            gate[c] += dot(xs[q, r], w_ref[first + b], NN)
            r, c = place(1, b)
            up[c] += dot(xs[q, r], w_ref[first + count + b], NN)
            r, c = place(2, b)
            hgrad[r] += dot(ss[q, c], w_ref[first + 2 * count + b], NT)
        for h in range(hidden):
            gate_pre = gate[h]
            up_pre = up[h]
            sig = jax.nn.sigmoid(gate_pre)
            activated = gate_pre * sig
            hid[h] = (activated * up_pre).astype(jnp.bfloat16)
            hidden_grad = hgrad[h]
            ggrad[h] = (hidden_grad * up_pre * sig * (1.0 + gate_pre * (1.0 - sig))).astype(
                jnp.bfloat16
            )
            ugrad[h] = (hidden_grad * activated).astype(jnp.bfloat16)
        prod[...] = jnp.zeros_like(prod)
        for b in range(count):
            r, c = place(0, b)
            pgrad[r] += dot(ggrad[c], w_ref[first + b], NT)
            keep(b, dot(xs[q, r], ggrad[c], TN))
            r, c = place(1, b)
            pgrad[r] += dot(ugrad[c], w_ref[first + count + b], NT)
            keep(count + b, dot(xs[q, r], ugrad[c], TN))
            r, c = place(2, b)
            prod[...] += dot(hid[r], w_ref[first + 2 * count + b], NN) * gs[q, c].astype(
                jnp.float32
            )
            keep(2 * count + b, dot(hid[r], ss[q, c], TN))
        for s in range(shards):
            there = slice(s * slots, (s + 1) * slots)
            for c in range(feat):
                wide[s, q, :, c * LANES : (c + 1) * LANES] = pgrad[c, there, :].astype(
                    jnp.bfloat16
                )
            score = jnp.sum(prod[there, :], axis=1, keepdims=True).astype(jnp.bfloat16)
            own_lane = (
                lax.broadcasted_iota(jnp.int32, (slots, table_lanes), 1) == expert_ref[q]
            )
            wide[s, q, :, width:] = jnp.where(own_lane, score.astype(jnp.float32), 0.0).astype(
                jnp.bfloat16
            )
        return carry

    lax.fori_loop(0, 2, one_expert, 0)
    for s in range(shards):
        total = dot(spread[s, 0], wide[s, 0], NN) + dot(spread[s, 1], wide[s, 1], NN)
        low, high = total[:, :half], total[:, half:]
        if added:
            low = low + low_so_far[s][...].astype(jnp.float32)
            high = high + high_so_far[s][...].astype(jnp.float32)
        low_refs[s][...] = low.astype(jnp.bfloat16)
        high_refs[s][...] = high.astype(jnp.bfloat16)


def run_experts(
    x_list, g_list, weights, places, layouts, experts, slots, so_far, parts_so_far, final
):
    shards = len(x_list)
    tok, table_width = x_list[0].shape
    width = g_list[0].shape[1]
    half = width // 2
    feat = width // LANES
    hidden = HID // LANES
    rows = shards * slots
    block_count = 2 * weights[0].shape[0]
    resumed = so_far is not None
    bf16, f32 = jnp.bfloat16, jnp.float32
    smem = pl.BlockSpec(memory_space=pltpu.SMEM)
    vmem = pl.BlockSpec(memory_space=pltpu.VMEM)
    grads = jax.ShapeDtypeStruct((block_count, LANES, LANES), bf16 if final else f32)
    added = len(parts_so_far) > 0
    operands = [*x_list, *g_list, *weights] + ([so_far] if resumed else [])
    operands += [low for low, _ in parts_so_far] + [high for _, high in parts_so_far]
    outs = pl.pallas_call(
        functools.partial(
            expert_kernel, shards, slots, half, len(weights), resumed, added
        ),
        in_specs=[smem] * 3 + [vmem] * len(operands),
        out_specs=[vmem] * (2 * shards + 1),
        out_shape=[jax.ShapeDtypeStruct((tok, half), bf16)] * shards
        + [jax.ShapeDtypeStruct((tok, table_width - half), bf16)] * shards
        + [grads],
        scratch_shapes=[
            pltpu.VMEM((block_count, LANES, LANES), bf16),
            pltpu.VMEM((2, feat, rows, LANES), bf16),
            pltpu.VMEM((2, feat, rows, LANES), bf16),
            pltpu.VMEM((2, feat, rows, LANES), bf16),
            pltpu.VMEM((hidden, rows, LANES), f32),
            pltpu.VMEM((hidden, rows, LANES), f32),
            pltpu.VMEM((hidden, rows, LANES), bf16),
            pltpu.VMEM((hidden, rows, LANES), f32),
            pltpu.VMEM((hidden, rows, LANES), bf16),
            pltpu.VMEM((hidden, rows, LANES), bf16),
            pltpu.VMEM((feat, rows, LANES), f32),
            pltpu.VMEM((shards, 2, slots, table_width), bf16),
            pltpu.VMEM((shards, 2, tok, slots), bf16),
            pltpu.VMEM((rows, LANES), f32),
        ],
        compiler_params=pltpu.CompilerParams(vmem_limit_bytes=30 * 1024 * 1024),
        cost_estimate=pl.CostEstimate(
            flops=2 * 2 * 108 * rows * LANES * LANES * 8,
            bytes_accessed=shards * tok * table_width * 6 + block_count * LANES * LANES * 6,
            transcendentals=0,
        ),
    )(layouts, experts, places, *operands)
    return outs[:shards], outs[shards : 2 * shards], outs[2 * shards]


def chip_ring(chips):
    broad = chips // 2
    return list(range(broad)) + list(range(chips - 1, broad - 1, -1))


def swap_all(pieces):
    return lax.all_to_all(pieces, "expert", split_axis=0, concat_axis=0, tiled=True)


def body(tokens, out_grad, expert_ids, route_weights, blocks, layout, moments, partner):
    expert_count = lax.axis_size("expert")
    replica_count = lax.axis_size("dp")
    tok_count, topk_count = expert_ids.shape
    width = tokens.shape[1]
    block_size = blocks.shape[-1]
    capacity = max(2, tok_count * topk_count * 7 // (expert_count * 6))
    slots = -(-capacity // 16) * 16
    table_lanes = -(-expert_count // LANES) * LANES
    bf16, f32 = jnp.bfloat16, jnp.float32
    chips = expert_count // 4
    ring = chip_ring(chips)
    steps = [
        (a + side * chips, b + side * chips)
        for a, b in zip(ring, ring[1:] + ring[:1])
        for side in range(2)
    ]
    onward = [(2 * a + core, 2 * b + core) for a, b in steps for core in range(2)]
    backward = [(b, a) for a, b in onward]
    sister = [(i, i ^ 1) for i in range(expert_count)]
    far = expert_count // 2
    mirror = [(i, i ^ far) for i in range(expert_count)]
    row_share = block_size // replica_count
    replica = lax.axis_index("dp")

    def step_on(value):
        return lax.ppermute(value, "expert", onward)

    def step_back(value):
        return lax.ppermute(value, "expert", backward)

    def own_rows(value):
        return lax.dynamic_slice_in_dim(value, replica * row_share, row_share, 2)

    def other_replica(value):
        return lax.ppermute(value, "dp", [(0, 1), (1, 0)])

    def other_core(value):
        return lax.ppermute(value, "expert", sister)

    def join_rows(rows):
        if replica_count != 2:
            return lax.all_gather(rows, "dp", axis=2, tiled=True)
        mine_here = (jnp.arange(2, dtype=jnp.int32) == replica)[None, None, :, None, None]
        both = jnp.where(mine_here, rows[:, :, None], other_replica(rows)[:, :, None])
        return both.reshape(rows.shape[:2] + (block_size,) + rows.shape[3:])

    def sum_rows(one, two):
        if replica_count != 2:
            return lax.psum_scatter(add(one, two), "dp", scatter_dimension=2, tiled=True).astype(f32)

        def half_of(index):
            return sum(
                lax.dynamic_slice_in_dim(value, index * row_share, row_share, 2).astype(f32)
                for value in (one, two)
            )

        theirs = other_replica(half_of(1 - replica).astype(bf16))
        return half_of(replica) + theirs.astype(f32)

    def add(left, right):
        return (left.astype(f32) + right.astype(f32)).astype(bf16)

    lane = jnp.arange(table_lanes, dtype=jnp.int32)
    named = expert_ids[:, :, None] == lane[None, None, :]
    table = jnp.sum(jnp.where(named, route_weights[:, :, None].astype(f32), 0.0), axis=1).astype(
        bf16
    )
    me = lax.axis_index("expert")

    note_rows = 16
    layout_flat = layout.reshape(-1)
    layout_note = jnp.zeros((note_rows * LANES,), bf16).at[: layout_flat.shape[0]].set(
        layout_flat.astype(bf16)
    )
    rows_now = own_rows(blocks[0])
    pieces = rows_now.reshape(expert_count, -1, LANES)
    piece_rows = pieces.shape[1]
    note = jnp.broadcast_to(
        layout_note.reshape(1, note_rows, LANES), (expert_count, note_rows, LANES)
    )
    spread = swap_all(jnp.concatenate([pieces, note], axis=1))
    all_slots = jnp.arange(expert_count, dtype=jnp.int32)

    def collect(spread_state, slot_order):
        order = partner.at[slot_order].get(mode="promise_in_bounds")
        moved = spread_state.at[order, :piece_rows].get(mode="promise_in_bounds")
        return swap_all(moved).reshape(rows_now.shape)

    rows_far = collect(spread, all_slots ^ far)
    x_at = {0: jnp.concatenate([tokens, table], axis=1)}
    g_at = {0: out_grad}
    most = chips // 2
    for s in range(1, most + 1):
        x_at[-s] = step_on(x_at[1 - s])
        g_at[s] = step_back(g_at[s - 1])
        if s < most:
            x_at[s] = step_back(x_at[s - 1])
            g_at[-s] = step_on(g_at[1 - s])
        if s == 1:
            x_at, g_at, rows_far, spread = lax.optimization_barrier((x_at, g_at, rows_far, spread))
    x_at[most] = x_at[-most]
    rows_near = collect(spread, all_slots)
    all_layouts = spread[:, piece_rows:].reshape(expert_count, -1)[:, : layout_flat.shape[0]]
    shards = [0]
    for s in range(1, most):
        shards += [s, -s]
    shards += [most]
    groups = [shards[i : i + 8] for i in range(0, len(shards), 8)]

    if replica_count == 2:
        places = jnp.stack([replica * row_share, (1 - replica) * row_share]).astype(jnp.int32)
    else:
        places = jnp.zeros((1,), jnp.int32)

    def both_cores(rows):
        halves = [rows, other_replica(rows)] if replica_count == 2 else [join_rows(rows)]
        return halves

    def to_weights(halves):
        weights = halves + [other_core(value) for value in halves]
        return [value.reshape(-1, value.shape[2], LANES) for value in weights]

    def run_pair(slot, weights, earlier, beside):
        pair = jnp.stack([slot, slot ^ 1])
        experts = partner.at[pair].get(mode="promise_in_bounds").astype(jnp.int32)
        layouts = all_layouts.at[experts].get(mode="promise_in_bounds")
        layouts = layouts.reshape(-1).astype(jnp.int32)
        parts, sums = {}, None
        for group in groups:
            lows, highs, sums = run_experts(
                [x_at[d] for d in group],
                [g_at[d] for d in group],
                weights,
                places,
                layouts,
                experts,
                slots,
                sums,
                [earlier[d] for d in group] if earlier else [],
                group is groups[-1],
            )
            for d, low, high in zip(group, lows, highs):
                parts[d] = (low, high)
        sums, beside = lax.optimization_barrier((sums, beside))
        half_count = sums.shape[0] // 2
        from_sister = other_core(sums[half_count:].reshape(blocks[0].shape))
        return parts, sums[:half_count].reshape(blocks[0].shape), from_sister, beside

    moment_pieces = moments[0].astype(bf16).reshape(expert_count, -1, LANES)
    halves_far = both_cores(rows_far)
    halves_far, x_at, g_at = lax.optimization_barrier((halves_far, x_at, g_at))
    weights_far = to_weights(halves_far)
    weights_far, moment_pieces, rows_near = lax.optimization_barrier(
        (weights_far, moment_pieces, rows_near)
    )
    weights_near = to_weights(both_cores(rows_near))
    parts, far_grad, far_sister, moment_spread = run_pair(
        me ^ far, weights_far, None, swap_all(moment_pieces)
    )
    far_sum = sum_rows(far_grad, far_sister).astype(bf16)
    far_sum, weights_near = lax.optimization_barrier((far_sum, weights_near))
    from_mirror = lax.ppermute(far_sum, "expert", mirror)
    parts, near_grad, near_sister, moved_moments = run_pair(
        me, weights_near, parts, collect(moment_spread, all_slots)
    )
    def own_share(distance, part):
        return parts[distance][part]

    upward = [step_on(own_share(most, 0)), None]
    downward = [None, step_back(own_share(most, 1))]
    for s in range(most - 1, 0, -1):
        for part in range(2):
            share = own_share(s, part)
            upward[part] = step_on(share if upward[part] is None else add(upward[part], share))
            share = own_share(-s, part)
            downward[part] = step_back(
                share if downward[part] is None else add(downward[part], share)
            )
    shard_grad = sum_rows(near_grad, near_sister) + from_mirror.astype(f32)
    new_moment = momentum_decay * moved_moments.astype(f32) + shard_grad
    new_shard = (rows_near.astype(f32) - step_rate * new_moment).astype(bf16)

    homes = [
        (parts[0][part].astype(f32) + upward[part].astype(f32) + downward[part].astype(f32)).astype(
            bf16
        )
        for part in range(2)
    ]
    half = homes[0].shape[1]
    token_grad = jnp.concatenate([homes[0], homes[1][:, : width - half]], axis=1)
    scores = homes[1][:, width - half :]
    route_grad = jnp.sum(jnp.where(named, scores[:, None, :].astype(f32), 0.0), axis=2).astype(bf16)
    return (token_grad, route_grad, join_rows(new_shard)[None], new_moment[None])


def solution(mesh):
    placed = (
        P(("dp", "expert"), None),
        P(("dp", "expert"), None),
        P(("dp", "expert"), None),
        P(("dp", "expert"), None),
        P("expert", None, None, None, None),
        P("expert", None, None, None),
        P("expert", None, None, "dp", None),
        P(),
    )
    return jax.shard_map(
        body,
        mesh=mesh,
        in_specs=placed,
        out_specs=(
            P(("dp", "expert"), None),
            P(("dp", "expert"), None),
            P("expert", None, None, None, None),
            P("expert", None, None, "dp", None),
        ),
        check_vma=False,
    )
```

```python
import functools

import jax
import jax.numpy as jnp
from jax import lax
from jax.experimental import pallas as pl
from jax.experimental.pallas import tpu as pltpu
from jax.sharding import PartitionSpec as P

HID = 1408
LANES = 128

momentum_decay = 0.9
step_rate = 0.01

NN = (((1,), (0,)), ((), ()))
NT = (((1,), (1,)), ((), ()))
TN = (((0,), (0,)), ((), ()))


def dot(left, right, dims):
    return lax.dot_general(left, right, dims, preferred_element_type=jnp.float32)


def expert_kernel(
    shards,
    slots,
    half,
    pieces,
    resumed,
    added,
    lay_ref,
    expert_ref,
    place_ref,
    *refs,
):
    x_refs, refs = refs[:shards], refs[shards:]
    g_refs, refs = refs[:shards], refs[shards:]
    piece_refs, refs = refs[:pieces], refs[pieces:]
    if resumed:
        so_far_ref, refs = refs[0], refs[1:]
    if added:
        low_so_far, refs = refs[:shards], refs[shards:]
        high_so_far, refs = refs[:shards], refs[shards:]
    low_refs, refs = refs[:shards], refs[shards:]
    high_refs, refs = refs[:shards], refs[shards:]
    (
        dw_ref,
        w_ref,
        xs,
        gs,
        ss,
        gate,
        up,
        hid,
        hgrad,
        ggrad,
        ugrad,
        pgrad,
        wide,
        spread,
        prod,
    ) = refs
    tok = LANES
    feat = xs.shape[1]
    hidden = gate.shape[0]
    width = feat * LANES
    count = w_ref.shape[0] // 6
    rows = shards * slots
    table_lanes = x_refs[0].shape[1] - width
    token_row = lax.broadcasted_iota(jnp.int32, (tok, tok), 0)
    token_col = lax.broadcasted_iota(jnp.int32, (tok, tok), 1)
    earlier_row = (token_row < token_col).astype(jnp.bfloat16)
    earlier_col = (token_col < token_row).astype(jnp.bfloat16)
    lane_tok = lax.broadcasted_iota(jnp.int32, (tok, table_lanes), 1)
    lane_few = lax.broadcasted_iota(jnp.int32, (8, table_lanes), 1)
    slot_rows = lax.broadcasted_iota(jnp.int32, (slots, tok), 0).astype(jnp.float32)
    slot_cols = lax.broadcasted_iota(jnp.int32, (tok, slots), 1).astype(jnp.float32)

    in_expert = pieces // 2
    for i, piece in enumerate(piece_refs):
        q, rows_in = i // in_expert, piece.shape[1]
        first = pl.multiple_of(place_ref[i % in_expert], 16)
        w_ref[q * 3 * count : (q + 1) * 3 * count, pl.ds(first, rows_in), :] = piece[...]

    for s in range(shards):
        there = slice(s * slots, (s + 1) * slots)
        table = x_refs[s][:, width:]
        gathers, weights = [], []
        for q in range(2):
            expert = expert_ref[q]
            weight_row = dot((lane_few == expert).astype(jnp.bfloat16), table, NT)[0:1]
            picked_row = weight_row > 0.0
            rank_row = dot(
                jnp.broadcast_to(picked_row, (8, tok)).astype(jnp.bfloat16), earlier_row, NN
            )[0:1]
            gather = jnp.where(jnp.logical_and(slot_rows == rank_row, picked_row), 1.0, 0.0)
            gathers.append(gather)
            weights.append(jnp.sum(gather * weight_row, axis=1, keepdims=True))
            picked_col = (
                jnp.max(
                    jnp.where(lane_tok == expert, table.astype(jnp.float32), 0.0),
                    axis=1,
                    keepdims=True,
                )
                > 0.0
            )
            rank_col = dot(
                earlier_col, jnp.broadcast_to(picked_col, (tok, tok)).astype(jnp.bfloat16), NN
            )[:, 0:1]
            spread[s, q] = jnp.where(
                jnp.logical_and(slot_cols == rank_col, picked_col), 1.0, 0.0
            ).astype(jnp.bfloat16)
        gather = jnp.concatenate(gathers, axis=0).astype(jnp.bfloat16)
        weight = jnp.concatenate(weights, axis=0)
        x_rows = dot(gather, x_refs[s][:, :width], NN).astype(jnp.bfloat16)
        g_rows = dot(gather, g_refs[s][...], NN)
        s_rows = (g_rows * weight).astype(jnp.bfloat16)
        g_rows = g_rows.astype(jnp.bfloat16)
        for q in range(2):
            own = slice(q * slots, (q + 1) * slots)
            for c in range(feat):
                cut = slice(c * LANES, (c + 1) * LANES)
                xs[q, c, there, :] = x_rows[own, cut]
                gs[q, c, there, :] = g_rows[own, cut]
                ss[q, c, there, :] = s_rows[own, cut]

    def one_expert(q, carry):
        gate[...] = jnp.zeros_like(gate)
        up[...] = jnp.zeros_like(up)
        hgrad[...] = jnp.zeros_like(hgrad)
        pgrad[...] = jnp.zeros_like(pgrad)
        first = q * (3 * count)

        def keep(b, grad):
            if resumed:
                grad = grad + so_far_ref[first + b]
            dw_ref[first + b] = grad.astype(dw_ref.dtype)

        def place(m, b):
            at = 2 * (first + m * count + b)
            return lay_ref[at], lay_ref[at + 1]

        for b in range(count):
            r, c = place(0, b)
            gate[c] += dot(xs[q, r], w_ref[first + b], NN)
            r, c = place(1, b)
            up[c] += dot(xs[q, r], w_ref[first + count + b], NN)
            r, c = place(2, b)
            hgrad[r] += dot(ss[q, c], w_ref[first + 2 * count + b], NT)
        for h in range(hidden):
            gate_pre = gate[h]
            up_pre = up[h]
            sig = jax.nn.sigmoid(gate_pre)
            activated = gate_pre * sig
            hid[h] = (activated * up_pre).astype(jnp.bfloat16)
            hidden_grad = hgrad[h]
            ggrad[h] = (hidden_grad * up_pre * sig * (1.0 + gate_pre * (1.0 - sig))).astype(
                jnp.bfloat16
            )
            ugrad[h] = (hidden_grad * activated).astype(jnp.bfloat16)
        prod[...] = jnp.zeros_like(prod)
        for b in range(count):
            r, c = place(0, b)
            pgrad[r] += dot(ggrad[c], w_ref[first + b], NT)
            keep(b, dot(xs[q, r], ggrad[c], TN))
            r, c = place(1, b)
            pgrad[r] += dot(ugrad[c], w_ref[first + count + b], NT)
            keep(count + b, dot(xs[q, r], ugrad[c], TN))
            r, c = place(2, b)
            prod[...] += dot(hid[r], w_ref[first + 2 * count + b], NN) * gs[q, c].astype(
                jnp.float32
            )
            keep(2 * count + b, dot(hid[r], ss[q, c], TN))
        for s in range(shards):
            there = slice(s * slots, (s + 1) * slots)
            for c in range(feat):
                wide[s, q, :, c * LANES : (c + 1) * LANES] = pgrad[c, there, :].astype(
                    jnp.bfloat16
                )
            score = jnp.sum(prod[there, :], axis=1, keepdims=True).astype(jnp.bfloat16)
            own_lane = (
                lax.broadcasted_iota(jnp.int32, (slots, table_lanes), 1) == expert_ref[q]
            )
            wide[s, q, :, width:] = jnp.where(own_lane, score.astype(jnp.float32), 0.0).astype(
                jnp.bfloat16
            )
        return carry

    lax.fori_loop(0, 2, one_expert, 0)
    for s in range(shards):
        total = dot(spread[s, 0], wide[s, 0], NN) + dot(spread[s, 1], wide[s, 1], NN)
        low, high = total[:, :half], total[:, half:]
        if added:
            low = low + low_so_far[s][...].astype(jnp.float32)
            high = high + high_so_far[s][...].astype(jnp.float32)
        low_refs[s][...] = low.astype(jnp.bfloat16)
        high_refs[s][...] = high.astype(jnp.bfloat16)


def run_experts(
    x_list, g_list, weights, places, layouts, experts, slots, so_far, parts_so_far, final
):
    shards = len(x_list)
    tok, table_width = x_list[0].shape
    width = g_list[0].shape[1]
    half = width // 2
    feat = width // LANES
    hidden = HID // LANES
    rows = shards * slots
    block_count = 2 * weights[0].shape[0]
    resumed = so_far is not None
    bf16, f32 = jnp.bfloat16, jnp.float32
    smem = pl.BlockSpec(memory_space=pltpu.SMEM)
    grads = jax.ShapeDtypeStruct((block_count, LANES, LANES), bf16 if final else f32)
    out_shape = [jax.ShapeDtypeStruct((tok, half), bf16)] * shards
    out_shape += [jax.ShapeDtypeStruct((tok, table_width - half), bf16)] * shards
    out_shape += [grads]

    def whole(value):
        return pl.BlockSpec(value.shape, lambda i: (0,) * len(value.shape))

    added = len(parts_so_far) > 0
    operands = [*x_list, *g_list, *weights] + ([so_far] if resumed else [])
    operands += [low for low, _ in parts_so_far] + [high for _, high in parts_so_far]
    outs = pl.pallas_call(
        functools.partial(
            expert_kernel, shards, slots, half, len(weights), resumed, added
        ),
        grid=(1,),
        in_specs=[smem] * 3 + [whole(value) for value in operands],
        out_specs=[whole(value) for value in out_shape],
        out_shape=out_shape,
        scratch_shapes=[
            pltpu.VMEM((block_count, LANES, LANES), bf16),
            pltpu.VMEM((2, feat, rows, LANES), bf16),
            pltpu.VMEM((2, feat, rows, LANES), bf16),
            pltpu.VMEM((2, feat, rows, LANES), bf16),
            pltpu.VMEM((hidden, rows, LANES), f32),
            pltpu.VMEM((hidden, rows, LANES), f32),
            pltpu.VMEM((hidden, rows, LANES), bf16),
            pltpu.VMEM((hidden, rows, LANES), f32),
            pltpu.VMEM((hidden, rows, LANES), bf16),
            pltpu.VMEM((hidden, rows, LANES), bf16),
            pltpu.VMEM((feat, rows, LANES), f32),
            pltpu.VMEM((shards, 2, slots, table_width), bf16),
            pltpu.VMEM((shards, 2, tok, slots), bf16),
            pltpu.VMEM((rows, LANES), f32),
        ],
        compiler_params=pltpu.CompilerParams(vmem_limit_bytes=58 * 1024 * 1024),
        cost_estimate=pl.CostEstimate(
            flops=2 * 2 * 108 * rows * LANES * LANES * 8,
            bytes_accessed=shards * tok * table_width * 6 + block_count * LANES * LANES * 6,
            transcendentals=0,
        ),
    )(layouts, experts, places, *operands)
    return outs[:shards], outs[shards : 2 * shards], outs[2 * shards]


def chip_ring(chips):
    broad = chips // 2
    return list(range(broad)) + list(range(chips - 1, broad - 1, -1))


def swap_all(pieces):
    return lax.all_to_all(pieces, "expert", split_axis=0, concat_axis=0, tiled=True)


def body(tokens, out_grad, expert_ids, route_weights, blocks, layout, moments, partner):
    expert_count = lax.axis_size("expert")
    replica_count = lax.axis_size("dp")
    tok_count, topk_count = expert_ids.shape
    width = tokens.shape[1]
    block_size = blocks.shape[-1]
    capacity = max(2, tok_count * topk_count * 7 // (expert_count * 6))
    slots = -(-capacity // 16) * 16
    table_lanes = -(-expert_count // LANES) * LANES
    bf16, f32 = jnp.bfloat16, jnp.float32
    chips = expert_count // 4
    ring = chip_ring(chips)
    steps = [
        (a + side * chips, b + side * chips)
        for a, b in zip(ring, ring[1:] + ring[:1])
        for side in range(2)
    ]
    onward = [(2 * a + core, 2 * b + core) for a, b in steps for core in range(2)]
    backward = [(b, a) for a, b in onward]
    sister = [(i, i ^ 1) for i in range(expert_count)]
    far = expert_count // 2
    mirror = [(i, i ^ far) for i in range(expert_count)]
    row_share = block_size // replica_count
    replica = lax.axis_index("dp")

    def step_on(value):
        return lax.ppermute(value, "expert", onward)

    def step_back(value):
        return lax.ppermute(value, "expert", backward)

    def own_rows(value):
        return lax.dynamic_slice_in_dim(value, replica * row_share, row_share, 2)

    def other_replica(value):
        return lax.ppermute(value, "dp", [(0, 1), (1, 0)])

    def other_core(value):
        return lax.ppermute(value, "expert", sister)

    def join_rows(rows):
        if replica_count != 2:
            return lax.all_gather(rows, "dp", axis=2, tiled=True)
        mine_here = (jnp.arange(2, dtype=jnp.int32) == replica)[None, None, :, None, None]
        both = jnp.where(mine_here, rows[:, :, None], other_replica(rows)[:, :, None])
        return both.reshape(rows.shape[:2] + (block_size,) + rows.shape[3:])

    def sum_rows(one, two):
        if replica_count != 2:
            return lax.psum_scatter(add(one, two), "dp", scatter_dimension=2, tiled=True).astype(f32)

        def half_of(index):
            return sum(
                lax.dynamic_slice_in_dim(value, index * row_share, row_share, 2).astype(f32)
                for value in (one, two)
            )

        theirs = other_replica(half_of(1 - replica).astype(bf16))
        return half_of(replica) + theirs.astype(f32)

    def add(left, right):
        return (left.astype(f32) + right.astype(f32)).astype(bf16)

    lane = jnp.arange(table_lanes, dtype=jnp.int32)
    named = expert_ids[:, :, None] == lane[None, None, :]
    table = jnp.sum(jnp.where(named, route_weights[:, :, None].astype(f32), 0.0), axis=1).astype(
        bf16
    )
    me = lax.axis_index("expert")

    note_rows = 16
    layout_flat = layout.reshape(-1)
    layout_note = jnp.zeros((note_rows * LANES,), bf16).at[: layout_flat.shape[0]].set(
        layout_flat.astype(bf16)
    )
    rows_now = own_rows(blocks[0])
    pieces = rows_now.reshape(expert_count, -1, LANES)
    piece_rows = pieces.shape[1]
    note = jnp.broadcast_to(
        layout_note.reshape(1, note_rows, LANES), (expert_count, note_rows, LANES)
    )
    spread = swap_all(jnp.concatenate([pieces, note], axis=1))
    all_slots = jnp.arange(expert_count, dtype=jnp.int32)

    def ordered(spread_state, slot_order):
        order = partner.at[slot_order].get(mode="promise_in_bounds")
        return spread_state.at[order].get(mode="promise_in_bounds")

    x_at = {0: jnp.concatenate([tokens, table], axis=1)}
    g_at = {0: out_grad}
    most = chips // 2
    for s in range(1, most + 1):
        x_at[-s] = step_on(x_at[1 - s])
        g_at[s] = step_back(g_at[s - 1])
        if s < most:
            x_at[s] = step_back(x_at[s - 1])
            g_at[-s] = step_on(g_at[1 - s])
        if s == 1:
            x_at, g_at, spread = lax.optimization_barrier((x_at, g_at, spread))
            state_pieces = spread[:, :piece_rows]
            far_pieces = ordered(state_pieces, all_slots ^ far)
            near_pieces = ordered(state_pieces, all_slots)
            rows_far, near_pieces = lax.optimization_barrier((swap_all(far_pieces), near_pieces))
            rows_far = rows_far.reshape(rows_now.shape)
    x_at[most] = x_at[-most]
    rows_near = swap_all(near_pieces).reshape(rows_now.shape)
    all_layouts = spread[:, piece_rows:].reshape(expert_count, -1)[:, : layout_flat.shape[0]]
    shards = [0]
    for s in range(1, most):
        shards += [s, -s]
    shards += [most]
    groups = [shards[i : i + 8] for i in range(0, len(shards), 8)]

    if replica_count == 2:
        places = jnp.stack([replica * row_share, (1 - replica) * row_share]).astype(jnp.int32)
    else:
        places = jnp.zeros((1,), jnp.int32)

    def both_cores(rows):
        halves = [rows, other_replica(rows)] if replica_count == 2 else [join_rows(rows)]
        return halves

    def to_weights(halves):
        weights = halves + [other_core(value) for value in halves]
        return [value.reshape(-1, value.shape[2], LANES) for value in weights]

    def run_pair(slot, weights, earlier, beside):
        pair = jnp.stack([slot, slot ^ 1])
        experts = partner.at[pair].get(mode="promise_in_bounds").astype(jnp.int32)
        layouts = all_layouts.at[experts].get(mode="promise_in_bounds")
        layouts = layouts.reshape(-1).astype(jnp.int32)
        parts, sums = {}, None
        for group in groups:
            lows, highs, sums = run_experts(
                [x_at[d] for d in group],
                [g_at[d] for d in group],
                weights,
                places,
                layouts,
                experts,
                slots,
                sums,
                [earlier[d] for d in group] if earlier else [],
                group is groups[-1],
            )
            for d, low, high in zip(group, lows, highs):
                parts[d] = (low, high)
        sums, beside = lax.optimization_barrier((sums, beside))
        half_count = sums.shape[0] // 2
        from_sister = other_core(sums[half_count:].reshape(blocks[0].shape))
        return parts, sums[:half_count].reshape(blocks[0].shape), from_sister, beside

    moment_pieces = moments[0].astype(bf16).reshape(expert_count, -1, LANES)
    halves_far = both_cores(rows_far)
    halves_far, x_at, g_at = lax.optimization_barrier((halves_far, x_at, g_at))
    weights_far = to_weights(halves_far)
    weights_far, moment_pieces, rows_near = lax.optimization_barrier(
        (weights_far, moment_pieces, rows_near)
    )
    weights_near = to_weights(both_cores(rows_near))
    parts, far_grad, far_sister, moment_spread = run_pair(
        me ^ far, weights_far, None, swap_all(moment_pieces)
    )
    far_sum = sum_rows(far_grad, far_sister).astype(bf16)
    moved_moments = swap_all(ordered(moment_spread, all_slots)).reshape(rows_now.shape)
    far_sum, weights_near, moved_moments = lax.optimization_barrier(
        (far_sum, weights_near, moved_moments)
    )
    from_mirror = lax.ppermute(far_sum, "expert", mirror)
    parts, near_grad, near_sister, _ = run_pair(me, weights_near, parts, ())
    def own_share(distance, part):
        return parts[distance][part]

    upward = [step_on(own_share(most, 0)), None]
    downward = [None, step_back(own_share(most, 1))]
    for s in range(most - 1, 0, -1):
        for part in range(2):
            share = own_share(s, part)
            upward[part] = step_on(share if upward[part] is None else add(upward[part], share))
            share = own_share(-s, part)
            downward[part] = step_back(
                share if downward[part] is None else add(downward[part], share)
            )
    shard_grad = sum_rows(near_grad, near_sister) + from_mirror.astype(f32)
    new_moment = momentum_decay * moved_moments.astype(f32) + shard_grad
    new_shard = (rows_near.astype(f32) - step_rate * new_moment).astype(bf16)

    homes = [
        (parts[0][part].astype(f32) + upward[part].astype(f32) + downward[part].astype(f32)).astype(
            bf16
        )
        for part in range(2)
    ]
    half = homes[0].shape[1]
    token_grad = jnp.concatenate([homes[0], homes[1][:, : width - half]], axis=1)
    scores = homes[1][:, width - half :]
    route_grad = jnp.sum(jnp.where(named, scores[:, None, :].astype(f32), 0.0), axis=2).astype(bf16)
    return (token_grad, route_grad, join_rows(new_shard)[None], new_moment[None])


def solution(mesh):
    placed = (
        P(("dp", "expert"), None),
        P(("dp", "expert"), None),
        P(("dp", "expert"), None),
        P(("dp", "expert"), None),
        P("expert", None, None, None, None),
        P("expert", None, None, None),
        P("expert", None, None, "dp", None),
        P(),
    )
    return jax.shard_map(
        body,
        mesh=mesh,
        in_specs=placed,
        out_specs=(
            P(("dp", "expert"), None),
            P(("dp", "expert"), None),
            P("expert", None, None, None, None),
            P("expert", None, None, "dp", None),
        ),
        check_vma=False,
    )
```

```python
import functools

import jax
import jax.numpy as jnp
from jax import lax
from jax.experimental import pallas as pl
from jax.experimental.pallas import tpu as pltpu
from jax.sharding import PartitionSpec as P

HID = 1408
LANES = 128

momentum_decay = 0.9
step_rate = 0.01

NN = (((1,), (0,)), ((), ()))
NT = (((1,), (1,)), ((), ()))
TN = (((0,), (0,)), ((), ()))


def dot(left, right, dims):
    return lax.dot_general(left, right, dims, preferred_element_type=jnp.float32)


def expert_kernel(
    shards,
    slots,
    half,
    pieces,
    resumed,
    added,
    lay_ref,
    expert_ref,
    place_ref,
    *refs,
):
    x_refs, refs = refs[:shards], refs[shards:]
    g_refs, refs = refs[:shards], refs[shards:]
    piece_refs, refs = refs[:pieces], refs[pieces:]
    if resumed:
        so_far_refs, refs = refs[:2], refs[2:]
    if added:
        low_so_far, refs = refs[:shards], refs[shards:]
        high_so_far, refs = refs[:shards], refs[shards:]
    low_refs, refs = refs[:shards], refs[shards:]
    high_refs, refs = refs[:shards], refs[shards:]
    grad_refs, refs = refs[:2], refs[2:]
    (
        w_ref,
        xs,
        gs,
        ss,
        gate,
        up,
        hid,
        hgrad,
        ggrad,
        ugrad,
        pgrad,
        wide,
        spread,
        prod,
    ) = refs
    tok = LANES
    feat = xs.shape[1]
    hidden = gate.shape[0]
    width = feat * LANES
    count = w_ref.shape[0] // 6
    rows = shards * slots
    table_lanes = x_refs[0].shape[1] - width
    token_row = lax.broadcasted_iota(jnp.int32, (tok, tok), 0)
    token_col = lax.broadcasted_iota(jnp.int32, (tok, tok), 1)
    earlier_row = (token_row < token_col).astype(jnp.bfloat16)
    earlier_col = (token_col < token_row).astype(jnp.bfloat16)
    lane_tok = lax.broadcasted_iota(jnp.int32, (tok, table_lanes), 1)
    lane_few = lax.broadcasted_iota(jnp.int32, (8, table_lanes), 1)
    slot_rows = lax.broadcasted_iota(jnp.int32, (slots, tok), 0).astype(jnp.float32)
    slot_cols = lax.broadcasted_iota(jnp.int32, (tok, slots), 1).astype(jnp.float32)

    in_expert = pieces // 2
    for i, piece in enumerate(piece_refs):
        q, rows_in = i // in_expert, piece.shape[1]
        first = pl.multiple_of(place_ref[i % in_expert], 16)
        w_ref[q * 3 * count : (q + 1) * 3 * count, pl.ds(first, rows_in), :] = piece[...]

    for s in range(shards):
        there = slice(s * slots, (s + 1) * slots)
        table = x_refs[s][:, width:]
        gathers, weights = [], []
        for q in range(2):
            expert = expert_ref[q]
            weight_row = dot((lane_few == expert).astype(jnp.bfloat16), table, NT)[0:1]
            picked_row = weight_row > 0.0
            rank_row = dot(
                jnp.broadcast_to(picked_row, (8, tok)).astype(jnp.bfloat16), earlier_row, NN
            )[0:1]
            gather = jnp.where(jnp.logical_and(slot_rows == rank_row, picked_row), 1.0, 0.0)
            gathers.append(gather)
            weights.append(jnp.sum(gather * weight_row, axis=1, keepdims=True))
            picked_col = (
                jnp.max(
                    jnp.where(lane_tok == expert, table.astype(jnp.float32), 0.0),
                    axis=1,
                    keepdims=True,
                )
                > 0.0
            )
            rank_col = dot(
                earlier_col, jnp.broadcast_to(picked_col, (tok, tok)).astype(jnp.bfloat16), NN
            )[:, 0:1]
            spread[s, q] = jnp.where(
                jnp.logical_and(slot_cols == rank_col, picked_col), 1.0, 0.0
            ).astype(jnp.bfloat16)
        gather = jnp.concatenate(gathers, axis=0).astype(jnp.bfloat16)
        weight = jnp.concatenate(weights, axis=0)
        x_rows = dot(gather, x_refs[s][:, :width], NN).astype(jnp.bfloat16)
        g_rows = dot(gather, g_refs[s][...], NN)
        s_rows = (g_rows * weight).astype(jnp.bfloat16)
        g_rows = g_rows.astype(jnp.bfloat16)
        for q in range(2):
            own = slice(q * slots, (q + 1) * slots)
            for c in range(feat):
                cut = slice(c * LANES, (c + 1) * LANES)
                xs[q, c, there, :] = x_rows[own, cut]
                gs[q, c, there, :] = g_rows[own, cut]
                ss[q, c, there, :] = s_rows[own, cut]

    def one_expert(q):
        gate[...] = jnp.zeros_like(gate)
        up[...] = jnp.zeros_like(up)
        hgrad[...] = jnp.zeros_like(hgrad)
        pgrad[...] = jnp.zeros_like(pgrad)
        first = q * (3 * count)

        def keep(b, grad):
            if resumed:
                grad = grad + so_far_refs[q][b]
            grad_refs[q][b] = grad.astype(grad_refs[q].dtype)

        def place(m, b):
            at = 2 * (first + m * count + b)
            return lay_ref[at], lay_ref[at + 1]

        for b in range(count):
            r, c = place(0, b)
            gate[c] += dot(xs[q, r], w_ref[first + b], NN)
            r, c = place(1, b)
            up[c] += dot(xs[q, r], w_ref[first + count + b], NN)
            r, c = place(2, b)
            hgrad[r] += dot(ss[q, c], w_ref[first + 2 * count + b], NT)
        for h in range(hidden):
            gate_pre = gate[h]
            up_pre = up[h]
            sig = jax.nn.sigmoid(gate_pre)
            activated = gate_pre * sig
            hid[h] = (activated * up_pre).astype(jnp.bfloat16)
            hidden_grad = hgrad[h]
            ggrad[h] = (hidden_grad * up_pre * sig * (1.0 + gate_pre * (1.0 - sig))).astype(
                jnp.bfloat16
            )
            ugrad[h] = (hidden_grad * activated).astype(jnp.bfloat16)
        prod[...] = jnp.zeros_like(prod)
        for b in range(count):
            r, c = place(0, b)
            pgrad[r] += dot(ggrad[c], w_ref[first + b], NT)
            keep(b, dot(xs[q, r], ggrad[c], TN))
            r, c = place(1, b)
            pgrad[r] += dot(ugrad[c], w_ref[first + count + b], NT)
            keep(count + b, dot(xs[q, r], ugrad[c], TN))
            r, c = place(2, b)
            prod[...] += dot(hid[r], w_ref[first + 2 * count + b], NN) * gs[q, c].astype(
                jnp.float32
            )
            keep(2 * count + b, dot(hid[r], ss[q, c], TN))
        for s in range(shards):
            there = slice(s * slots, (s + 1) * slots)
            for c in range(feat):
                wide[s, q, :, c * LANES : (c + 1) * LANES] = pgrad[c, there, :].astype(
                    jnp.bfloat16
                )
            score = jnp.sum(prod[there, :], axis=1, keepdims=True).astype(jnp.bfloat16)
            own_lane = (
                lax.broadcasted_iota(jnp.int32, (slots, table_lanes), 1) == expert_ref[q]
            )
            wide[s, q, :, width:] = jnp.where(own_lane, score.astype(jnp.float32), 0.0).astype(
                jnp.bfloat16
            )

    for q in range(2):
        one_expert(q)
    for s in range(shards):
        total = dot(spread[s, 0], wide[s, 0], NN) + dot(spread[s, 1], wide[s, 1], NN)
        low, high = total[:, :half], total[:, half:]
        if added:
            low = low + low_so_far[s][...].astype(jnp.float32)
            high = high + high_so_far[s][...].astype(jnp.float32)
        low_refs[s][...] = low.astype(jnp.bfloat16)
        high_refs[s][...] = high.astype(jnp.bfloat16)


def run_experts(
    x_list, g_list, weights, places, layouts, experts, slots, so_far, parts_so_far, final
):
    shards = len(x_list)
    tok, table_width = x_list[0].shape
    width = g_list[0].shape[1]
    half = width // 2
    feat = width // LANES
    hidden = HID // LANES
    rows = shards * slots
    block_count = 2 * weights[0].shape[0]
    resumed = so_far is not None
    bf16, f32 = jnp.bfloat16, jnp.float32
    smem = pl.BlockSpec(memory_space=pltpu.SMEM)
    grads = jax.ShapeDtypeStruct((block_count // 2, LANES, LANES), bf16 if final else f32)
    out_shape = [jax.ShapeDtypeStruct((tok, half), bf16)] * shards
    out_shape += [jax.ShapeDtypeStruct((tok, table_width - half), bf16)] * shards
    out_shape += [grads, grads]

    def whole(value):
        return pl.BlockSpec(value.shape, lambda i: (0,) * len(value.shape))

    added = len(parts_so_far) > 0
    operands = [*x_list, *g_list, *weights] + (list(so_far) if resumed else [])
    operands += [low for low, _ in parts_so_far] + [high for _, high in parts_so_far]
    outs = pl.pallas_call(
        functools.partial(
            expert_kernel, shards, slots, half, len(weights), resumed, added
        ),
        grid=(1,),
        in_specs=[smem] * 3 + [whole(value) for value in operands],
        out_specs=[whole(value) for value in out_shape],
        out_shape=out_shape,
        scratch_shapes=[
            pltpu.VMEM((block_count, LANES, LANES), bf16),
            pltpu.VMEM((2, feat, rows, LANES), bf16),
            pltpu.VMEM((2, feat, rows, LANES), bf16),
            pltpu.VMEM((2, feat, rows, LANES), bf16),
            pltpu.VMEM((hidden, rows, LANES), f32),
            pltpu.VMEM((hidden, rows, LANES), f32),
            pltpu.VMEM((hidden, rows, LANES), bf16),
            pltpu.VMEM((hidden, rows, LANES), f32),
            pltpu.VMEM((hidden, rows, LANES), bf16),
            pltpu.VMEM((hidden, rows, LANES), bf16),
            pltpu.VMEM((feat, rows, LANES), f32),
            pltpu.VMEM((shards, 2, slots, table_width), bf16),
            pltpu.VMEM((shards, 2, tok, slots), bf16),
            pltpu.VMEM((rows, LANES), f32),
        ],
        compiler_params=pltpu.CompilerParams(vmem_limit_bytes=58 * 1024 * 1024),
        cost_estimate=pl.CostEstimate(
            flops=2 * 2 * 108 * rows * LANES * LANES * 8,
            bytes_accessed=shards * tok * table_width * 6 + block_count * LANES * LANES * 6,
            transcendentals=0,
        ),
    )(layouts, experts, places, *operands)
    return outs[:shards], outs[shards : 2 * shards], outs[2 * shards :]


def chip_ring(chips):
    broad = chips // 2
    return list(range(broad)) + list(range(chips - 1, broad - 1, -1))


def swap_all(pieces):
    return lax.all_to_all(pieces, "expert", split_axis=0, concat_axis=0, tiled=True)


def body(tokens, out_grad, expert_ids, route_weights, blocks, layout, moments, partner):
    expert_count = lax.axis_size("expert")
    replica_count = lax.axis_size("dp")
    tok_count, topk_count = expert_ids.shape
    width = tokens.shape[1]
    block_size = blocks.shape[-1]
    capacity = max(2, tok_count * topk_count * 7 // (expert_count * 6))
    slots = -(-capacity // 16) * 16
    table_lanes = -(-expert_count // LANES) * LANES
    bf16, f32 = jnp.bfloat16, jnp.float32
    chips = expert_count // 4
    ring = chip_ring(chips)
    steps = [
        (a + side * chips, b + side * chips)
        for a, b in zip(ring, ring[1:] + ring[:1])
        for side in range(2)
    ]
    onward = [(2 * a + core, 2 * b + core) for a, b in steps for core in range(2)]
    backward = [(b, a) for a, b in onward]
    sister = [(i, i ^ 1) for i in range(expert_count)]
    far = expert_count // 2
    mirror = [(i, i ^ far) for i in range(expert_count)]
    row_share = block_size // replica_count
    replica = lax.axis_index("dp")

    def step_on(value):
        return lax.ppermute(value, "expert", onward)

    def step_back(value):
        return lax.ppermute(value, "expert", backward)

    def own_rows(value):
        return lax.dynamic_slice_in_dim(value, replica * row_share, row_share, 2)

    def other_replica(value):
        return lax.ppermute(value, "dp", [(0, 1), (1, 0)])

    def other_core(value):
        return lax.ppermute(value, "expert", sister)

    def join_rows(rows):
        if replica_count != 2:
            return lax.all_gather(rows, "dp", axis=2, tiled=True)
        mine_here = (jnp.arange(2, dtype=jnp.int32) == replica)[None, None, :, None, None]
        both = jnp.where(mine_here, rows[:, :, None], other_replica(rows)[:, :, None])
        return both.reshape(rows.shape[:2] + (block_size,) + rows.shape[3:])

    def sum_rows(one, two):
        if replica_count != 2:
            whole = lax.psum_scatter(add(one, two), "dp", scatter_dimension=2, tiled=True)
            return whole.astype(f32), None

        def half_of(index):
            return sum(
                lax.dynamic_slice_in_dim(value, index * row_share, row_share, 2).astype(f32)
                for value in (one, two)
            )

        return half_of(replica), other_replica(half_of(1 - replica).astype(bf16))

    def rows_total(mine, theirs):
        return mine if theirs is None else mine + theirs.astype(f32)

    def add(left, right):
        return (left.astype(f32) + right.astype(f32)).astype(bf16)

    lane = jnp.arange(table_lanes, dtype=jnp.int32)
    named = expert_ids[:, :, None] == lane[None, None, :]
    table = jnp.sum(jnp.where(named, route_weights[:, :, None].astype(f32), 0.0), axis=1).astype(
        bf16
    )
    me = lax.axis_index("expert")

    note_rows = 16
    layout_flat = layout.reshape(-1)
    layout_note = jnp.zeros((note_rows * LANES,), bf16).at[: layout_flat.shape[0]].set(
        layout_flat.astype(bf16)
    )
    rows_now = own_rows(blocks[0])
    pieces = rows_now.reshape(expert_count, -1, LANES)
    piece_rows = pieces.shape[1]
    note = jnp.broadcast_to(
        layout_note.reshape(1, note_rows, LANES), (expert_count, note_rows, LANES)
    )
    spread = swap_all(jnp.concatenate([pieces, note], axis=1))
    all_slots = jnp.arange(expert_count, dtype=jnp.int32)

    def ordered(spread_state, slot_order):
        order = partner.at[slot_order].get(mode="promise_in_bounds")
        return spread_state.at[order].get(mode="promise_in_bounds")

    x_at = {0: jnp.concatenate([tokens, table], axis=1)}
    g_at = {0: out_grad}
    most = chips // 2
    for s in range(1, most + 1):
        x_at[-s] = step_on(x_at[1 - s])
        g_at[s] = step_back(g_at[s - 1])
        if s < most:
            x_at[s] = step_back(x_at[s - 1])
            g_at[-s] = step_on(g_at[1 - s])
        if s == 1:
            x_at, g_at, spread = lax.optimization_barrier((x_at, g_at, spread))
            state_pieces = spread[:, :piece_rows]
            far_pieces = ordered(state_pieces, all_slots ^ far)
            near_pieces = ordered(state_pieces, all_slots)
            rows_far, near_pieces = lax.optimization_barrier((swap_all(far_pieces), near_pieces))
            rows_far = rows_far.reshape(rows_now.shape)
    x_at[most] = x_at[-most]
    rows_near = swap_all(near_pieces).reshape(rows_now.shape)
    all_layouts = spread[:, piece_rows:].reshape(expert_count, -1)[:, : layout_flat.shape[0]]
    shards = [0]
    for s in range(1, most):
        shards += [s, -s]
    shards += [most]
    groups = [shards[i : i + 8] for i in range(0, len(shards), 8)]

    if replica_count == 2:
        places = jnp.stack([replica * row_share, (1 - replica) * row_share]).astype(jnp.int32)
    else:
        places = jnp.zeros((1,), jnp.int32)

    def both_cores(rows):
        halves = [rows, other_replica(rows)] if replica_count == 2 else [join_rows(rows)]
        return halves

    def to_weights(halves):
        weights = halves + [other_core(value) for value in halves]
        return [value.reshape(-1, value.shape[2], LANES) for value in weights]

    def run_pair(slot, weights, earlier, beside):
        pair = jnp.stack([slot, slot ^ 1])
        experts = partner.at[pair].get(mode="promise_in_bounds").astype(jnp.int32)
        layouts = all_layouts.at[experts].get(mode="promise_in_bounds")
        layouts = layouts.reshape(-1).astype(jnp.int32)
        parts, sums = {}, None
        for group in groups:
            lows, highs, sums = run_experts(
                [x_at[d] for d in group],
                [g_at[d] for d in group],
                weights,
                places,
                layouts,
                experts,
                slots,
                sums,
                [earlier[d] for d in group] if earlier else [],
                group is groups[-1],
            )
            for d, low, high in zip(group, lows, highs):
                parts[d] = (low, high)
        sums, beside = lax.optimization_barrier((sums, beside))
        own_grad, other_grad = (value.reshape(blocks[0].shape) for value in sums)
        return parts, own_grad, other_core(other_grad), beside

    moment_pieces = moments[0].astype(bf16).reshape(expert_count, -1, LANES)
    halves_far = both_cores(rows_far)
    halves_far, x_at, g_at = lax.optimization_barrier((halves_far, x_at, g_at))
    weights_far = to_weights(halves_far)
    weights_far, moment_pieces, rows_near = lax.optimization_barrier(
        (weights_far, moment_pieces, rows_near)
    )
    parts, far_grad, far_sister, (moment_spread, halves_near) = run_pair(
        me ^ far, weights_far, None, (swap_all(moment_pieces), both_cores(rows_near))
    )
    weights_near = to_weights(halves_near)
    moved_moments = swap_all(ordered(moment_spread, all_slots)).reshape(rows_now.shape)
    far_mine, far_theirs = sum_rows(far_grad, far_sister)
    parts, near_grad, near_sister, (far_theirs, moved_moments) = run_pair(
        me, weights_near, parts, (far_theirs, moved_moments)
    )
    far_sum = rows_total(far_mine, far_theirs).astype(bf16)
    from_mirror = lax.ppermute(far_sum, "expert", mirror)
    near_mine, near_theirs = sum_rows(near_grad, near_sister)

    def own_share(distance, part):
        return parts[distance][part]

    upward = [step_on(own_share(most, 0)), None]
    downward = [None, step_back(own_share(most, 1))]
    upward, downward, from_mirror, near_theirs = lax.optimization_barrier(
        (upward, downward, from_mirror, near_theirs)
    )
    for s in range(most - 1, 0, -1):
        for part in range(2):
            share = own_share(s, part)
            upward[part] = step_on(share if upward[part] is None else add(upward[part], share))
            share = own_share(-s, part)
            downward[part] = step_back(
                share if downward[part] is None else add(downward[part], share)
            )
    shard_grad = rows_total(near_mine, near_theirs) + from_mirror.astype(f32)
    new_moment = momentum_decay * moved_moments.astype(f32) + shard_grad
    new_shard = (rows_near.astype(f32) - step_rate * new_moment).astype(bf16)

    homes = [
        (parts[0][part].astype(f32) + upward[part].astype(f32) + downward[part].astype(f32)).astype(
            bf16
        )
        for part in range(2)
    ]
    half = homes[0].shape[1]
    token_grad = jnp.concatenate([homes[0], homes[1][:, : width - half]], axis=1)
    scores = homes[1][:, width - half :]
    route_grad = jnp.sum(jnp.where(named, scores[:, None, :].astype(f32), 0.0), axis=2).astype(bf16)
    return (token_grad, route_grad, join_rows(new_shard)[None], new_moment[None])


def solution(mesh):
    placed = (
        P(("dp", "expert"), None),
        P(("dp", "expert"), None),
        P(("dp", "expert"), None),
        P(("dp", "expert"), None),
        P("expert", None, None, None, None),
        P("expert", None, None, None),
        P("expert", None, None, "dp", None),
        P(),
    )
    return jax.shard_map(
        body,
        mesh=mesh,
        in_specs=placed,
        out_specs=(
            P(("dp", "expert"), None),
            P(("dp", "expert"), None),
            P("expert", None, None, None, None),
            P("expert", None, None, "dp", None),
        ),
        check_vma=False,
    )
```

```python
import functools

import jax
import jax.numpy as jnp
from jax import lax
from jax.experimental import pallas as pl
from jax.experimental.pallas import tpu as pltpu
from jax.sharding import PartitionSpec as P

HID = 1408
LANES = 128

momentum_decay = 0.9
step_rate = 0.01

NN = (((1,), (0,)), ((), ()))
NT = (((1,), (1,)), ((), ()))
TN = (((0,), (0,)), ((), ()))


def dot(left, right, dims):
    return lax.dot_general(left, right, dims, preferred_element_type=jnp.float32)


def expert_kernel(
    shards,
    slots,
    half,
    pieces,
    resumed,
    added,
    lay_ref,
    expert_ref,
    place_ref,
    *refs,
):
    x_refs, refs = refs[:shards], refs[shards:]
    g_refs, refs = refs[:shards], refs[shards:]
    piece_refs, refs = refs[:pieces], refs[pieces:]
    if resumed:
        so_far_refs, refs = refs[:2], refs[2:]
    if added:
        low_so_far, refs = refs[:shards], refs[shards:]
        high_so_far, refs = refs[:shards], refs[shards:]
    low_refs, refs = refs[:shards], refs[shards:]
    high_refs, refs = refs[:shards], refs[shards:]
    grad_refs, refs = refs[:2], refs[2:]
    (
        w_ref,
        xs,
        gs,
        ss,
        gate,
        up,
        hid,
        hgrad,
        ggrad,
        ugrad,
        pgrad,
        wide,
        spread,
        prod,
    ) = refs
    tok = LANES
    feat = xs.shape[1]
    hidden = gate.shape[0]
    width = feat * LANES
    count = w_ref.shape[0] // 6
    rows = shards * slots
    table_lanes = x_refs[0].shape[1] - width
    token_row = lax.broadcasted_iota(jnp.int32, (tok, tok), 0)
    token_col = lax.broadcasted_iota(jnp.int32, (tok, tok), 1)
    earlier_row = (token_row < token_col).astype(jnp.bfloat16)
    earlier_col = (token_col < token_row).astype(jnp.bfloat16)
    lane_tok = lax.broadcasted_iota(jnp.int32, (tok, table_lanes), 1)
    lane_few = lax.broadcasted_iota(jnp.int32, (8, table_lanes), 1)
    slot_rows = lax.broadcasted_iota(jnp.int32, (slots, tok), 0).astype(jnp.float32)
    slot_cols = lax.broadcasted_iota(jnp.int32, (tok, slots), 1).astype(jnp.float32)

    in_expert = pieces // 2
    for i, piece in enumerate(piece_refs):
        q, rows_in = i // in_expert, piece.shape[1]
        first = pl.multiple_of(place_ref[i % in_expert], 16)
        w_ref[q * 3 * count : (q + 1) * 3 * count, pl.ds(first, rows_in), :] = piece[...]

    for s in range(shards):
        there = slice(s * slots, (s + 1) * slots)
        table = x_refs[s][:, width:]
        gathers, weights = [], []
        for q in range(2):
            expert = expert_ref[q]
            weight_row = dot((lane_few == expert).astype(jnp.bfloat16), table, NT)[0:1]
            picked_row = weight_row > 0.0
            rank_row = dot(
                jnp.broadcast_to(picked_row, (8, tok)).astype(jnp.bfloat16), earlier_row, NN
            )[0:1]
            gather = jnp.where(jnp.logical_and(slot_rows == rank_row, picked_row), 1.0, 0.0)
            gathers.append(gather)
            weights.append(jnp.sum(gather * weight_row, axis=1, keepdims=True))
            picked_col = (
                jnp.max(
                    jnp.where(lane_tok == expert, table.astype(jnp.float32), 0.0),
                    axis=1,
                    keepdims=True,
                )
                > 0.0
            )
            rank_col = dot(
                earlier_col, jnp.broadcast_to(picked_col, (tok, tok)).astype(jnp.bfloat16), NN
            )[:, 0:1]
            spread[s, q] = jnp.where(
                jnp.logical_and(slot_cols == rank_col, picked_col), 1.0, 0.0
            ).astype(jnp.bfloat16)
        gather = jnp.concatenate(gathers, axis=0).astype(jnp.bfloat16)
        weight = jnp.concatenate(weights, axis=0)
        x_rows = dot(gather, x_refs[s][:, :width], NN).astype(jnp.bfloat16)
        g_rows = dot(gather, g_refs[s][...], NN)
        s_rows = (g_rows * weight).astype(jnp.bfloat16)
        g_rows = g_rows.astype(jnp.bfloat16)
        for q in range(2):
            own = slice(q * slots, (q + 1) * slots)
            for c in range(feat):
                cut = slice(c * LANES, (c + 1) * LANES)
                xs[q, c, there, :] = x_rows[own, cut]
                gs[q, c, there, :] = g_rows[own, cut]
                ss[q, c, there, :] = s_rows[own, cut]

    def one_expert(q):
        gate[...] = jnp.zeros_like(gate)
        up[...] = jnp.zeros_like(up)
        hgrad[...] = jnp.zeros_like(hgrad)
        pgrad[...] = jnp.zeros_like(pgrad)
        first = q * (3 * count)

        def keep(b, grad):
            if resumed:
                grad = grad + so_far_refs[q][b]
            grad_refs[q][b] = grad.astype(grad_refs[q].dtype)

        def place(m, b):
            at = 2 * (first + m * count + b)
            return lay_ref[at], lay_ref[at + 1]

        for b in range(count):
            r, c = place(0, b)
            gate[c] += dot(xs[q, r], w_ref[first + b], NN)
            r, c = place(1, b)
            up[c] += dot(xs[q, r], w_ref[first + count + b], NN)
            r, c = place(2, b)
            hgrad[r] += dot(ss[q, c], w_ref[first + 2 * count + b], NT)
        for h in range(hidden):
            gate_pre = gate[h]
            up_pre = up[h]
            sig = jax.nn.sigmoid(gate_pre)
            activated = gate_pre * sig
            hid[h] = (activated * up_pre).astype(jnp.bfloat16)
            hidden_grad = hgrad[h]
            ggrad[h] = (hidden_grad * up_pre * sig * (1.0 + gate_pre * (1.0 - sig))).astype(
                jnp.bfloat16
            )
            ugrad[h] = (hidden_grad * activated).astype(jnp.bfloat16)
        prod[...] = jnp.zeros_like(prod)
        for b in range(count):
            r, c = place(0, b)
            pgrad[r] += dot(ggrad[c], w_ref[first + b], NT)
            keep(b, dot(xs[q, r], ggrad[c], TN))
            r, c = place(1, b)
            pgrad[r] += dot(ugrad[c], w_ref[first + count + b], NT)
            keep(count + b, dot(xs[q, r], ugrad[c], TN))
            r, c = place(2, b)
            prod[...] += dot(hid[r], w_ref[first + 2 * count + b], NN) * gs[q, c].astype(
                jnp.float32
            )
            keep(2 * count + b, dot(hid[r], ss[q, c], TN))
        for s in range(shards):
            there = slice(s * slots, (s + 1) * slots)
            for c in range(feat):
                wide[s, q, :, c * LANES : (c + 1) * LANES] = pgrad[c, there, :].astype(
                    jnp.bfloat16
                )
            score = jnp.sum(prod[there, :], axis=1, keepdims=True).astype(jnp.bfloat16)
            own_lane = (
                lax.broadcasted_iota(jnp.int32, (slots, table_lanes), 1) == expert_ref[q]
            )
            wide[s, q, :, width:] = jnp.where(own_lane, score.astype(jnp.float32), 0.0).astype(
                jnp.bfloat16
            )

    for q in range(2):
        one_expert(q)
    for s in range(shards):
        total = dot(spread[s, 0], wide[s, 0], NN) + dot(spread[s, 1], wide[s, 1], NN)
        low, high = total[:, :half], total[:, half:]
        if added:
            low = low + low_so_far[s][...].astype(jnp.float32)
            high = high + high_so_far[s][...].astype(jnp.float32)
        low_refs[s][...] = low.astype(jnp.bfloat16)
        high_refs[s][...] = high.astype(jnp.bfloat16)


def run_experts(
    x_list, g_list, weights, places, layouts, experts, slots, so_far, parts_so_far, final
):
    shards = len(x_list)
    tok, table_width = x_list[0].shape
    width = g_list[0].shape[1]
    half = width // 2
    feat = width // LANES
    hidden = HID // LANES
    rows = shards * slots
    block_count = 2 * weights[0].shape[0]
    resumed = so_far is not None
    bf16, f32 = jnp.bfloat16, jnp.float32
    smem = pl.BlockSpec(memory_space=pltpu.SMEM)
    grads = jax.ShapeDtypeStruct((block_count // 2, LANES, LANES), bf16 if final else f32)
    out_shape = [jax.ShapeDtypeStruct((tok, half), bf16)] * shards
    out_shape += [jax.ShapeDtypeStruct((tok, table_width - half), bf16)] * shards
    out_shape += [grads, grads]

    def whole(value):
        return pl.BlockSpec(value.shape, lambda i: (0,) * len(value.shape))

    added = len(parts_so_far) > 0
    operands = [*x_list, *g_list, *weights] + (list(so_far) if resumed else [])
    operands += [low for low, _ in parts_so_far] + [high for _, high in parts_so_far]
    outs = pl.pallas_call(
        functools.partial(
            expert_kernel, shards, slots, half, len(weights), resumed, added
        ),
        grid=(1,),
        in_specs=[smem] * 3 + [whole(value) for value in operands],
        out_specs=[whole(value) for value in out_shape],
        out_shape=out_shape,
        scratch_shapes=[
            pltpu.VMEM((block_count, LANES, LANES), bf16),
            pltpu.VMEM((2, feat, rows, LANES), bf16),
            pltpu.VMEM((2, feat, rows, LANES), bf16),
            pltpu.VMEM((2, feat, rows, LANES), bf16),
            pltpu.VMEM((hidden, rows, LANES), f32),
            pltpu.VMEM((hidden, rows, LANES), f32),
            pltpu.VMEM((hidden, rows, LANES), bf16),
            pltpu.VMEM((hidden, rows, LANES), f32),
            pltpu.VMEM((hidden, rows, LANES), bf16),
            pltpu.VMEM((hidden, rows, LANES), bf16),
            pltpu.VMEM((feat, rows, LANES), f32),
            pltpu.VMEM((shards, 2, slots, table_width), bf16),
            pltpu.VMEM((shards, 2, tok, slots), bf16),
            pltpu.VMEM((rows, LANES), f32),
        ],
        compiler_params=pltpu.CompilerParams(vmem_limit_bytes=58 * 1024 * 1024),
        cost_estimate=pl.CostEstimate(
            flops=2 * 2 * 108 * rows * LANES * LANES * 8,
            bytes_accessed=shards * tok * table_width * 6 + block_count * LANES * LANES * 6,
            transcendentals=0,
        ),
    )(layouts, experts, places, *operands)
    return outs[:shards], outs[shards : 2 * shards], outs[2 * shards :]


def chip_ring(chips):
    broad = chips // 2
    return list(range(broad)) + list(range(chips - 1, broad - 1, -1))


def swap_all(pieces):
    return lax.all_to_all(pieces, "expert", split_axis=0, concat_axis=0, tiled=True)


def body(tokens, out_grad, expert_ids, route_weights, blocks, layout, moments, partner):
    expert_count = lax.axis_size("expert")
    replica_count = lax.axis_size("dp")
    tok_count, topk_count = expert_ids.shape
    width = tokens.shape[1]
    block_size = blocks.shape[-1]
    capacity = max(2, tok_count * topk_count * 7 // (expert_count * 6))
    slots = -(-capacity // 16) * 16
    table_lanes = -(-expert_count // LANES) * LANES
    bf16, f32 = jnp.bfloat16, jnp.float32
    chips = expert_count // 4
    ring = chip_ring(chips)
    steps = [
        (a + side * chips, b + side * chips)
        for a, b in zip(ring, ring[1:] + ring[:1])
        for side in range(2)
    ]
    onward = [(2 * a + core, 2 * b + core) for a, b in steps for core in range(2)]
    backward = [(b, a) for a, b in onward]
    sister = [(i, i ^ 1) for i in range(expert_count)]
    far = expert_count // 2
    mirror = [(i, i ^ far) for i in range(expert_count)]
    row_share = block_size // replica_count
    replica = lax.axis_index("dp")

    def step_on(value):
        return lax.ppermute(value, "expert", onward)

    def step_back(value):
        return lax.ppermute(value, "expert", backward)

    def own_rows(value):
        return lax.dynamic_slice_in_dim(value, replica * row_share, row_share, 2)

    def other_replica(value):
        return lax.ppermute(value, "dp", [(0, 1), (1, 0)])

    def other_core(value):
        return lax.ppermute(value, "expert", sister)

    def join_rows(rows):
        if replica_count != 2:
            return lax.all_gather(rows, "dp", axis=2, tiled=True)
        mine_here = (jnp.arange(2, dtype=jnp.int32) == replica)[None, None, :, None, None]
        both = jnp.where(mine_here, rows[:, :, None], other_replica(rows)[:, :, None])
        return both.reshape(rows.shape[:2] + (block_size,) + rows.shape[3:])

    def sum_rows(one, two):
        if replica_count != 2:
            whole = lax.psum_scatter(add(one, two), "dp", scatter_dimension=2, tiled=True)
            return whole.astype(f32), None

        def half_of(index):
            return sum(
                lax.dynamic_slice_in_dim(value, index * row_share, row_share, 2).astype(f32)
                for value in (one, two)
            )

        return half_of(replica), other_replica(half_of(1 - replica).astype(bf16))

    def rows_total(mine, theirs):
        return mine if theirs is None else mine + theirs.astype(f32)

    def add(left, right):
        return (left.astype(f32) + right.astype(f32)).astype(bf16)

    lane = jnp.arange(table_lanes, dtype=jnp.int32)
    named = expert_ids[:, :, None] == lane[None, None, :]
    table = jnp.sum(jnp.where(named, route_weights[:, :, None].astype(f32), 0.0), axis=1).astype(
        bf16
    )
    me = lax.axis_index("expert")

    note_rows = 16
    layout_flat = layout.reshape(-1)
    layout_note = jnp.zeros((note_rows * LANES,), bf16).at[: layout_flat.shape[0]].set(
        layout_flat.astype(bf16)
    )
    rows_now = own_rows(blocks[0])
    pieces = rows_now.reshape(expert_count, -1, LANES)
    piece_rows = pieces.shape[1]
    note = jnp.broadcast_to(
        layout_note.reshape(1, note_rows, LANES), (expert_count, note_rows, LANES)
    )
    spread = swap_all(jnp.concatenate([pieces, note], axis=1))
    all_slots = jnp.arange(expert_count, dtype=jnp.int32)

    def ordered(spread_state, slot_order):
        order = partner.at[slot_order].get(mode="promise_in_bounds")
        return spread_state.at[order].get(mode="promise_in_bounds")

    x_at = {0: jnp.concatenate([tokens, table], axis=1)}
    g_at = {0: out_grad}
    most = chips // 2
    moment_pieces = moments[0].astype(bf16).reshape(expert_count, -1, LANES)
    for s in range(1, most + 1):
        x_at[-s] = step_on(x_at[1 - s])
        g_at[s] = step_back(g_at[s - 1])
        if s < most:
            x_at[s] = step_back(x_at[s - 1])
            g_at[-s] = step_on(g_at[1 - s])
        if s == 1:
            x_at, g_at, spread, moment_pieces = lax.optimization_barrier(
                (x_at, g_at, spread, moment_pieces)
            )
            state_pieces = spread[:, :piece_rows]
            far_pieces = ordered(state_pieces, all_slots ^ far)
            near_pieces = ordered(state_pieces, all_slots)
            rows_far, near_pieces = lax.optimization_barrier((swap_all(far_pieces), near_pieces))
            rows_far = rows_far.reshape(rows_now.shape)
    x_at[most] = x_at[-most]
    rows_near = swap_all(near_pieces).reshape(rows_now.shape)
    all_layouts = spread[:, piece_rows:].reshape(expert_count, -1)[:, : layout_flat.shape[0]]
    shards = [0]
    for s in range(1, most):
        shards += [s, -s]
    shards += [most]
    groups = [shards[i : i + 8] for i in range(0, len(shards), 8)]

    if replica_count == 2:
        places = jnp.stack([replica * row_share, (1 - replica) * row_share]).astype(jnp.int32)
    else:
        places = jnp.zeros((1,), jnp.int32)

    def both_cores(rows):
        halves = [rows, other_replica(rows)] if replica_count == 2 else [join_rows(rows)]
        return halves

    def to_weights(halves):
        weights = halves + [other_core(value) for value in halves]
        return [value.reshape(-1, value.shape[2], LANES) for value in weights]

    def pair_of(slot):
        pair = jnp.stack([slot, slot ^ 1])
        experts = partner.at[pair].get(mode="promise_in_bounds").astype(jnp.int32)
        layouts = all_layouts.at[experts].get(mode="promise_in_bounds")
        return experts, layouts.reshape(-1).astype(jnp.int32)

    def run_pair(pair, weights, earlier, beside):
        experts, layouts = pair
        parts, sums = {}, None
        for group in groups:
            lows, highs, sums = run_experts(
                [x_at[d] for d in group],
                [g_at[d] for d in group],
                weights,
                places,
                layouts,
                experts,
                slots,
                sums,
                [earlier[d] for d in group] if earlier else [],
                group is groups[-1],
            )
            for d, low, high in zip(group, lows, highs):
                parts[d] = (low, high)
        sums, beside = lax.optimization_barrier((sums, beside))
        own_grad, other_grad = (value.reshape(blocks[0].shape) for value in sums)
        return parts, own_grad, other_core(other_grad), beside

    halves_far = both_cores(rows_far)
    far_pair, near_pair = pair_of(me ^ far), pair_of(me)
    halves_far, x_at, g_at, far_pair, near_pair, places = lax.optimization_barrier(
        (halves_far, x_at, g_at, far_pair, near_pair, places)
    )
    weights_far = to_weights(halves_far)
    weights_far, moment_pieces, rows_near = lax.optimization_barrier(
        (weights_far, moment_pieces, rows_near)
    )
    parts, far_grad, far_sister, (moment_spread, halves_near) = run_pair(
        far_pair, weights_far, None, (swap_all(moment_pieces), both_cores(rows_near))
    )
    weights_near = to_weights(halves_near)
    moved_moments = swap_all(ordered(moment_spread, all_slots)).reshape(rows_now.shape)
    far_mine, far_theirs = sum_rows(far_grad, far_sister)
    parts, near_grad, near_sister, (far_theirs, moved_moments) = run_pair(
        near_pair, weights_near, parts, (far_theirs, moved_moments)
    )
    far_sum = rows_total(far_mine, far_theirs).astype(bf16)
    from_mirror = lax.ppermute(far_sum, "expert", mirror)
    near_mine, near_theirs = sum_rows(near_grad, near_sister)

    def own_share(distance, part):
        return parts[distance][part]

    upward = [step_on(own_share(most, 0)), None]
    downward = [None, step_back(own_share(most, 1))]
    shard_grad = rows_total(near_mine, near_theirs) + from_mirror.astype(f32)
    new_moment = momentum_decay * moved_moments.astype(f32) + shard_grad
    new_shard = (rows_near.astype(f32) - step_rate * new_moment).astype(bf16)

    upward, downward, new_shard = lax.optimization_barrier((upward, downward, new_shard))
    for s in range(most - 1, 0, -1):
        for part in range(2):
            share = own_share(s, part)
            upward[part] = step_on(share if upward[part] is None else add(upward[part], share))
            share = own_share(-s, part)
            downward[part] = step_back(
                share if downward[part] is None else add(downward[part], share)
            )
    homes = [
        (parts[0][part].astype(f32) + upward[part].astype(f32) + downward[part].astype(f32)).astype(
            bf16
        )
        for part in range(2)
    ]
    half = homes[0].shape[1]
    token_grad = jnp.concatenate([homes[0], homes[1][:, : width - half]], axis=1)
    scores = homes[1][:, width - half :]
    route_grad = jnp.sum(jnp.where(named, scores[:, None, :].astype(f32), 0.0), axis=2).astype(bf16)
    return (token_grad, route_grad, join_rows(new_shard)[None], new_moment[None])


def solution(mesh):
    placed = (
        P(("dp", "expert"), None),
        P(("dp", "expert"), None),
        P(("dp", "expert"), None),
        P(("dp", "expert"), None),
        P("expert", None, None, None, None),
        P("expert", None, None, None),
        P("expert", None, None, "dp", None),
        P(),
    )
    return jax.shard_map(
        body,
        mesh=mesh,
        in_specs=placed,
        out_specs=(
            P(("dp", "expert"), None),
            P(("dp", "expert"), None),
            P("expert", None, None, None, None),
            P("expert", None, None, "dp", None),
        ),
        check_vma=False,
    )
```

```python
import functools

import jax
import jax.numpy as jnp
from jax import lax
from jax.experimental import pallas as pl
from jax.experimental.pallas import tpu as pltpu
from jax.sharding import PartitionSpec as P

HID = 1408
LANES = 128

momentum_decay = 0.9
step_rate = 0.01

NN = (((1,), (0,)), ((), ()))
NT = (((1,), (1,)), ((), ()))
TN = (((0,), (0,)), ((), ()))


def dot(left, right, dims):
    return lax.dot_general(left, right, dims, preferred_element_type=jnp.float32)


def expert_kernel(
    shards,
    slots,
    half,
    pieces,
    resumed,
    added,
    lay_ref,
    expert_ref,
    place_ref,
    *refs,
):
    x_refs, refs = refs[:shards], refs[shards:]
    g_refs, refs = refs[:shards], refs[shards:]
    piece_refs, refs = refs[:pieces], refs[pieces:]
    if resumed:
        so_far_refs, refs = refs[:2], refs[2:]
    if added:
        low_so_far, refs = refs[:shards], refs[shards:]
        high_so_far, refs = refs[:shards], refs[shards:]
    low_refs, refs = refs[:shards], refs[shards:]
    high_refs, refs = refs[:shards], refs[shards:]
    grad_refs, refs = refs[:2], refs[2:]
    (
        w_ref,
        xs,
        gs,
        ss,
        gate,
        up,
        hid,
        hgrad,
        ggrad,
        ugrad,
        pgrad,
        wide,
        spread,
        prod,
    ) = refs
    tok = LANES
    feat = xs.shape[1]
    hidden = gate.shape[0]
    width = feat * LANES
    count = w_ref.shape[0] // 6
    rows = shards * slots
    table_lanes = x_refs[0].shape[1] - width
    token_row = lax.broadcasted_iota(jnp.int32, (tok, tok), 0)
    token_col = lax.broadcasted_iota(jnp.int32, (tok, tok), 1)
    earlier_row = (token_row < token_col).astype(jnp.bfloat16)
    earlier_col = (token_col < token_row).astype(jnp.bfloat16)
    lane_tok = lax.broadcasted_iota(jnp.int32, (tok, table_lanes), 1)
    lane_few = lax.broadcasted_iota(jnp.int32, (8, table_lanes), 1)
    slot_rows = lax.broadcasted_iota(jnp.int32, (slots, tok), 0).astype(jnp.float32)
    slot_cols = lax.broadcasted_iota(jnp.int32, (tok, slots), 1).astype(jnp.float32)

    in_expert = pieces // 2
    for i, piece in enumerate(piece_refs):
        q, rows_in = i // in_expert, piece.shape[1]
        first = pl.multiple_of(place_ref[i % in_expert], 16)
        w_ref[q * 3 * count : (q + 1) * 3 * count, pl.ds(first, rows_in), :] = piece[...]

    for s in range(shards):
        there = slice(s * slots, (s + 1) * slots)
        table = x_refs[s][:, width:]
        gathers, weights = [], []
        for q in range(2):
            expert = expert_ref[q]
            weight_row = dot((lane_few == expert).astype(jnp.bfloat16), table, NT)[0:1]
            picked_row = weight_row > 0.0
            rank_row = dot(
                jnp.broadcast_to(picked_row, (8, tok)).astype(jnp.bfloat16), earlier_row, NN
            )[0:1]
            gather = jnp.where(jnp.logical_and(slot_rows == rank_row, picked_row), 1.0, 0.0)
            gathers.append(gather)
            weights.append(jnp.sum(gather * weight_row, axis=1, keepdims=True))
            picked_col = (
                jnp.max(
                    jnp.where(lane_tok == expert, table.astype(jnp.float32), 0.0),
                    axis=1,
                    keepdims=True,
                )
                > 0.0
            )
            rank_col = dot(
                earlier_col, jnp.broadcast_to(picked_col, (tok, tok)).astype(jnp.bfloat16), NN
            )[:, 0:1]
            spread[s, q] = jnp.where(
                jnp.logical_and(slot_cols == rank_col, picked_col), 1.0, 0.0
            ).astype(jnp.bfloat16)
        gather = jnp.concatenate(gathers, axis=0).astype(jnp.bfloat16)
        weight = jnp.concatenate(weights, axis=0)
        x_rows = dot(gather, x_refs[s][:, :width], NN).astype(jnp.bfloat16)
        g_rows = dot(gather, g_refs[s][...], NN)
        s_rows = (g_rows * weight).astype(jnp.bfloat16)
        g_rows = g_rows.astype(jnp.bfloat16)
        for q in range(2):
            own = slice(q * slots, (q + 1) * slots)
            for c in range(feat):
                cut = slice(c * LANES, (c + 1) * LANES)
                xs[q, c, there, :] = x_rows[own, cut]
                gs[q, c, there, :] = g_rows[own, cut]
                ss[q, c, there, :] = s_rows[own, cut]

    def one_expert(q):
        gate[...] = jnp.zeros_like(gate)
        up[...] = jnp.zeros_like(up)
        hgrad[...] = jnp.zeros_like(hgrad)
        pgrad[...] = jnp.zeros_like(pgrad)
        first = q * (3 * count)

        def keep(b, grad):
            if resumed:
                grad = grad + so_far_refs[q][b]
            grad_refs[q][b] = grad.astype(grad_refs[q].dtype)

        def place(m, b):
            at = 2 * (first + m * count + b)
            return lay_ref[at], lay_ref[at + 1]

        for b in range(count):
            r, c = place(0, b)
            gate[c] += dot(xs[q, r], w_ref[first + b], NN)
            r, c = place(1, b)
            up[c] += dot(xs[q, r], w_ref[first + count + b], NN)
            r, c = place(2, b)
            hgrad[r] += dot(ss[q, c], w_ref[first + 2 * count + b], NT)
        for h in range(hidden):
            gate_pre = gate[h]
            up_pre = up[h]
            sig = jax.nn.sigmoid(gate_pre)
            activated = gate_pre * sig
            hid[h] = (activated * up_pre).astype(jnp.bfloat16)
            hidden_grad = hgrad[h]
            ggrad[h] = (hidden_grad * up_pre * sig * (1.0 + gate_pre * (1.0 - sig))).astype(
                jnp.bfloat16
            )
            ugrad[h] = (hidden_grad * activated).astype(jnp.bfloat16)
        prod[...] = jnp.zeros_like(prod)
        for b in range(count):
            r, c = place(0, b)
            pgrad[r] += dot(ggrad[c], w_ref[first + b], NT)
            keep(b, dot(xs[q, r], ggrad[c], TN))
            r, c = place(1, b)
            pgrad[r] += dot(ugrad[c], w_ref[first + count + b], NT)
            keep(count + b, dot(xs[q, r], ugrad[c], TN))
            r, c = place(2, b)
            prod[...] += dot(hid[r], w_ref[first + 2 * count + b], NN) * gs[q, c].astype(
                jnp.float32
            )
            keep(2 * count + b, dot(hid[r], ss[q, c], TN))
        for s in range(shards):
            there = slice(s * slots, (s + 1) * slots)
            for c in range(feat):
                wide[s, q, :, c * LANES : (c + 1) * LANES] = pgrad[c, there, :].astype(
                    jnp.bfloat16
                )
            score = jnp.sum(prod[there, :], axis=1, keepdims=True).astype(jnp.bfloat16)
            own_lane = (
                lax.broadcasted_iota(jnp.int32, (slots, table_lanes), 1) == expert_ref[q]
            )
            wide[s, q, :, width:] = jnp.where(own_lane, score.astype(jnp.float32), 0.0).astype(
                jnp.bfloat16
            )

    for q in range(2):
        one_expert(q)
    for s in range(shards):
        total = dot(spread[s, 0], wide[s, 0], NN) + dot(spread[s, 1], wide[s, 1], NN)
        low, high = total[:, :half], total[:, half:]
        if added:
            low = low + low_so_far[s][...].astype(jnp.float32)
            high = high + high_so_far[s][...].astype(jnp.float32)
        low_refs[s][...] = low.astype(jnp.bfloat16)
        high_refs[s][...] = high.astype(jnp.bfloat16)


def run_experts(
    x_list, g_list, weights, places, layouts, experts, slots, so_far, parts_so_far, final
):
    shards = len(x_list)
    tok, table_width = x_list[0].shape
    width = g_list[0].shape[1]
    half = width // 2
    feat = width // LANES
    hidden = HID // LANES
    rows = shards * slots
    block_count = 2 * weights[0].shape[0]
    resumed = so_far is not None
    bf16, f32 = jnp.bfloat16, jnp.float32
    smem = pl.BlockSpec(memory_space=pltpu.SMEM)
    grads = jax.ShapeDtypeStruct((block_count // 2, LANES, LANES), bf16 if final else f32)
    out_shape = [jax.ShapeDtypeStruct((tok, half), bf16)] * shards
    out_shape += [jax.ShapeDtypeStruct((tok, table_width - half), bf16)] * shards
    out_shape += [grads, grads]

    def whole(value):
        return pl.BlockSpec(value.shape, lambda i: (0,) * len(value.shape))

    added = len(parts_so_far) > 0
    operands = [*x_list, *g_list, *weights] + (list(so_far) if resumed else [])
    operands += [low for low, _ in parts_so_far] + [high for _, high in parts_so_far]
    outs = pl.pallas_call(
        functools.partial(
            expert_kernel, shards, slots, half, len(weights), resumed, added
        ),
        grid=(1,),
        in_specs=[smem] * 3 + [whole(value) for value in operands],
        out_specs=[whole(value) for value in out_shape],
        out_shape=out_shape,
        scratch_shapes=[
            pltpu.VMEM((block_count, LANES, LANES), bf16),
            pltpu.VMEM((2, feat, rows, LANES), bf16),
            pltpu.VMEM((2, feat, rows, LANES), bf16),
            pltpu.VMEM((2, feat, rows, LANES), bf16),
            pltpu.VMEM((hidden, rows, LANES), f32),
            pltpu.VMEM((hidden, rows, LANES), f32),
            pltpu.VMEM((hidden, rows, LANES), bf16),
            pltpu.VMEM((hidden, rows, LANES), f32),
            pltpu.VMEM((hidden, rows, LANES), bf16),
            pltpu.VMEM((hidden, rows, LANES), bf16),
            pltpu.VMEM((feat, rows, LANES), f32),
            pltpu.VMEM((shards, 2, slots, table_width), bf16),
            pltpu.VMEM((shards, 2, tok, slots), bf16),
            pltpu.VMEM((rows, LANES), f32),
        ],
        compiler_params=pltpu.CompilerParams(vmem_limit_bytes=58 * 1024 * 1024),
        cost_estimate=pl.CostEstimate(
            flops=2 * 2 * 108 * rows * LANES * LANES * 8,
            bytes_accessed=shards * tok * table_width * 6 + block_count * LANES * LANES * 6,
            transcendentals=0,
        ),
    )(layouts, experts, places, *operands)
    return outs[:shards], outs[shards : 2 * shards], outs[2 * shards :]


def chip_ring(chips):
    broad = chips // 2
    return list(range(broad)) + list(range(chips - 1, broad - 1, -1))


def swap_all(pieces):
    return lax.all_to_all(pieces, "expert", split_axis=0, concat_axis=0, tiled=True)


def body(tokens, out_grad, expert_ids, route_weights, blocks, layout, moments, partner):
    expert_count = lax.axis_size("expert")
    replica_count = lax.axis_size("dp")
    tok_count, topk_count = expert_ids.shape
    width = tokens.shape[1]
    block_size = blocks.shape[-1]
    capacity = max(2, tok_count * topk_count * 7 // (expert_count * 6))
    slots = -(-capacity // 16) * 16
    table_lanes = -(-expert_count // LANES) * LANES
    bf16, f32 = jnp.bfloat16, jnp.float32
    chips = expert_count // 4
    ring = chip_ring(chips)
    steps = [
        (a + side * chips, b + side * chips)
        for a, b in zip(ring, ring[1:] + ring[:1])
        for side in range(2)
    ]
    onward = [(2 * a + core, 2 * b + core) for a, b in steps for core in range(2)]
    backward = [(b, a) for a, b in onward]
    sister = [(i, i ^ 1) for i in range(expert_count)]
    far = expert_count // 2
    mirror = [(i, i ^ far) for i in range(expert_count)]
    row_share = block_size // replica_count
    replica = lax.axis_index("dp")

    def step_on(value):
        return lax.ppermute(value, "expert", onward)

    def step_back(value):
        return lax.ppermute(value, "expert", backward)

    def own_rows(value):
        return lax.dynamic_slice_in_dim(value, replica * row_share, row_share, 2)

    def other_replica(value):
        return lax.ppermute(value, "dp", [(0, 1), (1, 0)])

    def other_core(value):
        return lax.ppermute(value, "expert", sister)

    def join_rows(rows):
        if replica_count != 2:
            return lax.all_gather(rows, "dp", axis=2, tiled=True)
        mine_here = (jnp.arange(2, dtype=jnp.int32) == replica)[None, None, :, None, None]
        both = jnp.where(mine_here, rows[:, :, None], other_replica(rows)[:, :, None])
        return both.reshape(rows.shape[:2] + (block_size,) + rows.shape[3:])

    def sum_rows(one, two):
        if replica_count != 2:
            whole = lax.psum_scatter(add(one, two), "dp", scatter_dimension=2, tiled=True)
            return whole.astype(f32), None

        def half_of(index):
            return sum(
                lax.dynamic_slice_in_dim(value, index * row_share, row_share, 2).astype(f32)
                for value in (one, two)
            )

        return half_of(replica), other_replica(half_of(1 - replica).astype(bf16))

    def rows_total(mine, theirs):
        return mine if theirs is None else mine + theirs.astype(f32)

    def add(left, right):
        return (left.astype(f32) + right.astype(f32)).astype(bf16)

    lane = jnp.arange(table_lanes, dtype=jnp.int32)
    named = expert_ids[:, :, None] == lane[None, None, :]
    table = jnp.sum(jnp.where(named, route_weights[:, :, None].astype(f32), 0.0), axis=1).astype(
        bf16
    )
    me = lax.axis_index("expert")

    note_rows = 16
    layout_flat = layout.reshape(-1)
    layout_note = jnp.zeros((note_rows * LANES,), bf16).at[: layout_flat.shape[0]].set(
        layout_flat.astype(bf16)
    )
    rows_now = own_rows(blocks[0])
    pieces = rows_now.reshape(expert_count, -1, LANES)
    piece_rows = pieces.shape[1]
    note = jnp.broadcast_to(
        layout_note.reshape(1, note_rows, LANES), (expert_count, note_rows, LANES)
    )
    spread = swap_all(jnp.concatenate([pieces, note], axis=1))
    all_slots = jnp.arange(expert_count, dtype=jnp.int32)

    def ordered(spread_state, slot_order):
        order = partner.at[slot_order].get(mode="promise_in_bounds")
        return spread_state.at[order].get(mode="promise_in_bounds")

    x_at = {0: jnp.concatenate([tokens, table], axis=1)}
    g_at = {0: out_grad}
    most = chips // 2
    moment_pieces = moments[0].astype(bf16).reshape(expert_count, -1, LANES)
    for s in range(1, most + 1):
        x_at[-s] = step_on(x_at[1 - s])
        if s < most:
            x_at[s] = step_back(x_at[s - 1])
        if s == 1:
            x_at, g_at, spread, moment_pieces = lax.optimization_barrier(
                (x_at, g_at, spread, moment_pieces)
            )
        g_at[s] = step_back(g_at[s - 1])
        if s < most:
            g_at[-s] = step_on(g_at[1 - s])
        if s == 1:
            state_pieces = spread[:, :piece_rows]
            far_pieces = ordered(state_pieces, all_slots ^ far)
            near_pieces = ordered(state_pieces, all_slots)
            rows_far, near_pieces, g_at = lax.optimization_barrier(
                (swap_all(far_pieces), near_pieces, g_at)
            )
            rows_far = rows_far.reshape(rows_now.shape)
    x_at[most] = x_at[-most]
    rows_near = swap_all(near_pieces).reshape(rows_now.shape)
    all_layouts = spread[:, piece_rows:].reshape(expert_count, -1)[:, : layout_flat.shape[0]]
    shards = [0]
    for s in range(1, most):
        shards += [s, -s]
    shards += [most]
    groups = [shards[i : i + 8] for i in range(0, len(shards), 8)]

    if replica_count == 2:
        places = jnp.stack([replica * row_share, (1 - replica) * row_share]).astype(jnp.int32)
    else:
        places = jnp.zeros((1,), jnp.int32)

    def both_cores(rows):
        halves = [rows, other_replica(rows)] if replica_count == 2 else [join_rows(rows)]
        return halves

    def to_weights(halves):
        weights = halves + [other_core(value) for value in halves]
        return [value.reshape(-1, value.shape[2], LANES) for value in weights]

    def pair_of(slot):
        pair = jnp.stack([slot, slot ^ 1])
        experts = partner.at[pair].get(mode="promise_in_bounds").astype(jnp.int32)
        layouts = all_layouts.at[experts].get(mode="promise_in_bounds")
        return experts, layouts.reshape(-1).astype(jnp.int32)

    def run_pair(pair, weights, earlier, beside):
        experts, layouts = pair
        parts, sums = {}, None
        for group in groups:
            lows, highs, sums = run_experts(
                [x_at[d] for d in group],
                [g_at[d] for d in group],
                weights,
                places,
                layouts,
                experts,
                slots,
                sums,
                [earlier[d] for d in group] if earlier else [],
                group is groups[-1],
            )
            for d, low, high in zip(group, lows, highs):
                parts[d] = (low, high)
        sums, beside = lax.optimization_barrier((sums, beside))
        own_grad, other_grad = (value.reshape(blocks[0].shape) for value in sums)
        return parts, own_grad, other_core(other_grad), beside

    halves_far = both_cores(rows_far)
    far_pair, near_pair = pair_of(me ^ far), pair_of(me)
    halves_far, x_at, g_at, far_pair, near_pair, places = lax.optimization_barrier(
        (halves_far, x_at, g_at, far_pair, near_pair, places)
    )
    weights_far = to_weights(halves_far)
    weights_far, moment_pieces, rows_near = lax.optimization_barrier(
        (weights_far, moment_pieces, rows_near)
    )
    parts, far_grad, far_sister, (moment_spread, halves_near) = run_pair(
        far_pair, weights_far, None, (swap_all(moment_pieces), both_cores(rows_near))
    )
    weights_near = to_weights(halves_near)
    moved_moments = swap_all(ordered(moment_spread, all_slots)).reshape(rows_now.shape)
    far_mine, far_theirs = sum_rows(far_grad, far_sister)
    parts, near_grad, near_sister, (far_theirs, moved_moments) = run_pair(
        near_pair, weights_near, parts, (far_theirs, moved_moments)
    )
    far_sum = rows_total(far_mine, far_theirs).astype(bf16)
    from_mirror = lax.ppermute(far_sum, "expert", mirror)
    near_mine, near_theirs = sum_rows(near_grad, near_sister)

    def own_share(distance, part):
        return parts[distance][part]

    upward = [step_on(own_share(most, 0)), None]
    downward = [None, step_back(own_share(most, 1))]
    shard_grad = rows_total(near_mine, near_theirs) + from_mirror.astype(f32)
    new_moment = momentum_decay * moved_moments.astype(f32) + shard_grad
    new_shard = (rows_near.astype(f32) - step_rate * new_moment).astype(bf16)

    upward, downward, new_shard = lax.optimization_barrier((upward, downward, new_shard))
    for s in range(most - 1, 0, -1):
        for part in range(2):
            share = own_share(s, part)
            upward[part] = step_on(share if upward[part] is None else add(upward[part], share))
            share = own_share(-s, part)
            downward[part] = step_back(
                share if downward[part] is None else add(downward[part], share)
            )
    homes = [
        (parts[0][part].astype(f32) + upward[part].astype(f32) + downward[part].astype(f32)).astype(
            bf16
        )
        for part in range(2)
    ]
    half = homes[0].shape[1]
    token_grad = jnp.concatenate([homes[0], homes[1][:, : width - half]], axis=1)
    scores = homes[1][:, width - half :]
    route_grad = jnp.sum(jnp.where(named, scores[:, None, :].astype(f32), 0.0), axis=2).astype(bf16)
    return (token_grad, route_grad, join_rows(new_shard)[None], new_moment[None])


def solution(mesh):
    placed = (
        P(("dp", "expert"), None),
        P(("dp", "expert"), None),
        P(("dp", "expert"), None),
        P(("dp", "expert"), None),
        P("expert", None, None, None, None),
        P("expert", None, None, None),
        P("expert", None, None, "dp", None),
        P(),
    )
    return jax.shard_map(
        body,
        mesh=mesh,
        in_specs=placed,
        out_specs=(
            P(("dp", "expert"), None),
            P(("dp", "expert"), None),
            P("expert", None, None, None, None),
            P("expert", None, None, "dp", None),
        ),
        check_vma=False,
    )
```
